32 devices in a mesh: seq: 8 (over z, y), head: 4 (over x, core).
Axes of the slice: x: 2, y: 2, z: 4, core: 2. Of those that a mesh axis runs over, the one named last changes fastest.
Arguments:
- queries: bfloat16 [4096, 4096], P('seq', 'head'), may hold values from -6 to 6
- key_vectors: bfloat16 [4096, 4096], P('seq', 'head'), may hold values from -6 to 6
- value_vectors: bfloat16 [4096, 4096], P('seq', 'head'), may hold values from -6 to 6
- log_decay: float32 [4096, 32], P('seq', 'head'), may hold values from -0.78 to 0
- head_scale: float32 [32], P('head'), may hold values from 0.2 to 1.6
- send_rows: int32 [8, 2, 128], P('seq'), may hold values from 0 to 511, as said below
- take_rows: int32 [4096], P('seq'), may hold values from 0 to 767, as said below
- doc_lengths: int32 [8], replicated, may hold values from 1 to 1024, as said below
- cotangent: bfloat16 [4096, 4096], P('seq', 'head'), may hold values from -6 to 6
Outputs:
- normed: bfloat16 [4096, 4096], P('seq', 'head')
- grad_queries: bfloat16 [4096, 4096], P('seq', 'head')
- grad_keys: bfloat16 [4096, 4096], P('seq', 'head')
- grad_values: bfloat16 [4096, 4096], P('seq', 'head')
The draws below stay inside these ranges and needn't reach their ends.
Inputs may be any that keep to these rules, and one draw needn't show every extreme that they name: For shard d, send_rows[d, 0] lists local rows handed to shard d - 1 and send_rows[d, 1] rows handed to shard d + 1; a slot is live only if shard d - 1 (resp. d + 1) takes it; live rows of one shard are distinct over both lists and never a row that take_rows of shard d names among its own; the first shard hands nothing left and the last nothing right. take_rows at a position of shard d indexes [128 rows from shard d - 1, the 512 own rows, 128 rows from shard d + 1]; the values of one shard are distinct and take exactly as many rows from a neighbour as that neighbour hands over; the numbers handed between two neighbours are equal both ways and in every draw some pair hands 128. `doc_lengths`: document lengths sum to 4096; some document other than the first starts at a multiple of 512.
All inputs are finite; a program needn't handle non-finite values.
Results may differ from the reference program's by a relative error of at most 0.0061.
Values may be sent and summed in bfloat16 or wider, within the bound.
No kernel may reach another device: no remote copies, remote signals or barrier semaphores. Data moves between devices by JAX's collectives and lax.ppermute only.
A program may use at most 64 MiB of HBM per device.

```python
import math
import jax
import jax.numpy as jnp
from jax import lax

HEADS = 32
DK = 128
TOK_DEV = 512
NDOC = 8
CAP = 128
PACKED_TOKENS = 4096
N_SEQ = 8


def shuffled(key_one):
    return jax.random.permutation(key_one, TOK_DEV).astype(jnp.int32)


def routing(key):
    key_counts, key_full, key_order, key_mix = jax.random.split(key, 4)
    counts = jax.random.randint(key_counts, (N_SEQ - 1,), max(1, CAP // 3), CAP + 1).astype(jnp.int32)
    full_pair = jax.random.randint(key_full, (), 0, N_SEQ - 1)
    counts = jnp.where(jnp.arange(N_SEQ - 1) == full_pair, CAP, counts).astype(jnp.int32)
    zero_one = jnp.zeros((1,), jnp.int32)
    left_counts = jnp.concatenate([zero_one, counts])
    right_counts = jnp.concatenate([counts, zero_one])
    orders = jax.vmap(shuffled)(jax.random.split(key_order, N_SEQ))
    slots = jnp.arange(CAP, dtype=jnp.int32)
    left_list = orders[:, :CAP]
    right_list = jnp.take_along_axis(orders, left_counts[:, None] + slots[None, :], axis=1)
    sending = jnp.stack([left_list, right_list], axis=1).astype(jnp.int32)
    entries = jnp.arange(TOK_DEV, dtype=jnp.int32)[None, :]
    kept = (TOK_DEV - left_counts - right_counts)[:, None]
    own_index = jnp.clip(right_counts[:, None] + entries, 0, TOK_DEV - 1)
    own_rows = jnp.take_along_axis(orders, own_index, axis=1)
    lefts = left_counts[:, None]
    candidate = jnp.where(entries < lefts, entries, jnp.where(entries < lefts + kept, CAP + own_rows, CAP + TOK_DEV + entries - lefts - kept))
    mixing = jax.vmap(shuffled)(jax.random.split(key_mix, N_SEQ))
    taking = jnp.take_along_axis(candidate, mixing, axis=1).reshape(PACKED_TOKENS).astype(jnp.int32)
    return (sending, taking)


def draw_send_rows(key, part):
    return routing(key)[0]


def draw_take_rows(key, part):
    return routing(key)[1]


def draw_doc_lengths(key, part):
    key = jax.random.fold_in(key, 11)
    key_place, key_offset, key_sizes = jax.random.split(key, 3)
    longest = PACKED_TOKENS // 4
    remainder = PACKED_TOKENS - longest
    others = NDOC - 1
    aligned_doc = jax.random.randint(key_place, (), 1, NDOC - 1).astype(jnp.int32)
    after_docs = others - aligned_doc
    low_sum = jnp.maximum(aligned_doc, remainder - after_docs * longest)
    high_sum = jnp.minimum(aligned_doc * longest, remainder - after_docs)
    low_block = (low_sum + TOK_DEV - 1) // TOK_DEV
    high_block = high_sum // TOK_DEV
    before_left = (jax.random.randint(key_offset, (), low_block, high_block + 1) * TOK_DEV).astype(jnp.int32)
    after_left = (remainder - before_left).astype(jnp.int32)
    size_keys = jax.random.split(key_sizes, NDOC)
    lengths = []
    for slot_index in range(NDOC):
        in_before = slot_index < aligned_doc
        in_after = slot_index > aligned_doc
        remaining = jnp.where(in_before, before_left, after_left)
        left_docs = jnp.maximum(jnp.where(in_before, aligned_doc - slot_index, NDOC - slot_index), 1)
        lowest = jnp.maximum(1, remaining - (left_docs - 1) * longest)
        highest = jnp.maximum(jnp.minimum(longest, remaining - (left_docs - 1)), lowest)
        chosen = jax.random.randint(size_keys[slot_index], (), lowest, highest + 1)
        chosen = jnp.where(slot_index == aligned_doc, longest, chosen).astype(jnp.int32)
        before_left = (before_left - jnp.where(in_before, chosen, 0)).astype(jnp.int32)
        after_left = (after_left - jnp.where(in_after, chosen, 0)).astype(jnp.int32)
        lengths.append(chosen)
    return jnp.stack(lengths).astype(jnp.int32)


def draw_log_decay(key, part):
    key = jax.random.fold_in(key, 7)
    random_key_heads, random_key_shard, random_key_tokens, random_key_surge, random_key_layers = jax.random.split(key, 5)
    mixing = jax.random.uniform(random_key_heads, (HEADS,))
    fastest = math.log(1.0 / 40.0)
    slowest = math.log(0.1 / PACKED_TOKENS)
    rates = jnp.exp(fastest + mixing * (slowest - fastest))
    device_factor = jnp.exp(jax.random.uniform(random_key_shard, (N_SEQ, 1, HEADS), minval=-0.7, maxval=0.7))
    token_factor = jax.random.uniform(random_key_tokens, (N_SEQ, TOK_DEV, HEADS), minval=0.5, maxval=1.5)
    base = -(rates[None, None, :] * device_factor * token_factor).reshape(PACKED_TOKENS, HEADS)
    surge_position = jax.random.randint(random_key_surge, (4,), 0, PACKED_TOKENS)
    surge_hit = jnp.any(jnp.arange(PACKED_TOKENS)[:, None] == surge_position[None, :], axis=1)
    depth = jax.random.uniform(random_key_layers, (PACKED_TOKENS, 1), minval=0.2, maxval=0.7)
    return jnp.where(surge_hit[:, None], base - depth, base).astype(jnp.float32)


def draw_head_scale(key, part):
    key = jax.random.fold_in(key, 5)
    rising = jnp.exp(math.log(3.0) * jnp.arange(HEADS, dtype=jnp.float32) / (HEADS - 1)) / 3.0
    factor = jax.random.uniform(key, (HEADS,), minval=0.8, maxval=1.25)
    return (rising * factor).astype(jnp.float32)


def level_of(stream_key, dims, cuts, smallest, largest):
    def one(dim, blocks):
        steps = jax.random.uniform(jax.random.fold_in(jax.random.fold_in(stream_key, 6), dim), (blocks,), jnp.float32, smallest / len(cuts), largest / len(cuts))
        return jnp.repeat(jnp.exp(steps), dims[dim] // blocks).reshape((-1,) + (1,) * (len(dims) - dim - 1))

    factor_of = one(*cuts[0])
    for cut in cuts[1:]:
        factor_of = factor_of * one(*cut)
    return factor_of


def centred(stream_key, extent, deviation, most, pieces=(), kind=jnp.bfloat16):
    gain = level_of(stream_key, extent, pieces, -0.22, 0.18) if pieces else 1.0
    array = jax.random.normal(stream_key, extent, jnp.float32) * deviation * gain
    return jnp.minimum(jnp.maximum(array, -most), most).astype(kind)


def setup_inputs(seed: int = 0) -> dict:
    keys = jax.random.split(jax.random.key(seed), 10)
    return {
        "queries": centred(keys[0], (PACKED_TOKENS, HEADS * DK), 1.0, 6.0, ((0, 8), (1, 4))),
        "key_vectors": centred(keys[1], (PACKED_TOKENS, HEADS * DK), 1.0, 6.0, ((0, 8), (1, 4))),
        "value_vectors": centred(keys[2], (PACKED_TOKENS, HEADS * DK), 1.0, 6.0, ((0, 8), (1, 4))),
        "log_decay": draw_log_decay(jax.random.fold_in(keys[9], 71), 0),
        "head_scale": draw_head_scale(jax.random.fold_in(keys[9], 71), 0),
        "send_rows": draw_send_rows(jax.random.fold_in(keys[9], 71), 0),
        "take_rows": draw_take_rows(jax.random.fold_in(keys[9], 71), 0),
        "doc_lengths": draw_doc_lengths(jax.random.fold_in(keys[9], 71), 0),
        "cotangent": centred(keys[8], (PACKED_TOKENS, HEADS * DK), 1.0, 6.0, ((0, 8), (1, 4))),
    }


EPSILON = 1e-05

def shard_masks(log_shard, first_position, starts):
    length_rows = log_shard.shape[0]
    position = first_position + jnp.arange(length_rows, dtype=jnp.int32)
    opening = jnp.any(position[:, None] == starts[None, :], axis=1)
    segment = lax.optimization_barrier(jnp.sum((position[:, None] >= starts[None, :]).astype(jnp.int32), axis=1))
    cumulative = jnp.cumsum(log_shard, axis=0)
    below_diag = jnp.arange(length_rows)[:, None] >= jnp.arange(length_rows)[None, :]
    joined = (segment[:, None] == segment[None, :]) & below_diag
    spread = cumulative.T[:, :, None] - cumulative.T[:, None, :]
    weights = jnp.exp(jnp.where(joined[None], spread, -jnp.inf))
    carried = (segment == segment[0]) & jnp.logical_not(opening[0])
    entering = jnp.where(carried[:, None], jnp.exp(cumulative), 0.0)
    last_segment = segment == segment[-1]
    leaving = jnp.where(last_segment[:, None], jnp.exp(cumulative[-1][None, :] - cumulative), 0.0)
    through = jnp.exp(cumulative[-1]) * jnp.where(jnp.any(opening), 0.0, 1.0)
    return (weights, entering, leaving, through)

def rounded(values):
    return lax.optimization_barrier(values.astype(jnp.bfloat16)).astype(jnp.float32)

def shard_probs(shard_queries, shard_keys, weights, scaling):
    scores = jnp.einsum('ihd,jhd->hij', shard_queries.astype(jnp.float32), shard_keys.astype(jnp.float32))
    return rounded(scores * weights * scaling)

def shard_outputs(weighted, shard_queries, shard_values, entering, incoming, scaling):
    inside = jnp.einsum('hij,jhe->ihe', weighted, shard_values.astype(jnp.float32))
    from_state = jnp.einsum('ihd,hde->ihe', shard_queries.astype(jnp.float32), rounded(incoming))
    return inside + scaling * entering[:, :, None] * from_state

def shard_state(shard_keys, shard_values, leaving):
    key_weighted = rounded(shard_keys.astype(jnp.float32) * leaving[:, :, None])
    return jnp.einsum('jhd,jhe->hde', key_weighted, shard_values.astype(jnp.float32))

def query_state(shard_queries, entering, grad_float, scaling):
    query_weighted = rounded(shard_queries.astype(jnp.float32) * (entering * scaling)[:, :, None])
    return jnp.einsum('ihd,ihe->hde', query_weighted, grad_float)

def shard_grads(shard_queries, shard_keys, shard_values, weighted, weights, entering, leaving, incoming, outgoing, grad_float, scaling):
    query_float = shard_queries.astype(jnp.float32)
    key_float = shard_keys.astype(jnp.float32)
    value_float = shard_values.astype(jnp.float32)
    incoming_low = rounded(incoming)
    outgoing_low = rounded(outgoing)
    dscore = rounded(jnp.einsum('ihe,jhe->hij', grad_float, value_float) * weights * scaling)
    grad_q = jnp.einsum('hij,jhd->ihd', dscore, key_float) + scaling * entering[:, :, None] * jnp.einsum('ihe,hde->ihd', grad_float, incoming_low)
    grad_k = jnp.einsum('hij,ihd->jhd', dscore, query_float) + leaving[:, :, None] * jnp.einsum('jhe,hde->jhd', value_float, outgoing_low)
    grad_v = jnp.einsum('hij,ihe->jhe', weighted, grad_float) + leaving[:, :, None] * jnp.einsum('jhd,hde->jhe', key_float, outgoing_low)
    return (grad_q.astype(jnp.bfloat16), grad_k.astype(jnp.bfloat16), grad_v.astype(jnp.bfloat16))

def pick_rows(block_rows, index_rows):
    return block_rows[:, index_rows]

def place_rows(block_rows, index_rows, values):
    return block_rows.at[:, index_rows].set(values)

def add_rows(block_rows, index_rows, values):
    return block_rows.at[:, index_rows].add(values)

def reference(queries, key_vectors, value_vectors, log_decay, head_scale, send_rows, take_rows, doc_lengths, cotangent):
    features = HEADS * DK
    scaling = DK ** (-0.5)
    stacked = jnp.stack([queries, key_vectors, value_vectors]).reshape(3, N_SEQ, TOK_DEV, features)
    sending = send_rows.reshape(N_SEQ, 2 * CAP)
    picked = jax.vmap(pick_rows, in_axes=(1, 0), out_axes=1)(stacked, sending)
    zero_block = jnp.zeros((3, 1, CAP, features), stacked.dtype)
    from_left = jnp.concatenate([zero_block, picked[:, :-1, CAP:]], axis=1)
    from_right = jnp.concatenate([picked[:, 1:, :CAP], zero_block], axis=1)
    extended = jnp.concatenate([from_left, stacked, from_right], axis=2)
    taking = take_rows.reshape(N_SEQ, TOK_DEV)
    balanced = jax.vmap(pick_rows, in_axes=(1, 0), out_axes=1)(extended, taking).reshape(3, N_SEQ, TOK_DEV, HEADS, DK)
    starts = (jnp.cumsum(doc_lengths) - doc_lengths).astype(jnp.int32)
    firsts = jnp.arange(N_SEQ, dtype=jnp.int32) * TOK_DEV
    decays = log_decay.reshape(N_SEQ, TOK_DEV, HEADS)

    def forward_step(carried_state, inputs):
        shard_queries, shard_keys, shard_values, shard_logs, first_position = inputs
        weights, entering, leaving, through = shard_masks(shard_logs, first_position, starts)
        weighted = shard_probs(shard_queries, shard_keys, weights, scaling)
        outputs = shard_outputs(weighted, shard_queries, shard_values, entering, carried_state, scaling)
        end_state = shard_state(shard_keys, shard_values, leaving)
        return (through[:, None, None] * carried_state + end_state, (outputs, carried_state))
    final_state, (outputs, incoming) = lax.scan(forward_step, jnp.zeros((HEADS, DK, DK), jnp.float32), (balanced[0], balanced[1], balanced[2], decays, firsts))
    scaled = outputs * head_scale[None, None, :, None]
    upstream = cotangent.reshape(N_SEQ, TOK_DEV, HEADS, DK).astype(jnp.float32)
    inverse = lax.rsqrt(lax.optimization_barrier(jnp.sum(scaled * scaled, axis=(2, 3))) / features + EPSILON)[:, :, None, None]
    normed = (scaled * inverse).astype(jnp.bfloat16).reshape(PACKED_TOKENS, features)
    mean_dot = (lax.optimization_barrier(jnp.sum(upstream * scaled, axis=(2, 3))) / features)[:, :, None, None]
    grad_out = rounded((inverse * upstream - scaled * inverse ** 3 * mean_dot) * head_scale[None, None, :, None])

    def backward_step(carried_grad, inputs):
        shard_queries, shard_keys, shard_values, shard_logs, first_position, shard_incoming, grad_float = inputs
        weights, entering, leaving, through = shard_masks(shard_logs, first_position, starts)
        weighted = shard_probs(shard_queries, shard_keys, weights, scaling)
        grads = shard_grads(shard_queries, shard_keys, shard_values, weighted, weights, entering, leaving, shard_incoming, carried_grad, grad_float, scaling)
        pushed = query_state(shard_queries, entering, grad_float, scaling)
        return (pushed + through[:, None, None] * carried_grad, grads)
    first_grad, grads = lax.scan(backward_step, jnp.zeros((HEADS, DK, DK), jnp.float32), (balanced[0], balanced[1], balanced[2], decays, firsts, incoming, grad_out), reverse=True)
    stacked_grads = jnp.stack(grads).reshape(3, N_SEQ, TOK_DEV, features)
    ext_grads = jax.vmap(place_rows, in_axes=(1, 0, 1), out_axes=1)(jnp.zeros((3, N_SEQ, TOK_DEV + 2 * CAP, features), jnp.bfloat16), taking, stacked_grads)
    zero_grads = jnp.zeros((3, 1, CAP, features), jnp.bfloat16)
    to_left_back = jnp.concatenate([zero_grads, ext_grads[:, :-1, CAP + TOK_DEV:]], axis=1)
    to_right_back = jnp.concatenate([ext_grads[:, 1:, :CAP], zero_grads], axis=1)
    arrival = jax.vmap(add_rows, in_axes=(1, 0, 1), out_axes=1)(ext_grads[:, :, CAP:CAP + TOK_DEV], sending, jnp.concatenate([to_left_back, to_right_back], axis=2))
    arrival = arrival.reshape(3, PACKED_TOKENS, features)
    return (normed, arrival[0], arrival[1], arrival[2])
```

```python
import functools
import math

import jax
import jax.numpy as jnp
from jax import lax
from jax.experimental import pallas as pl
from jax.experimental.pallas import tpu as pltpu
from jax.sharding import PartitionSpec as P

EPSILON = 1e-05
LOG2E = math.log2(math.e)
MASKED = -1e30
VMEM_BYTES = 40 * 1024 * 1024
BF = jnp.bfloat16
F32 = jnp.float32
NT = (((1,), (1,)), ((), ()))
TN = (((0,), (0,)), ((), ()))


def dot(a, b):
    return jnp.dot(a, b, preferred_element_type=F32)


def dot_nt(a, b):
    return lax.dot_general(a, b, NT, preferred_element_type=F32)


def dot_tn(a, b):
    return lax.dot_general(a, b, TN, preferred_element_type=F32)


def along_rows(row, lanes=128):
    return jnp.broadcast_to(row, (lanes, row.shape[1])).T


def iota(shape, dim):
    return lax.broadcasted_iota(jnp.int32, shape, dim)


def one_hot(hit):
    return jnp.where(hit, 1.0, 0.0).astype(BF)


def params():
    return pltpu.CompilerParams(vmem_limit_bytes=VMEM_BYTES)


def cost(mflops, kbytes):
    return pl.CostEstimate(
        flops=int(mflops * 1e6), bytes_accessed=int(kbytes * 1024), transcendentals=0
    )


def pick_kernel(send_ref, *refs):
    count = len(refs) - 3
    sources = refs[:count]
    left_ref, right_ref, hot_ref = refs[count:]
    rows = sources[0].shape[0]
    capacity = send_ref.shape[1]

    @pl.when(pl.program_id(0) == 0)
    def _():
        lane = iota((capacity, rows), 1)
        for side in range(2):
            named = along_rows(send_ref[side : side + 1, :], 128)
            for start in range(0, rows, 128):
                hot_ref[side * capacity : (side + 1) * capacity, start : start + 128] = one_hot(
                    named == lane[:, :128] + start
                )

    for index, source in enumerate(sources):
        picked = dot(hot_ref[...], source[...]).astype(BF)
        left_ref[index] = picked[:capacity]
        right_ref[index] = picked[capacity:]


def pick(send, arrays, cols):
    rows, features = arrays[0].shape
    capacity = send.shape[1]
    count = len(arrays)
    block = pl.BlockSpec((rows, cols), lambda g: (0, g))
    out = pl.BlockSpec((count, capacity, cols), lambda g: (0, 0, g))
    shape = jax.ShapeDtypeStruct((count, capacity, features), BF)
    return pl.pallas_call(
        pick_kernel,
        grid=(features // cols,),
        in_specs=[pl.BlockSpec((2, capacity), lambda g: (0, 0))] + [block] * count,
        out_specs=[out, out],
        out_shape=[shape, shape],
        scratch_shapes=[pltpu.VMEM((2 * capacity, rows), BF)],
        compiler_params=params(),
        cost_estimate=cost(268 * count, 1536 * count),
        name="pick",
    )(send, *arrays)


def prep_kernel(
    docs_ref, first_ref, take_ref, log_ref, q_ref, k_ref, v_ref,
    qo_ref, ko_ref, vo_ref, hot_ref, weight_ref, cols_ref, through_ref,
    own_ref, mask_ref, rows_ref,
):
    rows = q_ref.shape[0]
    heads = log_ref.shape[1]
    capacity = hot_ref.shape[1] // 2
    step = pl.program_id(0)
    half = rows // 2

    @pl.when(step == 0)
    def _():
        first = first_ref[0]
        position = first + iota((rows, 1), 0)
        position_row = first + iota((1, rows), 1)
        segment = jnp.zeros((rows, 1), jnp.int32)
        segment_row = jnp.zeros((1, rows), jnp.int32)
        segment_first = jnp.int32(0)
        segment_last = jnp.int32(0)
        opens_first = jnp.int32(0)
        opens = jnp.int32(0)
        start = jnp.int32(0)
        for n in range(docs_ref.shape[0]):
            segment += (position >= start).astype(jnp.int32)
            segment_row += (position_row >= start).astype(jnp.int32)
            segment_first += (first >= start).astype(jnp.int32)
            segment_last += (first + rows - 1 >= start).astype(jnp.int32)
            opens_first += (first == start).astype(jnp.int32)
            opens += ((start >= first) & (start < first + rows)).astype(jnp.int32)
            start += docs_ref[n]
        below = iota((rows, rows), 0) >= iota((rows, rows), 1)
        scale = -0.5 * math.log2(q_ref.shape[1] // 2)
        mask_ref[...] = jnp.where((segment == segment_row) & below, scale, MASKED)
        triangle = one_hot(below)
        logs = jnp.concatenate([log_ref[...], jnp.zeros((rows, 128 - heads), F32)], axis=1)
        high = logs.astype(BF)
        rest = logs - high.astype(F32)
        middle = rest.astype(BF)
        low = (rest - middle.astype(F32)).astype(BF)
        running = (dot(triangle, high) + (dot(triangle, middle) + dot(triangle, low))) * LOG2E
        turned = running.T
        final = running[rows - 1 : rows, :]
        keep_f = segment == segment_last
        keep_e = (segment == segment_first) & (opens_first == 0)
        leaving = jnp.where(keep_f, jnp.exp2(final - running), 0.0)
        entering = jnp.where(keep_e, jnp.exp2(running + scale), 0.0)
        through = jnp.where(opens == 0, jnp.exp2(final), 0.0)
        t_high = through.astype(BF).astype(F32)
        t_middle = (through - t_high).astype(BF).astype(F32)
        t_low = through - t_high - t_middle
        line = iota((16, 128), 0)
        for h in range(heads):
            g, t = h // 2, h % 2
            cols_ref[g, :, t : t + 1] = leaving[:, h : h + 1]
            cols_ref[g, :, 2 + t : 3 + t] = entering[:, h : h + 1]
            cols_ref[g, :, 4 + t : 5 + t] = running[:, h : h + 1]
            rows_ref[g, t : t + 1, :] = turned[h : h + 1, :]
            parts = [
                jnp.broadcast_to(x[:, h : h + 1], (16, 128)) for x in (t_high, t_middle, t_low)
            ]
            through_ref[h] = jnp.where(
                line == 0,
                parts[0],
                jnp.where(line == 1, parts[1], jnp.where(line == 2, parts[2], 0.0)),
            ).astype(BF)
        lane = iota((rows, 128), 1)
        taken = along_rows(take_ref[...], 128)
        for start_row in range(0, rows, 128):
            own_ref[:, start_row : start_row + 128] = one_hot(
                taken - capacity == lane + start_row
            )
        hot_ref[:, :capacity] = one_hot(taken == lane)
        hot_ref[:, capacity:] = one_hot(taken - (capacity + rows) == lane)

    own = own_ref[...]
    qo_ref[...] = dot(own, q_ref[...]).astype(BF)
    ko_ref[...] = dot(own, k_ref[...]).astype(BF)
    vo_ref[...] = dot(own, v_ref[...]).astype(BF)
    for t in range(2):
        column = cols_ref[step, :, 4 + t : 5 + t]
        row = rows_ref[step, t : t + 1, :]
        for i in range(2):
            top, width = i * half, (i + 1) * half
            weight_ref[t, top : top + half, :width] = jnp.exp2(
                (column[top : top + half] - row[:, :width])
                + mask_ref[top : top + half, :width]
            )


def prep(docs, first, take, log_decay, q, k, v, capacity):
    rows, features = q.shape
    heads = log_decay.shape[1]
    pairs = heads // 2
    cols = features // pairs
    smem = pl.BlockSpec(memory_space=pltpu.SMEM)
    block = pl.BlockSpec((rows, cols), lambda g: (0, g))
    whole2 = lambda a, b: pl.BlockSpec((a, b), lambda g: (0, 0))
    whole3 = lambda a, b, c: pl.BlockSpec((a, b, c), lambda g: (0, 0, 0))
    own = jax.ShapeDtypeStruct((rows, features), BF)
    return pl.pallas_call(
        prep_kernel,
        grid=(pairs,),
        in_specs=[smem, smem, whole2(1, rows), whole2(rows, heads), block, block, block],
        out_specs=[
            block, block, block,
            whole2(rows, 2 * capacity),
            pl.BlockSpec((2, rows, rows), lambda g: (g, 0, 0)),
            whole3(pairs, rows, 8),
            whole3(heads, 16, 128),
        ],
        out_shape=[
            own, own, own,
            jax.ShapeDtypeStruct((rows, 2 * capacity), BF),
            jax.ShapeDtypeStruct((heads, rows, rows), F32),
            jax.ShapeDtypeStruct((pairs, rows, 8), F32),
            jax.ShapeDtypeStruct((heads, 16, 128), BF),
        ],
        scratch_shapes=[
            pltpu.VMEM((rows, rows), BF),
            pltpu.VMEM((rows, rows), F32),
            pltpu.VMEM((pairs, 8, rows), F32),
        ],
        compiler_params=params(),
        cost_estimate=cost(6000, 16000),
        name="prep",
    )(docs, first, take, log_decay, q, k, v)


def arrived(own_ref, hot_ref, left, right):
    extra = dot(hot_ref[...], jnp.concatenate([left, right], axis=0))
    return own_ref[...] + extra.astype(BF)


def state_kernel(hot_ref, ko_ref, vo_ref, left_ref, right_ref, cols_ref, through_ref, k_ref, v_ref, s_ref):
    dk = s_ref.shape[2]
    k = arrived(ko_ref, hot_ref, left_ref[0], right_ref[0])
    v = arrived(vo_ref, hot_ref, left_ref[1], right_ref[1])
    k_ref[...] = k
    v_ref[...] = v
    for t in range(2):
        part = slice(t * dk, (t + 1) * dk)
        kf = (k[:, part].astype(F32) * cols_ref[0, :, t : t + 1]).astype(BF)
        s_ref[t, :dk, :] = dot_tn(kf, v[:, part]).astype(BF)
        s_ref[t, dk:, :] = through_ref[t]


def state(hot, k_own, v_own, left, right, cols, through):
    rows, features = k_own.shape
    pairs = cols.shape[0]
    heads = 2 * pairs
    width = features // pairs
    dk = width // 2
    capacity = left.shape[1]
    block = pl.BlockSpec((rows, width), lambda g: (0, g))
    side = pl.BlockSpec((2, capacity, width), lambda g: (0, 0, g))
    full = jax.ShapeDtypeStruct((rows, features), BF)
    return pl.pallas_call(
        state_kernel,
        grid=(pairs,),
        in_specs=[
            pl.BlockSpec((rows, 2 * capacity), lambda g: (0, 0)),
            block, block, side, side,
            pl.BlockSpec((1, rows, 8), lambda g: (g, 0, 0)),
            pl.BlockSpec((2, 16, 128), lambda g: (g, 0, 0)),
        ],
        out_specs=[block, block, pl.BlockSpec((2, dk + 16, dk), lambda g: (g, 0, 0))],
        out_shape=[full, full, jax.ShapeDtypeStruct((heads, dk + 16, dk), BF)],
        compiler_params=params(),
        cost_estimate=cost(2000, 6000),
        name="state",
    )(hot, k_own, v_own, left, right, cols, through)


def inside_kernel(hot_ref, qo_ref, left_ref, right_ref, k_ref, v_ref, weight_ref, q_ref, p_ref, o_ref):
    rows, width = k_ref.shape
    dk, half = width // 2, rows // 2
    q = arrived(qo_ref, hot_ref, left_ref[0], right_ref[0])
    q_ref[...] = q
    for t in range(2):
        part = slice(t * dk, (t + 1) * dk)
        for i in range(2):
            top, reach = i * half, (i + 1) * half
            scores = dot_nt(q[top : top + half, part], k_ref[:reach, part])
            p = (scores * weight_ref[t, top : top + half, :reach]).astype(BF)
            p_ref[t, top : top + half, :reach] = p
            o_ref[top : top + half, part] = dot(p, v_ref[:reach, part])


def inside(hot, q_own, left, right, k, v, weight):
    rows, features = k.shape
    heads = weight.shape[0]
    pairs = heads // 2
    width = features // pairs
    capacity = left.shape[1]
    block = pl.BlockSpec((rows, width), lambda g: (0, g))
    side = pl.BlockSpec((1, capacity, width), lambda g: (0, 0, g))
    square = pl.BlockSpec((2, rows, rows), lambda g: (g, 0, 0))
    return pl.pallas_call(
        inside_kernel,
        grid=(pairs,),
        in_specs=[
            pl.BlockSpec((rows, 2 * capacity), lambda g: (0, 0)),
            block, side, side, block, block, square,
        ],
        out_specs=[block, square, block],
        out_shape=[
            jax.ShapeDtypeStruct((rows, features), BF),
            jax.ShapeDtypeStruct((heads, rows, rows), BF),
            jax.ShapeDtypeStruct((rows, features), F32),
        ],
        compiler_params=params(),
        cost_estimate=cost(3000, 18000),
        name="inside",
    )(hot, q_own, left, right, k, v, weight)


def joined(near_ref, far_ref, t, dk):
    through = jnp.sum(near_ref[t, dk:, :].astype(F32), axis=0, keepdims=True)
    near = near_ref[t, :dk, :].astype(F32)
    return (near + through * far_ref[t, :dk, :].astype(F32)).astype(BF)


def output_kernel(scale_ref, o_ref, q_ref, near_ref, far_ref, cols_ref, ct_ref, u_ref, h_ref, sums_ref, sq_ref, cross_ref):
    dk = q_ref.shape[1] // 2
    step = pl.program_id(0)

    @pl.when(step == 0)
    def _():
        sq_ref[...] = jnp.zeros_like(sq_ref)
        cross_ref[...] = jnp.zeros_like(cross_ref)

    squares, cross = sq_ref[...], cross_ref[...]
    for t in range(2):
        part = slice(t * dk, (t + 1) * dk)
        h = joined(near_ref, far_ref, t, dk)
        h_ref[t] = h
        outer = dot(q_ref[:, part], h) * cols_ref[0, :, 2 + t : 3 + t]
        u = (o_ref[:, part] + outer) * scale_ref[2 * step + t]
        u_ref[:, part] = u
        squares += u * u
        cross += ct_ref[:, part].astype(F32) * u
    sq_ref[...] = squares
    cross_ref[...] = cross

    @pl.when(step == pl.num_programs(0) - 1)
    def _():
        sums_ref[0:1, :] = jnp.sum(squares.T, axis=0, keepdims=True)
        sums_ref[1:2, :] = jnp.sum(cross.T, axis=0, keepdims=True)


def output(head_scale, o, q, near, far, cols, ct):
    rows, features = q.shape
    pairs = cols.shape[0]
    width = features // pairs
    dk = width // 2
    block = pl.BlockSpec((rows, width), lambda g: (0, g))
    message = pl.BlockSpec((2, dk + 16, dk), lambda g: (g, 0, 0))
    return pl.pallas_call(
        output_kernel,
        grid=(pairs,),
        in_specs=[
            pl.BlockSpec(memory_space=pltpu.SMEM),
            block, block, message, message,
            pl.BlockSpec((1, rows, 8), lambda g: (g, 0, 0)),
            block,
        ],
        out_specs=[
            block,
            pl.BlockSpec((2, dk, dk), lambda g: (g, 0, 0)),
            pl.BlockSpec((2, rows), lambda g: (0, 0)),
        ],
        out_shape=[
            jax.ShapeDtypeStruct((rows, features), F32),
            jax.ShapeDtypeStruct((2 * pairs, dk, dk), BF),
            jax.ShapeDtypeStruct((2, rows), F32),
        ],
        scratch_shapes=[pltpu.VMEM((rows, dk), F32), pltpu.VMEM((rows, dk), F32)],
        compiler_params=params(),
        cost_estimate=cost(400, 8000),
        name="output",
    )(head_scale, o, q, near, far, cols, ct)


def norm_kernel(total, scale_ref, sums_ref, u_ref, ct_ref, q_ref, cols_ref, through_ref, n_ref, g_ref, s_ref, inv_ref, mean_ref):
    dk = q_ref.shape[1] // 2
    step = pl.program_id(0)

    @pl.when(step == 0)
    def _():
        inverse = lax.rsqrt(along_rows(sums_ref[0:1, :], dk) / total + EPSILON)
        inv_ref[...] = inverse
        mean_ref[...] = inverse * inverse * inverse * (along_rows(sums_ref[1:2, :], dk) / total)

    inverse, mean = inv_ref[...], mean_ref[...]
    for t in range(2):
        part = slice(t * dk, (t + 1) * dk)
        u = u_ref[:, part]
        n_ref[:, part] = (u * inverse).astype(BF)
        g = ((inverse * ct_ref[:, part].astype(F32) - u * mean) * scale_ref[2 * step + t]).astype(BF)
        g_ref[:, part] = g
        qe = (q_ref[:, part].astype(F32) * cols_ref[0, :, 2 + t : 3 + t]).astype(BF)
        s_ref[t, :dk, :] = dot_tn(qe, g).astype(BF)
        s_ref[t, dk:, :] = through_ref[t]


def norm(total, head_scale, sums, u, ct, q, cols, through):
    rows, features = q.shape
    pairs = cols.shape[0]
    width = features // pairs
    dk = width // 2
    block = pl.BlockSpec((rows, width), lambda g: (0, g))
    full = jax.ShapeDtypeStruct((rows, features), BF)
    return pl.pallas_call(
        functools.partial(norm_kernel, total),
        grid=(pairs,),
        in_specs=[
            pl.BlockSpec(memory_space=pltpu.SMEM),
            pl.BlockSpec((2, rows), lambda g: (0, 0)),
            block, block, block,
            pl.BlockSpec((1, rows, 8), lambda g: (g, 0, 0)),
            pl.BlockSpec((2, 16, 128), lambda g: (g, 0, 0)),
        ],
        out_specs=[block, block, pl.BlockSpec((2, dk + 16, dk), lambda g: (g, 0, 0))],
        out_shape=[full, full, jax.ShapeDtypeStruct((2 * pairs, dk + 16, dk), BF)],
        scratch_shapes=[pltpu.VMEM((rows, dk), F32), pltpu.VMEM((rows, dk), F32)],
        compiler_params=params(),
        cost_estimate=cost(400, 8000),
        name="norm",
    )(head_scale, sums, u, ct, q, cols, through)


def slots_hot(take_ref, hot_ref, capacity, rows):
    taken = jnp.broadcast_to(take_ref[...], (capacity, rows))
    slot = iota((capacity, rows), 0)
    hot_ref[:capacity, :] = one_hot(taken == slot)
    hot_ref[capacity:, :] = one_hot(taken - (capacity + rows) == slot)


def grad_q_kernel(take_ref, g_ref, k_ref, v_ref, h_ref, weight_ref, cols_ref, dq_ref, z_ref, left_ref, right_ref, hot_ref):
    rows, width = k_ref.shape
    dk, half = width // 2, rows // 2
    capacity = left_ref.shape[1]

    @pl.when(pl.program_id(0) == 0)
    def _():
        slots_hot(take_ref, hot_ref, capacity, rows)

    for t in range(2):
        part = slice(t * dk, (t + 1) * dk)
        for i in range(2):
            top, reach = i * half, (i + 1) * half
            g = g_ref[top : top + half, part]
            scores = dot_nt(g, v_ref[:reach, part])
            z = (scores * weight_ref[t, top : top + half, :reach]).astype(BF)
            z_ref[t, top : top + half, :reach] = z
            outer = dot_nt(g, h_ref[t]) * cols_ref[0, top : top + half, 2 + t : 3 + t]
            dq_ref[top : top + half, part] = (dot(z, k_ref[:reach, part]) + outer).astype(BF)
    back = dot(hot_ref[...], dq_ref[...]).astype(BF)
    left_ref[0] = back[:capacity]
    right_ref[0] = back[capacity:]


def grad_q(take, g, k, v, h, weight, cols, capacity):
    rows, features = k.shape
    pairs = cols.shape[0]
    width = features // pairs
    dk = width // 2
    block = pl.BlockSpec((rows, width), lambda g: (0, g))
    side = pl.BlockSpec((1, capacity, width), lambda g: (0, 0, g))
    square = pl.BlockSpec((2, rows, rows), lambda g: (g, 0, 0))
    return pl.pallas_call(
        grad_q_kernel,
        grid=(pairs,),
        in_specs=[
            pl.BlockSpec((1, rows), lambda g: (0, 0)),
            block, block, block,
            pl.BlockSpec((2, dk, dk), lambda g: (g, 0, 0)),
            square,
            pl.BlockSpec((1, rows, 8), lambda g: (g, 0, 0)),
        ],
        out_specs=[block, square, side, side],
        out_shape=[
            jax.ShapeDtypeStruct((rows, features), BF),
            jax.ShapeDtypeStruct((2 * pairs, rows, rows), BF),
            jax.ShapeDtypeStruct((1, capacity, features), BF),
            jax.ShapeDtypeStruct((1, capacity, features), BF),
        ],
        scratch_shapes=[pltpu.VMEM((2 * capacity, rows), BF)],
        compiler_params=params(),
        cost_estimate=cost(3000, 18000),
        name="grad_q",
    )(take, g, k, v, h, weight, cols)


def inner_kernel(z_ref, p_ref, q_ref, g_ref, dk_ref, dv_ref):
    rows, width = q_ref.shape
    dk, half = width // 2, rows // 2
    for t in range(2):
        part = slice(t * dk, (t + 1) * dk)
        for square, source, target in ((z_ref, q_ref, dk_ref), (p_ref, g_ref, dv_ref)):
            for j in range(2):
                top = j * half
                target[top : top + half, part] = dot_tn(
                    square[t, top:, top : top + half], source[top:, part]
                )


def inner(z, p, q, g):
    rows, features = q.shape
    heads = z.shape[0]
    pairs = heads // 2
    block = pl.BlockSpec((rows, features // pairs), lambda g: (0, g))
    square = pl.BlockSpec((2, rows, rows), lambda g: (g, 0, 0))
    full = jax.ShapeDtypeStruct((rows, features), F32)
    return pl.pallas_call(
        inner_kernel,
        grid=(pairs,),
        in_specs=[square, square, block, block],
        out_specs=[block, block],
        out_shape=[full, full],
        compiler_params=params(),
        cost_estimate=cost(3000, 14000),
        name="inner",
    )(z, p, q, g)


def grad_kv_kernel(take_ref, near_ref, far_ref, k_ref, v_ref, cols_ref, dki_ref, dvi_ref, dk_ref, dv_ref, left_ref, right_ref, hot_ref):
    rows, width = k_ref.shape
    dk = width // 2
    capacity = left_ref.shape[1]

    @pl.when(pl.program_id(0) == 0)
    def _():
        slots_hot(take_ref, hot_ref, capacity, rows)

    for t in range(2):
        part = slice(t * dk, (t + 1) * dk)
        state_grad = joined(near_ref, far_ref, t, dk)
        leaving = cols_ref[0, :, t : t + 1]
        dk_ref[:, part] = (dki_ref[:, part] + leaving * dot_nt(v_ref[:, part], state_grad)).astype(BF)
        dv_ref[:, part] = (dvi_ref[:, part] + leaving * dot(k_ref[:, part], state_grad)).astype(BF)
    for index, source in enumerate((dk_ref, dv_ref)):
        back = dot(hot_ref[...], source[...]).astype(BF)
        left_ref[index] = back[:capacity]
        right_ref[index] = back[capacity:]


def grad_kv(take, near, far, k, v, cols, dk_inner, dv_inner, capacity):
    rows, features = k.shape
    pairs = cols.shape[0]
    width = features // pairs
    dk = width // 2
    block = pl.BlockSpec((rows, width), lambda g: (0, g))
    side = pl.BlockSpec((2, capacity, width), lambda g: (0, 0, g))
    message = pl.BlockSpec((2, dk + 16, dk), lambda g: (g, 0, 0))
    full = jax.ShapeDtypeStruct((rows, features), BF)
    return pl.pallas_call(
        grad_kv_kernel,
        grid=(pairs,),
        in_specs=[
            pl.BlockSpec((1, rows), lambda g: (0, 0)),
            message, message, block, block,
            pl.BlockSpec((1, rows, 8), lambda g: (g, 0, 0)),
            block, block,
        ],
        out_specs=[block, block, side, side],
        out_shape=[
            full, full,
            jax.ShapeDtypeStruct((2, capacity, features), BF),
            jax.ShapeDtypeStruct((2, capacity, features), BF),
        ],
        scratch_shapes=[pltpu.VMEM((2 * capacity, rows), BF)],
        compiler_params=params(),
        cost_estimate=cost(1000, 10000),
        name="grad_kv",
    )(take, near, far, k, v, cols, dk_inner, dv_inner)


def own_kernel(capacity, take_ref, *refs):
    count = (len(refs) - 1) // 2
    hot_ref = refs[-1]
    rows = refs[0].shape[0]

    @pl.when(pl.program_id(0) == 0)
    def _():
        taken = jnp.broadcast_to(take_ref[...], (rows, rows))
        hot_ref[...] = one_hot(taken - capacity == iota((rows, rows), 0))

    for source, target in zip(refs[:count], refs[count : 2 * count]):
        target[...] = dot(hot_ref[...], source[...]).astype(BF)


def own(take, arrays, capacity, cols):
    rows, features = arrays[0].shape
    count = len(arrays)
    block = pl.BlockSpec((rows, cols), lambda g: (0, g))
    full = jax.ShapeDtypeStruct((rows, features), BF)
    return pl.pallas_call(
        functools.partial(own_kernel, capacity),
        grid=(features // cols,),
        in_specs=[pl.BlockSpec((1, rows), lambda g: (0, 0))] + [block] * count,
        out_specs=[block] * count,
        out_shape=[full] * count,
        scratch_shapes=[pltpu.VMEM((rows, rows), BF)],
        compiler_params=params(),
        cost_estimate=cost(540 * count, 2048 * count),
        name="own",
    )(take, *arrays)


def finish_kernel(send_ref, left_ref, right_ref, *refs):
    count = (len(refs) - 1) // 2
    hot_ref = refs[-1]
    rows = refs[0].shape[0]
    capacity = send_ref.shape[1]

    @pl.when(pl.program_id(0) == 0)
    def _():
        line = iota((rows, capacity), 0)
        for side in range(2):
            named = jnp.broadcast_to(send_ref[side : side + 1, :], (rows, capacity))
            hot_ref[:, side * capacity : (side + 1) * capacity] = one_hot(named == line)

    for index in range(count):
        back = jnp.concatenate([left_ref[index], right_ref[index]], axis=0)
        refs[count + index][...] = refs[index][...] + dot(hot_ref[...], back).astype(BF)


def finish(send, left, right, arrays, cols):
    rows, features = arrays[0].shape
    count = len(arrays)
    capacity = send.shape[1]
    block = pl.BlockSpec((rows, cols), lambda g: (0, g))
    side = pl.BlockSpec((count, capacity, cols), lambda g: (0, 0, g))
    full = jax.ShapeDtypeStruct((rows, features), BF)
    return pl.pallas_call(
        finish_kernel,
        grid=(features // cols,),
        in_specs=[pl.BlockSpec((2, capacity), lambda g: (0, 0)), side, side] + [block] * count,
        out_specs=[block] * count,
        out_shape=[full] * count,
        scratch_shapes=[pltpu.VMEM((rows, 2 * capacity), BF)],
        compiler_params=params(),
        cost_estimate=cost(270 * count, 3000 * count),
        name="finish",
    )(send, left, right, *arrays)


def shifted(array, by):
    peers = lax.axis_size("seq")
    return lax.ppermute(
        array, "seq", [(i, i + by) for i in range(peers) if 0 <= i + by < peers]
    )


def carried(message, direction):
    reach = lax.axis_size("seq") // 4
    if reach <= 2:
        return shifted(message, direction), shifted(message, 2 * direction)
    size = message.shape[2]
    own_state = message[:, :size].astype(F32)
    through = jnp.sum(message[:, size:, :1].astype(F32), axis=1, keepdims=True)

    def relay(_, state_here):
        return shifted((through * state_here + own_state).astype(BF), direction).astype(F32)

    incoming = lax.fori_loop(0, reach, relay, jnp.zeros_like(own_state)).astype(BF)
    near = jnp.concatenate([incoming, jnp.zeros_like(message[:, size:])], axis=1)
    return near, jnp.zeros_like(message)


def on_device(
    queries, key_vectors, value_vectors, log_decay, head_scale,
    send_rows, take_rows, doc_lengths, cotangent,
):
    rows, features = queries.shape
    heads = head_scale.shape[0]
    capacity = send_rows.shape[2]
    cols = 2 * (features // heads)
    send = send_rows.reshape(2, capacity)
    take = take_rows.reshape(1, rows)
    first = (lax.axis_index("seq") * rows).astype(jnp.int32).reshape(1)
    total = features * lax.axis_size("head")

    kv_left, kv_right = pick(send, (key_vectors, value_vectors), cols)
    q_left, q_right = pick(send, (queries,), cols)
    kv_before, kv_after = shifted(kv_right, 1), shifted(kv_left, -1)
    q_before, q_after = shifted(q_right, 1), shifted(q_left, -1)
    q_own, k_own, v_own, hot, weight, columns, through = prep(
        doc_lengths, first, take, log_decay, queries, key_vectors, value_vectors, capacity
    )
    k, v, message = state(hot, k_own, v_own, kv_before, kv_after, columns, through)
    near, far = carried(message, 1)
    q, probs, o_inside = inside(hot, q_own, q_before, q_after, k, v, weight)
    u, state_low, sums = output(head_scale, o_inside, q, near, far, columns, cotangent)
    sums = lax.psum(sums, "head")
    normed, g, grad_message = norm(total, head_scale, sums, u, cotangent, q, columns, through)
    grad_near, grad_far = carried(grad_message, -1)
    dq, z, dq_left, dq_right = grad_q(take, g, k, v, state_low, weight, columns, capacity)
    dq_before, dq_after = shifted(dq_right, 1), shifted(dq_left, -1)
    dk_inner, dv_inner = inner(z, probs, q, g)
    dk, dv, kv_left, kv_right = grad_kv(
        take, grad_near, grad_far, k, v, columns, dk_inner, dv_inner, capacity
    )
    dkv_before, dkv_after = shifted(kv_right, 1), shifted(kv_left, -1)
    dq_own, dk_own, dv_own = own(take, (dq, dk, dv), capacity, cols)
    (grad_queries,) = finish(send, dq_before, dq_after, (dq_own,), cols)
    grad_keys, grad_values = finish(send, dkv_before, dkv_after, (dk_own, dv_own), cols)
    return normed, grad_queries, grad_keys, grad_values


def solution(mesh):
    both = P("seq", "head")
    in_specs = (both, both, both, both, P("head"), P("seq", None, None), P("seq"), P(), both)
    return jax.shard_map(
        on_device, mesh=mesh, in_specs=in_specs, out_specs=(both,) * 4, check_vma=False
    )
```

```python
import functools
import math

import jax
import jax.numpy as jnp
from jax import lax
from jax.experimental import pallas as pl
from jax.experimental.pallas import tpu as pltpu
from jax.sharding import PartitionSpec as P

EPSILON = 1e-05
LOG2E = math.log2(math.e)
MASKED = -1e30
MIB = 1024 * 1024
BF = jnp.bfloat16
F32 = jnp.float32
NT = (((1,), (1,)), ((), ()))
TN = (((0,), (0,)), ((), ()))


def dot(a, b):
    return jnp.dot(a, b, preferred_element_type=F32)


def dot_nt(a, b):
    return lax.dot_general(a, b, NT, preferred_element_type=F32)


def dot_tn(a, b):
    return lax.dot_general(a, b, TN, preferred_element_type=F32)


def along_rows(row, lanes=128):
    return jnp.broadcast_to(row, (lanes, row.shape[1])).T


def iota(shape, dim):
    return lax.broadcasted_iota(jnp.int32, shape, dim)


def one_hot(hit):
    return jnp.where(hit, 1.0, 0.0).astype(BF)


def in_hbm(shape, dtype):
    return pltpu.HBM(shape, dtype)


def stay(*arrays):
    return [pltpu.with_memory_space_constraint(a, pltpu.HBM) for a in arrays]


def params(mib=20):
    return pltpu.CompilerParams(vmem_limit_bytes=mib * MIB)


def planned(us):
    return pl.CostEstimate(flops=int(us * 1.1e9), bytes_accessed=1_000_000, transcendentals=0)


def pick_rows(hot_ref, sources, left_ref, right_ref):
    capacity = left_ref.shape[1]
    for index, source in enumerate(sources):
        picked = dot(hot_ref[...], source[...]).astype(BF)
        left_ref[index] = picked[:capacity]
        right_ref[index] = picked[capacity:]


def pick_kernel(send_ref, *refs):
    *sources, left_ref, right_ref, hot_ref = refs
    rows = sources[0].shape[0]
    capacity = send_ref.shape[1]

    @pl.when(pl.program_id(0) == 0)
    def _():
        lane = iota((capacity, 128), 1)
        for side in range(2):
            named = along_rows(send_ref[side : side + 1, :], 128)
            for start in range(0, rows, 128):
                hot_ref[side * capacity : (side + 1) * capacity, start : start + 128] = one_hot(
                    named == lane + start
                )

    pick_rows(hot_ref, sources, left_ref, right_ref)


def pick(send, arrays, cols):
    rows, features = arrays[0].shape
    capacity = send.shape[1]
    count = len(arrays)
    block = pl.BlockSpec((rows, cols), lambda g: (0, g))
    out = pl.BlockSpec((count, capacity, cols), lambda g: (0, 0, g))
    shape = jax.ShapeDtypeStruct((count, capacity, features), BF)
    return pl.pallas_call(
        pick_kernel,
        grid=(features // cols,),
        in_specs=[pl.BlockSpec((2, capacity), lambda g: (0, 0))] + [block] * count,
        out_specs=[out, out, pl.BlockSpec((2 * capacity, rows), lambda g: (0, 0))],
        out_shape=[shape, shape, in_hbm((2 * capacity, rows), BF)],
        compiler_params=params(56),
        cost_estimate=planned(2),
        name="pick",
    )(send, *arrays)


def prep_kernel(
    docs_ref, first_ref, take_ref, log_ref, named_ref, q_ref, k_ref, v_ref,
    left_ref, right_ref, qo_ref, ko_ref, vo_ref, hot_ref, mask_ref, cols_ref, rows_ref, through_ref, own_ref,
):
    rows = q_ref.shape[0]
    heads = log_ref.shape[1]
    capacity = hot_ref.shape[1] // 2

    @pl.when(pl.program_id(0) == 0)
    def _():
        first = first_ref[0]
        position = first + iota((rows, 1), 0)
        position_row = first + iota((1, rows), 1)
        segment = jnp.zeros((rows, 1), jnp.int32)
        segment_row = jnp.zeros((1, rows), jnp.int32)
        segment_first = jnp.int32(0)
        segment_last = jnp.int32(0)
        opens_first = jnp.int32(0)
        opens = jnp.int32(0)
        start = jnp.int32(0)
        for n in range(docs_ref.shape[0]):
            segment += (position >= start).astype(jnp.int32)
            segment_row += (position_row >= start).astype(jnp.int32)
            segment_first += (first >= start).astype(jnp.int32)
            segment_last += (first + rows - 1 >= start).astype(jnp.int32)
            opens_first += (first == start).astype(jnp.int32)
            opens += ((start >= first) & (start < first + rows)).astype(jnp.int32)
            start += docs_ref[n]
        below = iota((rows, rows), 0) >= iota((rows, rows), 1)
        scale = -0.5 * math.log2(q_ref.shape[1] // 2)
        mask_ref[...] = jnp.where((segment == segment_row) & below, scale, MASKED)
        triangle = one_hot(below)
        logs = jnp.concatenate([log_ref[...], jnp.zeros((rows, 128 - heads), F32)], axis=1)
        high = logs.astype(BF)
        rest = logs - high.astype(F32)
        middle = rest.astype(BF)
        low = (rest - middle.astype(F32)).astype(BF)
        running = (dot(triangle, high) + (dot(triangle, middle) + dot(triangle, low))) * LOG2E
        turned = running.T
        final = running[rows - 1 : rows, :]
        keep_f = segment == segment_last
        keep_e = (segment == segment_first) & (opens_first == 0)
        leaving = jnp.where(keep_f, jnp.exp2(final - running), 0.0)
        entering = jnp.where(keep_e, jnp.exp2(running + scale), 0.0)
        through = jnp.where(opens == 0, jnp.exp2(final), 0.0)
        t_high = through.astype(BF).astype(F32)
        t_middle = (through - t_high).astype(BF).astype(F32)
        t_low = through - t_high - t_middle
        line = iota((16, 128), 0)
        for h in range(heads):
            g, t = h // 2, h % 2
            cols_ref[g, :, t : t + 1] = leaving[:, h : h + 1]
            cols_ref[g, :, 2 + t : 3 + t] = entering[:, h : h + 1]
            cols_ref[g, :, 4 + t : 5 + t] = running[:, h : h + 1]
            rows_ref[g, t : t + 1, :] = turned[h : h + 1, :]
            parts = [
                jnp.broadcast_to(x[:, h : h + 1], (16, 128)) for x in (t_high, t_middle, t_low)
            ]
            through_ref[h] = jnp.where(
                line == 0,
                parts[0],
                jnp.where(line == 1, parts[1], jnp.where(line == 2, parts[2], 0.0)),
            ).astype(BF)
        lane = iota((rows, 128), 1)
        taken = along_rows(take_ref[...], 128)
        for start_row in range(0, rows, 128):
            own_ref[:, start_row : start_row + 128] = one_hot(
                taken - capacity == lane + start_row
            )
        hot_ref[:, :capacity] = one_hot(taken == lane)
        hot_ref[:, capacity:] = one_hot(taken - (capacity + rows) == lane)

    pick_rows(named_ref, (q_ref,), left_ref, right_ref)
    own = own_ref[...]
    qo_ref[...] = dot(own, q_ref[...]).astype(BF)
    ko_ref[...] = dot(own, k_ref[...]).astype(BF)
    vo_ref[...] = dot(own, v_ref[...]).astype(BF)


def prep(docs, first, take, log_decay, named, q, k, v, capacity):
    rows, features = q.shape
    heads = log_decay.shape[1]
    pairs = heads // 2
    cols = features // pairs
    smem = pl.BlockSpec(memory_space=pltpu.SMEM)
    block = pl.BlockSpec((rows, cols), lambda g: (0, g))
    whole2 = lambda a, b: pl.BlockSpec((a, b), lambda g: (0, 0))
    whole3 = lambda a, b, c: pl.BlockSpec((a, b, c), lambda g: (0, 0, 0))
    side = pl.BlockSpec((1, capacity, cols), lambda g: (0, 0, g))
    own = jax.ShapeDtypeStruct((rows, features), BF)
    slots = jax.ShapeDtypeStruct((1, capacity, features), BF)
    return pl.pallas_call(
        prep_kernel,
        grid=(pairs,),
        in_specs=[
            smem, smem, whole2(1, rows), whole2(rows, heads),
            whole2(2 * capacity, rows), block, block, block,
        ],
        out_specs=[
            side, side, block, block, block,
            whole2(rows, 2 * capacity),
            whole2(rows, rows),
            whole3(pairs, rows, 8),
            whole3(pairs, 8, rows),
            whole3(heads, 16, 128),
        ],
        out_shape=[
            slots, slots, own, own, own,
            jax.ShapeDtypeStruct((rows, 2 * capacity), BF),
            in_hbm((rows, rows), F32),
            in_hbm((pairs, rows, 8), F32),
            in_hbm((pairs, 8, rows), F32),
            in_hbm((heads, 16, 128), BF),
        ],
        scratch_shapes=[pltpu.VMEM((rows, rows), BF)],
        compiler_params=params(),
        cost_estimate=planned(30),
        name="prep",
    )(docs, first, take, log_decay, *stay(named, q, k, v))


def arrived(own_ref, hot_ref, left, right):
    extra = dot(hot_ref[...], jnp.concatenate([left, right], axis=0))
    return own_ref[...] + extra.astype(BF)


def state_kernel(hot_ref, ko_ref, vo_ref, left_ref, right_ref, cols_ref, through_ref, k_ref, v_ref, s_ref):
    dk = s_ref.shape[2]
    k = arrived(ko_ref, hot_ref, left_ref[0], right_ref[0])
    v = arrived(vo_ref, hot_ref, left_ref[1], right_ref[1])
    k_ref[...] = k
    v_ref[...] = v
    for t in range(2):
        part = slice(t * dk, (t + 1) * dk)
        kf = (k[:, part].astype(F32) * cols_ref[0, :, t : t + 1]).astype(BF)
        s_ref[t, :dk, :] = dot_tn(kf, v[:, part]).astype(BF)
        s_ref[t, dk:, :] = through_ref[t]


def state(hot, k_own, v_own, left, right, cols, through):
    rows, features = k_own.shape
    pairs = cols.shape[0]
    heads = 2 * pairs
    width = features // pairs
    dk = width // 2
    capacity = left.shape[1]
    block = pl.BlockSpec((rows, width), lambda g: (0, g))
    side = pl.BlockSpec((2, capacity, width), lambda g: (0, 0, g))
    full = in_hbm((rows, features), BF)
    return pl.pallas_call(
        state_kernel,
        grid=(pairs,),
        in_specs=[
            pl.BlockSpec((rows, 2 * capacity), lambda g: (0, 0)),
            block, block, side, side,
            pl.BlockSpec((1, rows, 8), lambda g: (g, 0, 0)),
            pl.BlockSpec((2, 16, 128), lambda g: (g, 0, 0)),
        ],
        out_specs=[block, block, pl.BlockSpec((2, dk + 16, dk), lambda g: (g, 0, 0))],
        out_shape=[full, full, jax.ShapeDtypeStruct((heads, dk + 16, dk), BF)],
        compiler_params=params(),
        cost_estimate=planned(30),
        name="state",
    )(hot, k_own, v_own, left, right, *stay(cols, through))


def decay(cols_ref, rows_ref, mask_ref, t, top, half, reach):
    column = cols_ref[0, top : top + half, 4 + t : 5 + t]
    row = rows_ref[0, t : t + 1, :reach]
    return jnp.exp2((column - row) + mask_ref[top : top + half, :reach])


def inside_kernel(hot_ref, qo_ref, left_ref, right_ref, k_ref, v_ref, mask_ref, cols_ref, rows_ref, q_ref, o_ref):
    rows, width = k_ref.shape
    dk, half = width // 2, rows // 2
    q = arrived(qo_ref, hot_ref, left_ref[0], right_ref[0])
    q_ref[...] = q
    for t in range(2):
        part = slice(t * dk, (t + 1) * dk)
        for i in range(2):
            top, reach = i * half, (i + 1) * half
            scores = dot_nt(q[top : top + half, part], k_ref[:reach, part])
            weight = decay(cols_ref, rows_ref, mask_ref, t, top, half, reach)
            p = (scores * weight).astype(BF)
            o_ref[top : top + half, part] = dot(p, v_ref[:reach, part])


def tables(rows):
    return [
        pl.BlockSpec((rows, rows), lambda g: (0, 0)),
        pl.BlockSpec((1, rows, 8), lambda g: (g, 0, 0)),
        pl.BlockSpec((1, 8, rows), lambda g: (g, 0, 0)),
    ]


def inside(hot, q_own, left, right, k, v, mask, cols, turned):
    rows, features = k.shape
    pairs = cols.shape[0]
    width = features // pairs
    capacity = left.shape[1]
    block = pl.BlockSpec((rows, width), lambda g: (0, g))
    side = pl.BlockSpec((1, capacity, width), lambda g: (0, 0, g))
    return pl.pallas_call(
        inside_kernel,
        grid=(pairs,),
        in_specs=[
            pl.BlockSpec((rows, 2 * capacity), lambda g: (0, 0)),
            block, side, side, block, block, *tables(rows),
        ],
        out_specs=[block, block],
        out_shape=[
            in_hbm((rows, features), BF),
            jax.ShapeDtypeStruct((rows, features), F32),
        ],
        compiler_params=params(),
        cost_estimate=planned(30),
        name="inside",
    )(hot, q_own, left, right, *stay(k, v, mask, cols, turned))


def joined(near_ref, far_ref, t, dk):
    through = jnp.sum(near_ref[t, dk:, :].astype(F32), axis=0, keepdims=True)
    near = near_ref[t, :dk, :].astype(F32)
    return (near + through * far_ref[t, :dk, :].astype(F32)).astype(BF)


def output_kernel(scale_ref, o_ref, q_ref, near_ref, far_ref, cols_ref, ct_ref, u_ref, h_ref, sums_ref, sq_ref, cross_ref):
    dk = q_ref.shape[1] // 2
    step = pl.program_id(0)

    @pl.when(step == 0)
    def _():
        sq_ref[...] = jnp.zeros_like(sq_ref)
        cross_ref[...] = jnp.zeros_like(cross_ref)

    squares, cross = sq_ref[...], cross_ref[...]
    for t in range(2):
        part = slice(t * dk, (t + 1) * dk)
        h = joined(near_ref, far_ref, t, dk)
        h_ref[t] = h
        outer = dot(q_ref[:, part], h) * cols_ref[0, :, 2 + t : 3 + t]
        u = (o_ref[:, part] + outer) * scale_ref[2 * step + t]
        u_ref[:, part] = u
        squares += u * u
        cross += ct_ref[:, part].astype(F32) * u
    sq_ref[...] = squares
    cross_ref[...] = cross

    @pl.when(step == pl.num_programs(0) - 1)
    def _():
        sums_ref[0:1, :] = jnp.sum(squares.T, axis=0, keepdims=True)
        sums_ref[1:2, :] = jnp.sum(cross.T, axis=0, keepdims=True)


def output(head_scale, o, q, near, far, cols, ct):
    rows, features = q.shape
    pairs = cols.shape[0]
    width = features // pairs
    dk = width // 2
    block = pl.BlockSpec((rows, width), lambda g: (0, g))
    message = pl.BlockSpec((2, dk + 16, dk), lambda g: (g, 0, 0))
    return pl.pallas_call(
        output_kernel,
        grid=(pairs,),
        in_specs=[
            pl.BlockSpec(memory_space=pltpu.SMEM),
            block, block, message, message,
            pl.BlockSpec((1, rows, 8), lambda g: (g, 0, 0)),
            block,
        ],
        out_specs=[
            block,
            pl.BlockSpec((2, dk, dk), lambda g: (g, 0, 0)),
            pl.BlockSpec((2, rows), lambda g: (0, 0)),
        ],
        out_shape=[
            in_hbm((rows, features), F32),
            in_hbm((2 * pairs, dk, dk), BF),
            jax.ShapeDtypeStruct((2, rows), F32),
        ],
        scratch_shapes=[pltpu.VMEM((rows, dk), F32), pltpu.VMEM((rows, dk), F32)],
        compiler_params=params(),
        cost_estimate=planned(3),
        name="output",
    )(head_scale, o, *stay(q), near, far, *stay(cols, ct))


def norm_kernel(total, scale_ref, sums_ref, u_ref, ct_ref, q_ref, cols_ref, through_ref, n_ref, g_ref, s_ref, inv_ref, mean_ref):
    dk = q_ref.shape[1] // 2
    step = pl.program_id(0)

    @pl.when(step == 0)
    def _():
        inverse = lax.rsqrt(along_rows(sums_ref[0:1, :], dk) / total + EPSILON)
        inv_ref[...] = inverse
        mean_ref[...] = inverse * inverse * inverse * (along_rows(sums_ref[1:2, :], dk) / total)

    inverse, mean = inv_ref[...], mean_ref[...]
    for t in range(2):
        part = slice(t * dk, (t + 1) * dk)
        u = u_ref[:, part]
        n_ref[:, part] = (u * inverse).astype(BF)
        g = ((inverse * ct_ref[:, part].astype(F32) - u * mean) * scale_ref[2 * step + t]).astype(BF)
        g_ref[:, part] = g
        qe = (q_ref[:, part].astype(F32) * cols_ref[0, :, 2 + t : 3 + t]).astype(BF)
        s_ref[t, :dk, :] = dot_tn(qe, g).astype(BF)
        s_ref[t, dk:, :] = through_ref[t]


def norm(total, head_scale, sums, u, ct, q, cols, through):
    rows, features = q.shape
    pairs = cols.shape[0]
    width = features // pairs
    dk = width // 2
    block = pl.BlockSpec((rows, width), lambda g: (0, g))
    full = jax.ShapeDtypeStruct((rows, features), BF)
    return pl.pallas_call(
        functools.partial(norm_kernel, total),
        grid=(pairs,),
        in_specs=[
            pl.BlockSpec(memory_space=pltpu.SMEM),
            pl.BlockSpec((2, rows), lambda g: (0, 0)),
            block, block, block,
            pl.BlockSpec((1, rows, 8), lambda g: (g, 0, 0)),
            pl.BlockSpec((2, 16, 128), lambda g: (g, 0, 0)),
        ],
        out_specs=[block, block, pl.BlockSpec((2, dk + 16, dk), lambda g: (g, 0, 0))],
        out_shape=[full, full, jax.ShapeDtypeStruct((2 * pairs, dk + 16, dk), BF)],
        scratch_shapes=[pltpu.VMEM((rows, dk), F32), pltpu.VMEM((rows, dk), F32)],
        compiler_params=params(),
        cost_estimate=planned(4),
        name="norm",
    )(head_scale, sums, *stay(u, ct, q, cols, through))


def slots_hot(take_ref, hot_ref, capacity, rows):
    taken = jnp.broadcast_to(take_ref[...], (capacity, rows))
    slot = iota((capacity, rows), 0)
    hot_ref[:capacity, :] = one_hot(taken == slot)
    hot_ref[capacity:, :] = one_hot(taken - (capacity + rows) == slot)


def grad_inner_kernel(take_ref, g_ref, q_ref, k_ref, v_ref, h_ref, mask_ref, cols_ref, rows_ref, dq_ref, dk_ref, dv_ref, left_ref, right_ref, hot_ref):
    rows, width = k_ref.shape
    dk, half = width // 2, rows // 2
    capacity = left_ref.shape[1]

    @pl.when(pl.program_id(0) == 0)
    def _():
        slots_hot(take_ref, hot_ref, capacity, rows)

    for t in range(2):
        part = slice(t * dk, (t + 1) * dk)
        for i in (1, 0):
            top, reach = i * half, (i + 1) * half
            here = slice(top, top + half)
            g, q = g_ref[here, part], q_ref[here, part]
            k, v = k_ref[:reach, part], v_ref[:reach, part]
            weight = decay(cols_ref, rows_ref, mask_ref, t, top, half, reach)
            z = (dot_nt(g, v) * weight).astype(BF)
            p = (dot_nt(q, k) * weight).astype(BF)
            outer = dot_nt(g, h_ref[t]) * cols_ref[0, here, 2 + t : 3 + t]
            dq_ref[here, part] = (dot(z, k) + outer).astype(BF)
            if i:
                dk_ref[:reach, part] = dot_tn(z, q)
                dv_ref[:reach, part] = dot_tn(p, g)
            else:
                dk_ref[:reach, part] += dot_tn(z, q)
                dv_ref[:reach, part] += dot_tn(p, g)
    back = dot(hot_ref[...], dq_ref[...]).astype(BF)
    left_ref[0] = back[:capacity]
    right_ref[0] = back[capacity:]


def grad_inner(take, g, q, k, v, h, mask, cols, turned, capacity):
    rows, features = k.shape
    pairs = cols.shape[0]
    width = features // pairs
    dk = width // 2
    block = pl.BlockSpec((rows, width), lambda g: (0, g))
    side = pl.BlockSpec((1, capacity, width), lambda g: (0, 0, g))
    full = jax.ShapeDtypeStruct((rows, features), F32)
    return pl.pallas_call(
        grad_inner_kernel,
        grid=(pairs,),
        in_specs=[
            pl.BlockSpec((1, rows), lambda g: (0, 0)),
            block, block, block, block,
            pl.BlockSpec((2, dk, dk), lambda g: (g, 0, 0)),
            *tables(rows),
        ],
        out_specs=[block, block, block, side, side],
        out_shape=[
            jax.ShapeDtypeStruct((rows, features), BF),
            full, full,
            jax.ShapeDtypeStruct((1, capacity, features), BF),
            jax.ShapeDtypeStruct((1, capacity, features), BF),
        ],
        scratch_shapes=[pltpu.VMEM((2 * capacity, rows), BF)],
        compiler_params=params(),
        cost_estimate=planned(30),
        name="grad_inner",
    )(take, g, *stay(q, k, v, h, mask, cols, turned))


def grad_kv_kernel(take_ref, near_ref, far_ref, k_ref, v_ref, cols_ref, dki_ref, dvi_ref, dk_ref, dv_ref, left_ref, right_ref, hot_ref):
    rows, width = k_ref.shape
    dk = width // 2
    capacity = left_ref.shape[1]

    @pl.when(pl.program_id(0) == 0)
    def _():
        slots_hot(take_ref, hot_ref, capacity, rows)

    for t in range(2):
        part = slice(t * dk, (t + 1) * dk)
        state_grad = joined(near_ref, far_ref, t, dk)
        leaving = cols_ref[0, :, t : t + 1]
        dk_ref[:, part] = (dki_ref[:, part] + leaving * dot_nt(v_ref[:, part], state_grad)).astype(BF)
        dv_ref[:, part] = (dvi_ref[:, part] + leaving * dot(k_ref[:, part], state_grad)).astype(BF)
    for index, source in enumerate((dk_ref, dv_ref)):
        back = dot(hot_ref[...], source[...]).astype(BF)
        left_ref[index] = back[:capacity]
        right_ref[index] = back[capacity:]


def grad_kv(take, near, far, k, v, cols, dk_inner, dv_inner, capacity):
    rows, features = k.shape
    pairs = cols.shape[0]
    width = features // pairs
    dk = width // 2
    block = pl.BlockSpec((rows, width), lambda g: (0, g))
    side = pl.BlockSpec((2, capacity, width), lambda g: (0, 0, g))
    message = pl.BlockSpec((2, dk + 16, dk), lambda g: (g, 0, 0))
    full = jax.ShapeDtypeStruct((rows, features), BF)
    return pl.pallas_call(
        grad_kv_kernel,
        grid=(pairs,),
        in_specs=[
            pl.BlockSpec((1, rows), lambda g: (0, 0)),
            message, message, block, block,
            pl.BlockSpec((1, rows, 8), lambda g: (g, 0, 0)),
            block, block,
        ],
        out_specs=[block, block, side, side],
        out_shape=[
            full, full,
            jax.ShapeDtypeStruct((2, capacity, features), BF),
            jax.ShapeDtypeStruct((2, capacity, features), BF),
        ],
        scratch_shapes=[pltpu.VMEM((2 * capacity, rows), BF)],
        compiler_params=params(),
        cost_estimate=planned(30),
        name="grad_kv",
    )(take, near, far, *stay(k, v, cols), dk_inner, dv_inner)


def own_kernel(capacity, count, take_ref, *refs):
    hot_ref = refs[-1]
    rows = refs[0].shape[0]

    @pl.when(pl.program_id(0) == 0)
    def _():
        taken = jnp.broadcast_to(take_ref[...], (rows, rows))
        hot_ref[...] = one_hot(taken - capacity == iota((rows, rows), 0))

    for source, target in zip(refs[:count], refs[-1 - count : -1]):
        target[...] = dot(hot_ref[...], source[...]).astype(BF)


def own(take, arrays, capacity, cols, after=None):
    rows, features = arrays[0].shape
    count = len(arrays)
    block = pl.BlockSpec((rows, cols), lambda g: (0, g))
    full = jax.ShapeDtypeStruct((rows, features), BF)
    later = [] if after is None else [after]
    return pl.pallas_call(
        functools.partial(own_kernel, capacity, count),
        grid=(features // cols,),
        in_specs=[pl.BlockSpec((1, rows), lambda g: (0, 0))]
        + [block] * count
        + [pl.BlockSpec((16, 128), lambda g: (0, 0))] * len(later),
        out_specs=[block] * count,
        out_shape=[full] * count,
        scratch_shapes=[pltpu.VMEM((rows, rows), BF)],
        compiler_params=params(),
        cost_estimate=planned(2),
        name="own",
    )(take, *arrays, *later)


def finish_kernel(send_ref, left_ref, right_ref, *refs):
    count = (len(refs) - 1) // 2
    hot_ref = refs[-1]
    rows = refs[0].shape[0]
    capacity = send_ref.shape[1]

    @pl.when(pl.program_id(0) == 0)
    def _():
        line = iota((rows, capacity), 0)
        for side in range(2):
            named = jnp.broadcast_to(send_ref[side : side + 1, :], (rows, capacity))
            hot_ref[:, side * capacity : (side + 1) * capacity] = one_hot(named == line)

    for index in range(count):
        back = jnp.concatenate([left_ref[index], right_ref[index]], axis=0)
        refs[count + index][...] = refs[index][...] + dot(hot_ref[...], back).astype(BF)


def finish(send, left, right, arrays, cols):
    rows, features = arrays[0].shape
    count = len(arrays)
    capacity = send.shape[1]
    block = pl.BlockSpec((rows, cols), lambda g: (0, g))
    side = pl.BlockSpec((count, capacity, cols), lambda g: (0, 0, g))
    full = jax.ShapeDtypeStruct((rows, features), BF)
    return pl.pallas_call(
        finish_kernel,
        grid=(features // cols,),
        in_specs=[pl.BlockSpec((2, capacity), lambda g: (0, 0)), side, side] + [block] * count,
        out_specs=[block] * count,
        out_shape=[full] * count,
        scratch_shapes=[pltpu.VMEM((rows, 2 * capacity), BF)],
        compiler_params=params(),
        cost_estimate=planned(2),
        name="finish",
    )(send, left, right, *arrays)


def shifted(array, by):
    peers = lax.axis_size("seq")
    return lax.ppermute(
        array, "seq", [(i, i + by) for i in range(peers) if 0 <= i + by < peers]
    )


def carried(message, direction):
    reach = lax.axis_size("seq") // 4
    if reach <= 2:
        return shifted(message, direction), shifted(message, 2 * direction)
    size = message.shape[2]
    own_state = message[:, :size].astype(F32)
    through = jnp.sum(message[:, size:, :1].astype(F32), axis=1, keepdims=True)

    def relay(_, state_here):
        return shifted((through * state_here + own_state).astype(BF), direction).astype(F32)

    incoming = lax.fori_loop(0, reach, relay, jnp.zeros_like(own_state)).astype(BF)
    near = jnp.concatenate([incoming, jnp.zeros_like(message[:, size:])], axis=1)
    return near, jnp.zeros_like(message)


def on_device(
    queries, key_vectors, value_vectors, log_decay, head_scale,
    send_rows, take_rows, doc_lengths, cotangent,
):
    rows, features = queries.shape
    heads = head_scale.shape[0]
    capacity = send_rows.shape[2]
    cols = 2 * (features // heads)
    send = send_rows.reshape(2, capacity)
    take = take_rows.reshape(1, rows)
    first = (lax.axis_index("seq") * rows).astype(jnp.int32).reshape(1)
    total = features * lax.axis_size("head")

    kv_left, kv_right, named = pick(send, (key_vectors, value_vectors), cols)
    kv_before, kv_after = shifted(kv_right, 1), shifted(kv_left, -1)
    q_left, q_right, q_own, k_own, v_own, hot, mask, columns, turned, through = prep(
        doc_lengths, first, take, log_decay, named, queries, key_vectors, value_vectors, capacity
    )
    q_before, q_after = shifted(q_right, 1), shifted(q_left, -1)
    k, v, message = state(hot, k_own, v_own, kv_before, kv_after, columns, through)
    near, far = carried(message, 1)
    q, o_inside = inside(hot, q_own, q_before, q_after, k, v, mask, columns, turned)
    u, state_low, sums = output(head_scale, o_inside, q, near, far, columns, cotangent)
    sums = lax.psum(sums, "head")
    normed, g, grad_message = norm(total, head_scale, sums, u, cotangent, q, columns, through)
    grad_near, grad_far = carried(grad_message, -1)
    dq, dk_inner, dv_inner, dq_left, dq_right = grad_inner(
        take, g, q, k, v, state_low, mask, columns, turned, capacity
    )
    dq_before, dq_after = shifted(dq_right, 1), shifted(dq_left, -1)
    dk, dv, kv_left, kv_right = grad_kv(
        take, grad_near, grad_far, k, v, columns, dk_inner, dv_inner, capacity
    )
    dkv_before, dkv_after = shifted(kv_right, 1), shifted(kv_left, -1)
    (dq_own,) = own(take, (dq,), capacity, cols, dk)
    (grad_queries,) = finish(send, dq_before, dq_after, (dq_own,), cols)
    dk_own, dv_own = own(take, (dk, dv), capacity, cols, *stay(grad_queries))
    grad_keys, grad_values = finish(send, dkv_before, dkv_after, (dk_own, dv_own), cols)
    return normed, grad_queries, grad_keys, grad_values


def solution(mesh):
    both = P("seq", "head")
    in_specs = (both, both, both, both, P("head"), P("seq", None, None), P("seq"), P(), both)
    return jax.shard_map(
        on_device, mesh=mesh, in_specs=in_specs, out_specs=(both,) * 4, check_vma=False
    )
```

```python
import functools
import math

import jax
import jax.numpy as jnp
from jax import lax
from jax.experimental import pallas as pl
from jax.experimental.pallas import tpu as pltpu
from jax.sharding import PartitionSpec as P

EPSILON = 1e-05
LOG2E = math.log2(math.e)
MASKED = -1e30
MIB = 1024 * 1024
BF = jnp.bfloat16
F32 = jnp.float32
NT = (((1,), (1,)), ((), ()))
TN = (((0,), (0,)), ((), ()))
CHUNK = 256


def dot(a, b):
    return jnp.dot(a, b, preferred_element_type=F32)


def dot_nt(a, b):
    return lax.dot_general(a, b, NT, preferred_element_type=F32)


def dot_tn(a, b):
    return lax.dot_general(a, b, TN, preferred_element_type=F32)


def along_rows(row, lanes=128):
    return jnp.broadcast_to(row, (lanes, row.shape[1])).T


def iota(shape, dim):
    return lax.broadcasted_iota(jnp.int32, shape, dim)


def one_hot(hit):
    return jnp.where(hit, 1.0, 0.0).astype(BF)


def pieces(x):
    high = x.astype(BF)
    rest = x - high.astype(F32)
    middle = rest.astype(BF)
    return high, middle, (rest - middle.astype(F32)).astype(BF)


def chunks(features):
    return [slice(start, start + CHUNK) for start in range(0, features, CHUNK)]


def head_slices(features, heads):
    width = features // heads
    return [slice(h * width, (h + 1) * width) for h in range(heads)]


def local(kernel, name, us, out_shape, operands, scalars=0, scratch=(), spaces=None):
    vmem = pl.BlockSpec(memory_space=pltpu.VMEM)
    smem = pl.BlockSpec(memory_space=pltpu.SMEM)
    specs = [smem] * scalars + [vmem] * (len(operands) - scalars)
    if spaces is not None:
        specs = [pl.BlockSpec(memory_space=space) for space in spaces]
    return pl.pallas_call(
        kernel,
        in_specs=specs,
        out_specs=[vmem] * len(out_shape),
        out_shape=out_shape,
        scratch_shapes=list(scratch),
        compiler_params=pltpu.CompilerParams(vmem_limit_bytes=16 * MIB),
        cost_estimate=pl.CostEstimate(
            flops=int(us * 1.1e9), bytes_accessed=1_000_000, transcendentals=0
        ),
        name=name,
    )(*operands)


def sds(shape, dtype=BF):
    return jax.ShapeDtypeStruct(shape, dtype)


def pick_kernel(send_hbm, k_hbm, v_hbm, left_ref, right_ref, hot_ref, send_ref, k_ref, v_ref, sem):
    rows, features = k_ref.shape
    capacity = send_ref.shape[1]
    named_copy = pltpu.make_async_copy(send_hbm, send_ref, sem.at[0])
    named_copy.start()
    copies = []
    for source, target in ((k_hbm, k_ref), (v_hbm, v_ref)):
        for part in chunks(features):
            copy = pltpu.make_async_copy(
                source.at[:, part], target.at[:, part], sem.at[1 + len(copies)]
            )
            copy.start()
            copies.append(copy)
    named_copy.wait()
    lane = iota((capacity, 128), 1)
    for side in range(2):
        named = along_rows(send_ref[side : side + 1, :])
        for start in range(0, rows, 128):
            hot_ref[side * capacity : (side + 1) * capacity, start : start + 128] = one_hot(
                named == lane + start
            )
    parts = chunks(features)
    for index, target in enumerate((k_ref, v_ref)):
        for number, part in enumerate(parts):
            copies[index * len(parts) + number].wait()
            picked = dot(hot_ref[...], target[:, part]).astype(BF)
            left_ref[index, :, part] = picked[:capacity]
            right_ref[index, :, part] = picked[capacity:]


def pick(send, k, v):
    rows, features = k.shape
    capacity = send.shape[1]
    slots = sds((2, capacity, features))
    return local(
        pick_kernel,
        "pick",
        2,
        [slots, slots, sds((2 * capacity, rows))],
        [pltpu.with_memory_space_constraint(x, pltpu.HBM) for x in (send, k, v)],
        scratch=(
            pltpu.VMEM((2, capacity), jnp.int32),
            pltpu.VMEM((rows, features), BF),
            pltpu.VMEM((rows, features), BF),
            pltpu.SemaphoreType.DMA((1 + 2 * len(chunks(features)),)),
        ),
        spaces=(pl.ANY, pl.ANY, pl.ANY),
    )


def prep_kernel(
    docs_ref, first_ref, take_ref, log_ref, named_ref, q_ref, k_ref, v_ref,
    left_ref, right_ref, qo_ref, ko_ref, vo_ref, hot_ref,
    mask_ref, cols_ref, rows_ref, through_ref, state_ref, leave_ref, own_ref,
):
    rows, features = q_ref.shape
    heads = log_ref.shape[0]
    capacity = hot_ref.shape[1] // 2
    for part in chunks(features):
        picked = dot(named_ref[...], q_ref[:, part]).astype(BF)
        left_ref[0, :, part] = picked[:capacity]
        right_ref[0, :, part] = picked[capacity:]

    first = first_ref[0]
    position = first + iota((rows, 1), 0)
    position_row = first + iota((1, rows), 1)
    segment = jnp.zeros((rows, 1), jnp.int32)
    segment_row = jnp.zeros((1, rows), jnp.int32)
    segment_first = jnp.int32(0)
    segment_last = jnp.int32(0)
    opens_first = jnp.int32(0)
    opens = jnp.int32(0)
    start = jnp.int32(0)
    for n in range(docs_ref.shape[0]):
        segment += (position >= start).astype(jnp.int32)
        segment_row += (position_row >= start).astype(jnp.int32)
        segment_first += (first >= start).astype(jnp.int32)
        segment_last += (first + rows - 1 >= start).astype(jnp.int32)
        opens_first += (first == start).astype(jnp.int32)
        opens += ((start >= first) & (start < first + rows)).astype(jnp.int32)
        start += docs_ref[n]
    below = iota((rows, rows), 0) >= iota((rows, rows), 1)
    scale = -0.5 * math.log2(features // heads)
    mask_ref[...] = jnp.where((segment == segment_row) & below, scale, MASKED)
    triangle = one_hot(below)
    logs = jnp.concatenate([log_ref[...], jnp.zeros((128 - heads, rows), F32)], axis=0).T
    high, middle, low = pieces(logs)
    running = (dot(triangle, high) + (dot(triangle, middle) + dot(triangle, low))) * LOG2E
    rows_ref[...] = running.T[:heads]
    final = running[rows - 1 : rows, :]
    keep_f = segment == segment_last
    keep_e = (segment == segment_first) & (opens_first == 0)
    leaving = jnp.where(keep_f, jnp.exp2(final - running), 0.0)
    entering = jnp.where(keep_e, jnp.exp2(running + scale), 0.0)
    through = jnp.where(opens == 0, jnp.exp2(final), 0.0)
    cols_ref[0], cols_ref[1], cols_ref[2] = leaving, entering, running
    parts = [x.astype(F32) for x in pieces(through)]
    line = iota((16, 128), 0)
    for h in range(heads):
        high, middle, low = [jnp.broadcast_to(x[:, h : h + 1], (16, 128)) for x in parts]
        through_ref[h] = jnp.where(
            line == 0, high, jnp.where(line == 1, middle, jnp.where(line == 2, low, 0.0))
        ).astype(BF)

    lane = iota((rows, 128), 1)
    taken = along_rows(take_ref[...])
    for start_row in range(0, rows, 128):
        own_ref[:, start_row : start_row + 128] = one_hot(taken - capacity == lane + start_row)
    hot_ref[:, :capacity] = one_hot(taken == lane)
    hot_ref[:, capacity:] = one_hot(taken - (capacity + rows) == lane)
    leave_ref[...] = sum(dot_tn(hot_ref[...], piece) for piece in pieces(leaving))
    for part in chunks(features):
        for source, target in ((k_ref, ko_ref), (v_ref, vo_ref), (q_ref, qo_ref)):
            target[:, part] = dot(own_ref[...], source[:, part]).astype(BF)
    for h, part in enumerate(head_slices(features, heads)):
        kf = (ko_ref[:, part].astype(F32) * cols_ref[0, :, h : h + 1]).astype(BF)
        state_ref[h] = dot_tn(kf, vo_ref[:, part])


def prep(docs, first, take, log_decay, named, q, k, v):
    rows, features = q.shape
    heads = log_decay.shape[0]
    width = features // heads
    capacity = named.shape[0] // 2
    slots, own_rows = sds((1, capacity, features)), sds((rows, features))
    return local(
        prep_kernel,
        "prep",
        30,
        [
            slots, slots, own_rows, own_rows, own_rows,
            sds((rows, 2 * capacity)),
            sds((rows, rows), F32),
            sds((3, rows, 128), F32),
            sds((heads, rows), F32),
            sds((heads, 16, 128)),
            sds((heads, width, width), F32),
            sds((2 * capacity, 128), F32),
        ],
        (docs, first, take, log_decay, named, q, k, v),
        scalars=2,
        scratch=(pltpu.VMEM((rows, rows), BF),),
    )


def state_kernel(left_ref, right_ref, leave_ref, own_ref, through_ref, message_ref):
    heads, width = own_ref.shape[:2]
    for h, part in enumerate(head_slices(heads * width, heads)):
        k = jnp.concatenate([left_ref[0, :, part], right_ref[0, :, part]], axis=0)
        v = jnp.concatenate([left_ref[1, :, part], right_ref[1, :, part]], axis=0)
        kf = (k.astype(F32) * leave_ref[:, h : h + 1]).astype(BF)
        message_ref[h, :width, :] = (own_ref[h] + dot_tn(kf, v)).astype(BF)
        message_ref[h, width:, :] = through_ref[h]


def assemble(hot_ref, left_ref, right_ref, index, own_rows, target):
    for part in chunks(target.shape[1]):
        extra = jnp.concatenate([left_ref[index, :, part], right_ref[index, :, part]], axis=0)
        target[:, part] = own_rows[:, part] + dot(hot_ref[...], extra).astype(BF)


def assemble_kernel(hot_ref, left_ref, right_ref, ko_ref, vo_ref, _, k_ref, v_ref):
    assemble(hot_ref, left_ref, right_ref, 0, ko_ref, k_ref)
    assemble(hot_ref, left_ref, right_ref, 1, vo_ref, v_ref)


def decay(mask_ref, cols_ref, rows_ref, h, top, half, reach):
    column = cols_ref[2, top : top + half, h : h + 1]
    row = rows_ref[h : h + 1, :reach]
    return jnp.exp2((column - row) + mask_ref[top : top + half, :reach])


def inside_kernel(hot_ref, left_ref, right_ref, qo_ref, k_ref, v_ref, mask_ref, cols_ref, rows_ref, q_ref, p_ref, o_ref):
    rows, features = k_ref.shape
    assemble(hot_ref, left_ref, right_ref, 0, qo_ref, q_ref)
    heads, half = p_ref.shape[0], rows // 2
    for h, part in enumerate(head_slices(features, heads)):
        for i in range(2):
            top, reach = i * half, (i + 1) * half
            here = slice(top, top + half)
            scores = dot_nt(q_ref[here, part], k_ref[:reach, part])
            weight = decay(mask_ref, cols_ref, rows_ref, h, top, half, reach)
            p = (scores * weight).astype(BF)
            p_ref[h, here, :reach] = p
            o_ref[here, part] = dot(p, v_ref[:reach, part])


def joined(near_ref, far_ref, h, width):
    through = jnp.sum(near_ref[h, width:, :].astype(F32), axis=0, keepdims=True)
    near = near_ref[h, :width, :].astype(F32)
    return (near + through * far_ref[h, :width, :].astype(F32)).astype(BF)


def output_kernel(scale_ref, o_ref, q_ref, near_ref, far_ref, cols_ref, ct_ref, u_ref, h_ref, sums_ref):
    rows, features = q_ref.shape
    heads, width = h_ref.shape[:2]
    squares = jnp.zeros((rows, width), F32)
    cross = jnp.zeros((rows, width), F32)
    for h, part in enumerate(head_slices(features, heads)):
        carried_in = joined(near_ref, far_ref, h, width)
        h_ref[h] = carried_in
        outer = dot(q_ref[:, part], carried_in) * cols_ref[1, :, h : h + 1]
        u = (o_ref[:, part] + outer) * scale_ref[h]
        u_ref[:, part] = u
        squares += u * u
        cross += ct_ref[:, part].astype(F32) * u
    sums_ref[0:1, :] = jnp.sum(squares.T, axis=0, keepdims=True)
    sums_ref[1:2, :] = jnp.sum(cross.T, axis=0, keepdims=True)


def norm_kernel(total, scale_ref, u_ref, ct_ref, q_ref, cols_ref, through_ref, *refs):
    *sums, g_ref, message_ref, inverse_ref = refs
    rows, features = q_ref.shape
    heads = through_ref.shape[0]
    width = features // heads
    summed = sums[0][...]
    for more in sums[1:]:
        summed += more[...]
    inverse = lax.rsqrt(along_rows(summed[0:1, :], width) / total + EPSILON)
    mean = inverse * inverse * inverse * (along_rows(summed[1:2, :], width) / total)
    inverse_ref[...] = inverse
    for h, part in enumerate(head_slices(features, heads)):
        g = (inverse * ct_ref[:, part].astype(F32) - u_ref[:, part] * mean) * scale_ref[h]
        g = g.astype(BF)
        g_ref[:, part] = g
        qe = (q_ref[:, part].astype(F32) * cols_ref[1, :, h : h + 1]).astype(BF)
        message_ref[h, :width, :] = dot_tn(qe, g).astype(BF)
        message_ref[h, width:, :] = through_ref[h]


def normed_kernel(u_ref, inverse_ref, _, normed_ref):
    rows, features = u_ref.shape
    width = inverse_ref.shape[1]
    for part in head_slices(features, features // width):
        normed_ref[:, part] = (u_ref[:, part] * inverse_ref[...]).astype(BF)


def send_back(hot, source, left_ref, right_ref, index):
    capacity = left_ref.shape[1]
    for part in chunks(source.shape[1]):
        back = dot(hot, source[:, part]).astype(BF)
        left_ref[index, :, part] = back[:capacity]
        right_ref[index, :, part] = back[capacity:]


def slots_hot(take_ref, capacity):
    rows = take_ref.shape[1]
    taken = jnp.broadcast_to(take_ref[...], (capacity, rows))
    slot = iota((capacity, rows), 0)
    return jnp.concatenate(
        [one_hot(taken == slot), one_hot(taken - (capacity + rows) == slot)], axis=0
    )


def grad_q_kernel(take_ref, g_ref, k_ref, v_ref, h_ref, mask_ref, cols_ref, rows_ref, dq_ref, z_ref, left_ref, right_ref):
    rows, features = k_ref.shape
    heads, half = h_ref.shape[0], rows // 2
    for h, part in enumerate(head_slices(features, heads)):
        for i in range(2):
            top, reach = i * half, (i + 1) * half
            here = slice(top, top + half)
            g = g_ref[here, part]
            weight = decay(mask_ref, cols_ref, rows_ref, h, top, half, reach)
            z = (dot_nt(g, v_ref[:reach, part]) * weight).astype(BF)
            z_ref[h, here, :reach] = z
            outer = dot_nt(g, h_ref[h]) * cols_ref[1, here, h : h + 1]
            dq_ref[here, part] = (dot(z, k_ref[:reach, part]) + outer).astype(BF)
    send_back(slots_hot(take_ref, left_ref.shape[1]), dq_ref, left_ref, right_ref, 0)


def inner_kernel(z_ref, p_ref, q_ref, g_ref, dk_ref, dv_ref):
    rows, features = q_ref.shape
    heads, half = z_ref.shape[0], rows // 2
    for h, part in enumerate(head_slices(features, heads)):
        for square, source, target in ((z_ref, q_ref, dk_ref), (p_ref, g_ref, dv_ref)):
            for j in range(2):
                here = slice(j * half, (j + 1) * half)
                target[here, part] = dot_tn(square[h, j * half :, here], source[j * half :, part])


def grad_kv_kernel(take_ref, near_ref, far_ref, k_ref, v_ref, cols_ref, dki_ref, dvi_ref, dk_ref, dv_ref, left_ref, right_ref):
    rows, features = k_ref.shape
    heads = near_ref.shape[0]
    for h, part in enumerate(head_slices(features, heads)):
        state_grad = joined(near_ref, far_ref, h, features // heads)
        leaving = cols_ref[0, :, h : h + 1]
        dk_ref[:, part] = (dki_ref[:, part] + leaving * dot_nt(v_ref[:, part], state_grad)).astype(BF)
        dv_ref[:, part] = (dvi_ref[:, part] + leaving * dot(k_ref[:, part], state_grad)).astype(BF)
    hot = slots_hot(take_ref, left_ref.shape[1])
    send_back(hot, dk_ref, left_ref, right_ref, 0)
    send_back(hot, dv_ref, left_ref, right_ref, 1)


def own_kernel(capacity, count, take_ref, *refs):
    rows = refs[0].shape[0]
    taken = jnp.broadcast_to(take_ref[...], (rows, rows))
    hot = one_hot(taken - capacity == iota((rows, rows), 0))
    for source, target in zip(refs[:count], refs[-count:]):
        for part in chunks(source.shape[1]):
            target[:, part] = dot(hot, source[:, part]).astype(BF)


def finish_kernel(count, send_ref, left_ref, right_ref, *refs):
    rows = refs[0].shape[0]
    capacity = send_ref.shape[1]
    line = iota((rows, capacity), 0)
    hot = jnp.concatenate(
        [
            one_hot(jnp.broadcast_to(send_ref[side : side + 1, :], (rows, capacity)) == line)
            for side in range(2)
        ],
        axis=1,
    )
    for index, (source, target) in enumerate(zip(refs[:count], refs[count : 2 * count])):
        for part in chunks(source.shape[1]):
            back = jnp.concatenate([left_ref[index, :, part], right_ref[index, :, part]], axis=0)
            target[:, part] = source[:, part] + dot(hot, back).astype(BF)
    for order in refs[2 * count :]:
        order[...] = jnp.zeros_like(order)


def shifted(array, by):
    peers = lax.axis_size("seq")
    return lax.ppermute(array, "seq", [(i, i + by) for i in range(peers) if 0 <= i + by < peers])


def turned_by(array, by):
    peers = lax.axis_size("head")
    return lax.ppermute(array, "head", [(i, (i + by) % peers) for i in range(peers)])


def carried(message, direction):
    reach = lax.axis_size("seq") // 4
    if reach <= 2:
        return shifted(message, direction), shifted(message, 2 * direction)
    size = message.shape[2]
    own_state = message[:, :size].astype(F32)
    through = jnp.sum(message[:, size:, :1].astype(F32), axis=1, keepdims=True)

    def relay(_, state_here):
        return shifted((through * state_here + own_state).astype(BF), direction).astype(F32)

    incoming = lax.fori_loop(0, reach, relay, jnp.zeros_like(own_state)).astype(BF)
    near = jnp.concatenate([incoming, jnp.zeros_like(message[:, size:])], axis=1)
    return near, jnp.zeros_like(message)


def on_device(
    queries, key_vectors, value_vectors, log_decay, head_scale,
    send_rows, take_rows, doc_lengths, cotangent,
):
    rows, features = queries.shape
    heads = head_scale.shape[0]
    width = features // heads
    capacity = send_rows.shape[2]
    send = send_rows.reshape(2, capacity)
    take = take_rows.reshape(1, rows)
    first = (lax.axis_index("seq") * rows).astype(jnp.int32).reshape(1)
    total = features * lax.axis_size("head")
    full, full32 = sds((rows, features)), sds((rows, features), F32)
    squares = sds((heads, rows, rows))
    message_shape = sds((heads, width + 16, width))
    one_side, two_sides = sds((1, capacity, features)), sds((2, capacity, features))

    kv_left, kv_right, named = pick(send, key_vectors, value_vectors)
    kv_before, kv_after = shifted(kv_right, 1), shifted(kv_left, -1)
    (
        q_left, q_right, q_own, k_own, v_own, hot, mask, cols, turned, through, state_own, leave
    ) = prep(doc_lengths, first, take, log_decay.T, named, queries, key_vectors, value_vectors)
    q_before, q_after = shifted(q_right, 1), shifted(q_left, -1)
    (message,) = local(
        state_kernel, "state", 30, [message_shape], (kv_before, kv_after, leave, state_own, through)
    )
    near, far = carried(message, 1)
    k, v = local(
        assemble_kernel,
        "assemble",
        5,
        [full, full],
        (hot, kv_before, kv_after, k_own, v_own, message),
    )
    q, probs, o_inside = local(
        inside_kernel,
        "inside",
        30,
        [full, squares, full32],
        (hot, q_before, q_after, q_own, k, v, mask, cols, turned),
    )
    u, state_low, sums = local(
        output_kernel,
        "output",
        3,
        [full32, sds((heads, width, width)), sds((2, rows), F32)],
        (head_scale, o_inside, q, near, far, cols, cotangent),
        scalars=1,
    )
    others = [turned_by(sums, by) for by in range(1, lax.axis_size("head"))]
    g, grad_message, inverse = local(
        functools.partial(norm_kernel, total),
        "norm",
        4,
        [full, message_shape, sds((rows, width), F32)],
        (head_scale, u, cotangent, q, cols, through, sums, *others),
        scalars=1,
    )
    grad_near, grad_far = carried(grad_message, -1)
    dq, z, dq_left, dq_right = local(
        grad_q_kernel,
        "grad_q",
        30,
        [full, squares, one_side, one_side],
        (take, g, k, v, state_low, mask, cols, turned),
    )
    dq_before, dq_after = shifted(dq_right, 1), shifted(dq_left, -1)
    dk_inner, dv_inner = local(inner_kernel, "inner", 5, [full32, full32], (z, probs, q, g))
    dk, dv, dkv_left, dkv_right = local(
        grad_kv_kernel,
        "grad_kv",
        30,
        [full, full, two_sides, two_sides],
        (take, grad_near, grad_far, k, v, cols, dk_inner, dv_inner),
    )
    dkv_before, dkv_after = shifted(dkv_right, 1), shifted(dkv_left, -1)
    (normed,) = local(normed_kernel, "normed", 2, [full], (u, inverse, dk))
    (dq_own,) = local(
        functools.partial(own_kernel, capacity, 1), "own_q", 2, [full], (take, dq, dk)
    )
    grad_queries, order = local(
        functools.partial(finish_kernel, 1),
        "finish_q",
        2,
        [full, sds((16, 128))],
        (send, dq_before, dq_after, dq_own),
    )
    dk_own, dv_own = local(
        functools.partial(own_kernel, capacity, 2), "own_kv", 2, [full, full],
        (take, dk, dv, order),
    )
    grad_keys, grad_values = local(
        functools.partial(finish_kernel, 2),
        "finish_kv",
        2,
        [full, full],
        (send, dkv_before, dkv_after, dk_own, dv_own),
    )
    return normed, grad_queries, grad_keys, grad_values


def solution(mesh):
    both = P("seq", "head")
    in_specs = (both, both, both, both, P("head"), P("seq", None, None), P("seq"), P(), both)
    return jax.shard_map(
        on_device, mesh=mesh, in_specs=in_specs, out_specs=(both,) * 4, check_vma=False
    )
```

```python
import functools
import math

import jax
import jax.numpy as jnp
from jax import lax
from jax.experimental import pallas as pl
from jax.experimental.pallas import tpu as pltpu
from jax.sharding import PartitionSpec as P

EPSILON = 1e-05
LOG2E = math.log2(math.e)
MASKED = -1e30
MIB = 1024 * 1024
BF = jnp.bfloat16
F32 = jnp.float32
NT = (((1,), (1,)), ((), ()))
TN = (((0,), (0,)), ((), ()))
CHUNK = 256


def dot(a, b):
    return jnp.dot(a, b, preferred_element_type=F32)


def dot_nt(a, b):
    return lax.dot_general(a, b, NT, preferred_element_type=F32)


def dot_tn(a, b):
    return lax.dot_general(a, b, TN, preferred_element_type=F32)


def along_rows(row, lanes=128):
    return jnp.broadcast_to(row, (lanes, row.shape[1])).T


def iota(shape, dim):
    return lax.broadcasted_iota(jnp.int32, shape, dim)


def one_hot(hit):
    return jnp.where(hit, 1.0, 0.0).astype(BF)


def pieces(x):
    high = x.astype(BF)
    rest = x - high.astype(F32)
    middle = rest.astype(BF)
    return high, middle, (rest - middle.astype(F32)).astype(BF)


def chunks(features):
    return [slice(start, start + CHUNK) for start in range(0, features, CHUNK)]


def head_slices(features, heads):
    width = features // heads
    return [slice(h * width, (h + 1) * width) for h in range(heads)]


def local(kernel, name, us, out_shape, operands, scalars=0, scratch=(), spaces=None):
    vmem = pl.BlockSpec(memory_space=pltpu.VMEM)
    smem = pl.BlockSpec(memory_space=pltpu.SMEM)
    specs = [smem] * scalars + [vmem] * (len(operands) - scalars)
    if spaces is not None:
        specs = [pl.BlockSpec(memory_space=space) for space in spaces]
    return pl.pallas_call(
        kernel,
        in_specs=specs,
        out_specs=[vmem] * len(out_shape),
        out_shape=out_shape,
        scratch_shapes=list(scratch),
        compiler_params=pltpu.CompilerParams(vmem_limit_bytes=16 * MIB),
        cost_estimate=pl.CostEstimate(
            flops=int(us * 1.1e9), bytes_accessed=1_000_000, transcendentals=0
        ),
        name=name,
    )(*operands)


def sds(shape, dtype=BF):
    return jax.ShapeDtypeStruct(shape, dtype)


def pick_kernel(send_hbm, k_hbm, v_hbm, left_ref, right_ref, hot_ref, send_ref, k_ref, v_ref, sem):
    rows, features = k_ref.shape
    capacity = send_ref.shape[1]
    named_copy = pltpu.make_async_copy(send_hbm, send_ref, sem.at[0])
    named_copy.start()
    copies = []
    for source, target in ((k_hbm, k_ref), (v_hbm, v_ref)):
        for part in chunks(features):
            copy = pltpu.make_async_copy(
                source.at[:, part], target.at[:, part], sem.at[1 + len(copies)]
            )
            copy.start()
            copies.append(copy)
    named_copy.wait()
    lane = iota((capacity, 128), 1)
    for side in range(2):
        named = along_rows(send_ref[side : side + 1, :])
        for start in range(0, rows, 128):
            hot_ref[side * capacity : (side + 1) * capacity, start : start + 128] = one_hot(
                named == lane + start
            )
    parts = chunks(features)
    for index, target in enumerate((k_ref, v_ref)):
        for number, part in enumerate(parts):
            copies[index * len(parts) + number].wait()
            picked = dot(hot_ref[...], target[:, part]).astype(BF)
            left_ref[index, :, part] = picked[:capacity]
            right_ref[index, :, part] = picked[capacity:]


def pick(send, k, v):
    rows, features = k.shape
    capacity = send.shape[1]
    slots = sds((2, capacity, features))
    return local(
        pick_kernel,
        "pick",
        2,
        [slots, slots, sds((2 * capacity, rows))],
        [pltpu.with_memory_space_constraint(x, pltpu.HBM) for x in (send, k, v)],
        scratch=(
            pltpu.VMEM((2, capacity), jnp.int32),
            pltpu.VMEM((rows, features), BF),
            pltpu.VMEM((rows, features), BF),
            pltpu.SemaphoreType.DMA((1 + 2 * len(chunks(features)),)),
        ),
        spaces=(pl.ANY, pl.ANY, pl.ANY),
    )


def prep_kernel(
    docs_ref, take_ref, log_ref, named_ref, q_ref, k_ref, v_ref,
    left_ref, right_ref, qo_ref, ko_ref, vo_ref, hot_ref,
    mask_ref, cols_ref, rows_ref, through_ref, state_ref, leave_ref, own_ref,
):
    rows, features = q_ref.shape
    heads = log_ref.shape[0]
    capacity = hot_ref.shape[1] // 2
    for part in chunks(features):
        picked = dot(named_ref[...], q_ref[:, part]).astype(BF)
        left_ref[0, :, part] = picked[:capacity]
        right_ref[0, :, part] = picked[capacity:]

    first = (lax.axis_index("seq") * rows).astype(jnp.int32)
    position = first + iota((rows, 1), 0)
    position_row = first + iota((1, rows), 1)
    segment = jnp.zeros((rows, 1), jnp.int32)
    segment_row = jnp.zeros((1, rows), jnp.int32)
    segment_first = jnp.int32(0)
    segment_last = jnp.int32(0)
    opens_first = jnp.int32(0)
    opens = jnp.int32(0)
    start = jnp.int32(0)
    for n in range(docs_ref.shape[0]):
        segment += (position >= start).astype(jnp.int32)
        segment_row += (position_row >= start).astype(jnp.int32)
        segment_first += (first >= start).astype(jnp.int32)
        segment_last += (first + rows - 1 >= start).astype(jnp.int32)
        opens_first += (first == start).astype(jnp.int32)
        opens += ((start >= first) & (start < first + rows)).astype(jnp.int32)
        start += docs_ref[n]
    below = iota((rows, rows), 0) >= iota((rows, rows), 1)
    scale = -0.5 * math.log2(features // heads)
    mask_ref[...] = jnp.where((segment == segment_row) & below, scale, MASKED)
    triangle = one_hot(below)
    logs = jnp.concatenate([log_ref[...], jnp.zeros((128 - heads, rows), F32)], axis=0).T
    high, middle, low = pieces(logs)
    running = (dot(triangle, high) + (dot(triangle, middle) + dot(triangle, low))) * LOG2E
    rows_ref[...] = running.T[:heads]
    final = running[rows - 1 : rows, :]
    keep_f = segment == segment_last
    keep_e = (segment == segment_first) & (opens_first == 0)
    leaving = jnp.where(keep_f, jnp.exp2(final - running), 0.0)
    entering = jnp.where(keep_e, jnp.exp2(running + scale), 0.0)
    through = jnp.where(opens == 0, jnp.exp2(final), 0.0)
    cols_ref[0], cols_ref[1], cols_ref[2] = leaving, entering, running
    parts = [x.astype(F32) for x in pieces(through)]
    line = iota((16, 128), 0)
    for h in range(heads):
        high, middle, low = [jnp.broadcast_to(x[:, h : h + 1], (16, 128)) for x in parts]
        through_ref[h] = jnp.where(
            line == 0, high, jnp.where(line == 1, middle, jnp.where(line == 2, low, 0.0))
        ).astype(BF)

    lane = iota((rows, 128), 1)
    taken = along_rows(take_ref[...])
    for start_row in range(0, rows, 128):
        own_ref[:, start_row : start_row + 128] = one_hot(taken - capacity == lane + start_row)
    hot_ref[:, :capacity] = one_hot(taken == lane)
    hot_ref[:, capacity:] = one_hot(taken - (capacity + rows) == lane)
    leave_ref[...] = sum(dot_tn(hot_ref[...], piece) for piece in pieces(leaving))
    for part in chunks(features):
        for source, target in ((k_ref, ko_ref), (v_ref, vo_ref), (q_ref, qo_ref)):
            target[:, part] = dot(own_ref[...], source[:, part]).astype(BF)
    for h, part in enumerate(head_slices(features, heads)):
        kf = (ko_ref[:, part].astype(F32) * cols_ref[0, :, h : h + 1]).astype(BF)
        state_ref[h] = dot_tn(kf, vo_ref[:, part])


def prep(docs, take, log_decay, named, q, k, v):
    rows, features = q.shape
    heads = log_decay.shape[0]
    width = features // heads
    capacity = named.shape[0] // 2
    slots, own_rows = sds((1, capacity, features)), sds((rows, features))
    return local(
        prep_kernel,
        "prep",
        30,
        [
            slots, slots, own_rows, own_rows, own_rows,
            sds((rows, 2 * capacity)),
            sds((rows, rows), F32),
            sds((3, rows, 128), F32),
            sds((heads, rows), F32),
            sds((heads, 16, 128)),
            sds((heads, width, width), F32),
            sds((2 * capacity, 128), F32),
        ],
        (docs, take, log_decay, named, q, k, v),
        scalars=1,
        scratch=(pltpu.VMEM((rows, rows), BF),),
    )


def state_kernel(left_ref, right_ref, leave_ref, own_ref, through_ref, message_ref):
    heads, width = own_ref.shape[:2]
    for h, part in enumerate(head_slices(heads * width, heads)):
        k = jnp.concatenate([left_ref[0, :, part], right_ref[0, :, part]], axis=0)
        v = jnp.concatenate([left_ref[1, :, part], right_ref[1, :, part]], axis=0)
        kf = (k.astype(F32) * leave_ref[:, h : h + 1]).astype(BF)
        message_ref[h, :width, :] = (own_ref[h] + dot_tn(kf, v)).astype(BF)
        message_ref[h, width:, :] = through_ref[h]


def assemble(hot_ref, left_ref, right_ref, index, own_rows, target):
    for part in chunks(target.shape[1]):
        extra = jnp.concatenate([left_ref[index, :, part], right_ref[index, :, part]], axis=0)
        target[:, part] = own_rows[:, part] + dot(hot_ref[...], extra).astype(BF)


def assemble_kernel(hot_ref, left_ref, right_ref, ko_ref, vo_ref, _, k_ref, v_ref):
    assemble(hot_ref, left_ref, right_ref, 0, ko_ref, k_ref)
    assemble(hot_ref, left_ref, right_ref, 1, vo_ref, v_ref)


def decay(mask_ref, cols_ref, rows_ref, h, top, half, reach):
    column = cols_ref[2, top : top + half, h : h + 1]
    row = rows_ref[h : h + 1, :reach]
    return jnp.exp2((column - row) + mask_ref[top : top + half, :reach])


def inside_kernel(hot_ref, left_ref, right_ref, qo_ref, k_ref, v_ref, mask_ref, cols_ref, rows_ref, q_ref, p_ref, o_ref):
    rows, features = k_ref.shape
    assemble(hot_ref, left_ref, right_ref, 0, qo_ref, q_ref)
    heads, half = p_ref.shape[0], rows // 2
    for h, part in enumerate(head_slices(features, heads)):
        for i in range(2):
            top, reach = i * half, (i + 1) * half
            here = slice(top, top + half)
            scores = dot_nt(q_ref[here, part], k_ref[:reach, part])
            weight = decay(mask_ref, cols_ref, rows_ref, h, top, half, reach)
            p = (scores * weight).astype(BF)
            p_ref[h, here, :reach] = p
            o_ref[here, part] = dot(p, v_ref[:reach, part])


def shards_before(direction):
    index = lax.axis_index("seq")
    return index if direction > 0 else lax.axis_size("seq") - 1 - index


def joined(before, near_ref, far_ref, h, width):
    through = jnp.sum(near_ref[h, width:, :].astype(F32), axis=0, keepdims=True)
    near = near_ref[h, :width, :].astype(F32)
    far = through * far_ref[h, :width, :].astype(F32)
    near = jnp.where(before >= 1, near, 0.0)
    return (near + jnp.where(before >= 2, far, 0.0)).astype(BF)


def output_kernel(scale_ref, o_ref, q_ref, near_ref, far_ref, cols_ref, ct_ref, u_ref, h_ref, sums_ref):
    rows, features = q_ref.shape
    heads, width = h_ref.shape[:2]
    before = shards_before(1)
    squares = jnp.zeros((rows, width), F32)
    cross = jnp.zeros((rows, width), F32)
    for h, part in enumerate(head_slices(features, heads)):
        carried_in = joined(before, near_ref, far_ref, h, width)
        h_ref[h] = carried_in
        outer = dot(q_ref[:, part], carried_in) * cols_ref[1, :, h : h + 1]
        u = (o_ref[:, part] + outer) * scale_ref[h]
        u_ref[:, part] = u
        squares += u * u
        cross += ct_ref[:, part].astype(F32) * u
    sums_ref[0:1, :] = jnp.sum(squares.T, axis=0, keepdims=True)
    sums_ref[1:2, :] = jnp.sum(cross.T, axis=0, keepdims=True)


def norm_kernel(total, scale_ref, u_ref, ct_ref, q_ref, cols_ref, through_ref, *refs):
    *sums, g_ref, message_ref, inverse_ref = refs
    rows, features = q_ref.shape
    heads = through_ref.shape[0]
    width = features // heads
    summed = sums[0][...]
    for more in sums[1:]:
        summed += more[...]
    inverse = lax.rsqrt(along_rows(summed[0:1, :], width) / total + EPSILON)
    mean = inverse * inverse * inverse * (along_rows(summed[1:2, :], width) / total)
    inverse_ref[...] = inverse
    for h, part in enumerate(head_slices(features, heads)):
        g = (inverse * ct_ref[:, part].astype(F32) - u_ref[:, part] * mean) * scale_ref[h]
        g = g.astype(BF)
        g_ref[:, part] = g
        qe = (q_ref[:, part].astype(F32) * cols_ref[1, :, h : h + 1]).astype(BF)
        message_ref[h, :width, :] = dot_tn(qe, g).astype(BF)
        message_ref[h, width:, :] = through_ref[h]


def normed_kernel(u_ref, inverse_ref, _, normed_ref):
    rows, features = u_ref.shape
    width = inverse_ref.shape[1]
    for part in head_slices(features, features // width):
        normed_ref[:, part] = (u_ref[:, part] * inverse_ref[...]).astype(BF)


def send_back(hot, source, left_ref, right_ref, index):
    capacity = left_ref.shape[1]
    for part in chunks(source.shape[1]):
        back = dot(hot, source[:, part]).astype(BF)
        left_ref[index, :, part] = back[:capacity]
        right_ref[index, :, part] = back[capacity:]


def slots_hot(take_ref, capacity):
    rows = take_ref.shape[1]
    taken = jnp.broadcast_to(take_ref[...], (capacity, rows))
    slot = iota((capacity, rows), 0)
    return jnp.concatenate(
        [one_hot(taken == slot), one_hot(taken - (capacity + rows) == slot)], axis=0
    )


def grad_q_kernel(take_ref, g_ref, k_ref, v_ref, h_ref, mask_ref, cols_ref, rows_ref, dq_ref, z_ref, left_ref, right_ref):
    rows, features = k_ref.shape
    heads, half = h_ref.shape[0], rows // 2
    for h, part in enumerate(head_slices(features, heads)):
        for i in range(2):
            top, reach = i * half, (i + 1) * half
            here = slice(top, top + half)
            g = g_ref[here, part]
            weight = decay(mask_ref, cols_ref, rows_ref, h, top, half, reach)
            z = (dot_nt(g, v_ref[:reach, part]) * weight).astype(BF)
            z_ref[h, here, :reach] = z
            outer = dot_nt(g, h_ref[h]) * cols_ref[1, here, h : h + 1]
            dq_ref[here, part] = (dot(z, k_ref[:reach, part]) + outer).astype(BF)
    send_back(slots_hot(take_ref, left_ref.shape[1]), dq_ref, left_ref, right_ref, 0)


def inner_kernel(z_ref, p_ref, q_ref, g_ref, dk_ref, dv_ref):
    rows, features = q_ref.shape
    heads, half = z_ref.shape[0], rows // 2
    for h, part in enumerate(head_slices(features, heads)):
        for square, source, target in ((z_ref, q_ref, dk_ref), (p_ref, g_ref, dv_ref)):
            for j in range(2):
                here = slice(j * half, (j + 1) * half)
                target[here, part] = dot_tn(square[h, j * half :, here], source[j * half :, part])


def grad_kv_kernel(take_ref, near_ref, far_ref, k_ref, v_ref, cols_ref, dki_ref, dvi_ref, dk_ref, dv_ref, left_ref, right_ref):
    rows, features = k_ref.shape
    heads = near_ref.shape[0]
    before = shards_before(-1)
    for h, part in enumerate(head_slices(features, heads)):
        state_grad = joined(before, near_ref, far_ref, h, features // heads)
        leaving = cols_ref[0, :, h : h + 1]
        dk_ref[:, part] = (dki_ref[:, part] + leaving * dot_nt(v_ref[:, part], state_grad)).astype(BF)
        dv_ref[:, part] = (dvi_ref[:, part] + leaving * dot(k_ref[:, part], state_grad)).astype(BF)
    hot = slots_hot(take_ref, left_ref.shape[1])
    send_back(hot, dk_ref, left_ref, right_ref, 0)
    send_back(hot, dv_ref, left_ref, right_ref, 1)


def own_kernel(capacity, count, take_ref, *refs):
    rows = refs[0].shape[0]
    taken = jnp.broadcast_to(take_ref[...], (rows, rows))
    hot = one_hot(taken - capacity == iota((rows, rows), 0))
    for source, target in zip(refs[:count], refs[-count:]):
        for part in chunks(source.shape[1]):
            target[:, part] = dot(hot, source[:, part]).astype(BF)


def finish_kernel(count, send_ref, left_ref, right_ref, *refs):
    rows = refs[0].shape[0]
    capacity = send_ref.shape[1]
    line = iota((rows, capacity), 0)
    hot = jnp.concatenate(
        [
            one_hot(jnp.broadcast_to(send_ref[side : side + 1, :], (rows, capacity)) == line)
            for side in range(2)
        ],
        axis=1,
    )
    for index, (source, target) in enumerate(zip(refs[:count], refs[count : 2 * count])):
        for part in chunks(source.shape[1]):
            back = jnp.concatenate([left_ref[index, :, part], right_ref[index, :, part]], axis=0)
            target[:, part] = source[:, part] + dot(hot, back).astype(BF)
    for order in refs[2 * count :]:
        order[...] = jnp.zeros_like(order)


def shifted(array, by):
    peers = lax.axis_size("seq")
    return lax.ppermute(array, "seq", [(i, (i + by) % peers) for i in range(peers)])


def shifted_open(array, by):
    peers = lax.axis_size("seq")
    return lax.ppermute(array, "seq", [(i, i + by) for i in range(peers) if 0 <= i + by < peers])


def turned_by(array, by):
    peers = lax.axis_size("head")
    return lax.ppermute(array, "head", [(i, (i + by) % peers) for i in range(peers)])


def carried(message, direction):
    peers = lax.axis_size("seq")
    reach = peers // 4
    if reach <= 2:
        return shifted(message, direction), shifted(message, 2 * direction)
    size = message.shape[2]
    own_state = message[:, :size].astype(F32)
    through = jnp.sum(message[:, size:, :1].astype(F32), axis=1, keepdims=True)

    def relay(_, state_here):
        return shifted_open((through * state_here + own_state).astype(BF), direction).astype(F32)

    incoming = lax.fori_loop(0, reach, relay, jnp.zeros_like(own_state)).astype(BF)
    near = jnp.concatenate([incoming, jnp.zeros_like(message[:, size:])], axis=1)
    return near, jnp.zeros_like(message)


def on_device(
    queries, key_vectors, value_vectors, log_decay, head_scale,
    send_rows, take_rows, doc_lengths, cotangent,
):
    rows, features = queries.shape
    heads = head_scale.shape[0]
    width = features // heads
    capacity = send_rows.shape[2]
    send = send_rows.reshape(2, capacity)
    take = take_rows.reshape(1, rows)
    total = features * lax.axis_size("head")
    full, full32 = sds((rows, features)), sds((rows, features), F32)
    squares = sds((heads, rows, rows))
    message_shape = sds((heads, width + 16, width))
    one_side, two_sides = sds((1, capacity, features)), sds((2, capacity, features))

    kv_left, kv_right, named = pick(send, key_vectors, value_vectors)
    kv_before, kv_after = shifted(kv_right, 1), shifted(kv_left, -1)
    (
        q_left, q_right, q_own, k_own, v_own, hot, mask, cols, turned, through, state_own, leave
    ) = prep(doc_lengths, take, log_decay.T, named, queries, key_vectors, value_vectors)
    q_before, q_after = shifted(q_right, 1), shifted(q_left, -1)
    (message,) = local(
        state_kernel, "state", 30, [message_shape], (kv_before, kv_after, leave, state_own, through)
    )
    near, far = carried(message, 1)
    k, v = local(
        assemble_kernel,
        "assemble",
        5,
        [full, full],
        (hot, kv_before, kv_after, k_own, v_own, message),
    )
    q, probs, o_inside = local(
        inside_kernel,
        "inside",
        30,
        [full, squares, full32],
        (hot, q_before, q_after, q_own, k, v, mask, cols, turned),
    )
    u, state_low, sums = local(
        output_kernel,
        "output",
        3,
        [full32, sds((heads, width, width)), sds((2, rows), F32)],
        (head_scale, o_inside, q, near, far, cols, cotangent),
        scalars=1,
    )
    others = [turned_by(sums, by) for by in range(1, lax.axis_size("head"))]
    g, grad_message, inverse = local(
        functools.partial(norm_kernel, total),
        "norm",
        4,
        [full, message_shape, sds((rows, width), F32)],
        (head_scale, u, cotangent, q, cols, through, sums, *others),
        scalars=1,
    )
    grad_near, grad_far = carried(grad_message, -1)
    dq, z, dq_left, dq_right = local(
        grad_q_kernel,
        "grad_q",
        30,
        [full, squares, one_side, one_side],
        (take, g, k, v, state_low, mask, cols, turned),
    )
    dq_before, dq_after = shifted(dq_right, 1), shifted(dq_left, -1)
    dk_inner, dv_inner = local(inner_kernel, "inner", 5, [full32, full32], (z, probs, q, g))
    dk, dv, dkv_left, dkv_right = local(
        grad_kv_kernel,
        "grad_kv",
        30,
        [full, full, two_sides, two_sides],
        (take, grad_near, grad_far, k, v, cols, dk_inner, dv_inner),
    )
    dkv_before, dkv_after = shifted(dkv_right, 1), shifted(dkv_left, -1)
    (normed,) = local(normed_kernel, "normed", 2, [full], (u, inverse, dk))
    (dq_own,) = local(
        functools.partial(own_kernel, capacity, 1), "own_q", 2, [full], (take, dq, dk)
    )
    grad_queries, order = local(
        functools.partial(finish_kernel, 1),
        "finish_q",
        2,
        [full, sds((16, 128))],
        (send, dq_before, dq_after, dq_own),
    )
    dk_own, dv_own = local(
        functools.partial(own_kernel, capacity, 2), "own_kv", 2, [full, full],
        (take, dk, dv, order),
    )
    grad_keys, grad_values = local(
        functools.partial(finish_kernel, 2),
        "finish_kv",
        2,
        [full, full],
        (send, dkv_before, dkv_after, dk_own, dv_own),
    )
    return normed, grad_queries, grad_keys, grad_values


def solution(mesh):
    both = P("seq", "head")
    in_specs = (both, both, both, both, P("head"), P("seq", None, None), P("seq"), P(), both)
    return jax.shard_map(
        on_device, mesh=mesh, in_specs=in_specs, out_specs=(both,) * 4, check_vma=False
    )
```

```python
import functools
import math

import jax
import jax.numpy as jnp
from jax import lax
from jax.experimental import pallas as pl
from jax.experimental.pallas import tpu as pltpu
from jax.sharding import PartitionSpec as P

EPSILON = 1e-05
LOG2E = math.log2(math.e)
MASKED = -1e30
MIB = 1024 * 1024
BF = jnp.bfloat16
F32 = jnp.float32
NT = (((1,), (1,)), ((), ()))
TN = (((0,), (0,)), ((), ()))
CHUNK = 256


def dot(a, b):
    return jnp.dot(a, b, preferred_element_type=F32)


def dot_nt(a, b):
    return lax.dot_general(a, b, NT, preferred_element_type=F32)


def dot_tn(a, b):
    return lax.dot_general(a, b, TN, preferred_element_type=F32)


def along_rows(row, lanes=128):
    return jnp.broadcast_to(row, (lanes, row.shape[1])).T


def iota(shape, dim):
    return lax.broadcasted_iota(jnp.int32, shape, dim)


def one_hot(hit):
    return jnp.where(hit, 1.0, 0.0).astype(BF)


def pieces(x):
    high = x.astype(BF)
    rest = x - high.astype(F32)
    middle = rest.astype(BF)
    return high, middle, (rest - middle.astype(F32)).astype(BF)


def chunks(features):
    return [slice(start, start + CHUNK) for start in range(0, features, CHUNK)]


def head_slices(features, heads):
    width = features // heads
    return [slice(h * width, (h + 1) * width) for h in range(heads)]


def local(kernel, name, us, out_shape, operands, scalars=0, scratch=(), spaces=None):
    vmem = pl.BlockSpec(memory_space=pltpu.VMEM)
    smem = pl.BlockSpec(memory_space=pltpu.SMEM)
    specs = [smem] * scalars + [vmem] * (len(operands) - scalars)
    if spaces is not None:
        specs = [pl.BlockSpec(memory_space=space) for space in spaces]
    return pl.pallas_call(
        kernel,
        in_specs=specs,
        out_specs=[vmem] * len(out_shape),
        out_shape=out_shape,
        scratch_shapes=list(scratch),
        compiler_params=pltpu.CompilerParams(vmem_limit_bytes=16 * MIB),
        cost_estimate=pl.CostEstimate(
            flops=int(us * 1.1e9), bytes_accessed=1_000_000, transcendentals=0
        ),
        name=name,
    )(*operands)


def sds(shape, dtype=BF):
    return jax.ShapeDtypeStruct(shape, dtype)


def pick_kernel(send_hbm, k_hbm, v_hbm, left_ref, right_ref, hot_ref, send_ref, k_ref, v_ref, sem):
    rows, features = k_ref.shape
    capacity = send_ref.shape[1]
    named_copy = pltpu.make_async_copy(send_hbm, send_ref, sem.at[0])
    named_copy.start()
    copies = []
    for source, target in ((k_hbm, k_ref), (v_hbm, v_ref)):
        for start in range(0, rows, 128):
            part = slice(start, start + 128)
            copy = pltpu.make_async_copy(source.at[part], target.at[part], sem.at[1 + len(copies)])
            copy.start()
            copies.append(copy)
    named_copy.wait()
    lane = iota((capacity, 128), 1)
    for side in range(2):
        named = along_rows(send_ref[side : side + 1, :])
        for start in range(0, rows, 128):
            hot_ref[side * capacity : (side + 1) * capacity, start : start + 128] = one_hot(
                named == lane + start
            )
    for index, target in enumerate((k_ref, v_ref)):
        for copy in copies[index * len(copies) // 2 : (index + 1) * len(copies) // 2]:
            copy.wait()
        for part in chunks(features):
            picked = dot(hot_ref[...], target[:, part]).astype(BF)
            left_ref[index, :, part] = picked[:capacity]
            right_ref[index, :, part] = picked[capacity:]


def pick(send, k, v):
    rows, features = k.shape
    capacity = send.shape[1]
    slots = sds((2, capacity, features))
    return local(
        pick_kernel,
        "pick",
        2,
        [slots, slots, sds((2 * capacity, rows))],
        [pltpu.with_memory_space_constraint(x, pltpu.HBM) for x in (send, k, v)],
        scratch=(
            pltpu.VMEM((2, capacity), jnp.int32),
            pltpu.VMEM((rows, features), BF),
            pltpu.VMEM((rows, features), BF),
            pltpu.SemaphoreType.DMA((1 + 2 * (rows // 128),)),
        ),
        spaces=(pl.ANY, pl.ANY, pl.ANY),
    )


def prep_kernel(
    docs_ref, take_ref, log_ref, named_ref, q_ref, k_ref, v_ref,
    left_ref, right_ref, qo_ref, ko_ref, vo_ref, hot_ref,
    mask_ref, cols_ref, rows_ref, facts_ref, state_ref, leave_ref, own_ref,
):
    rows, features = q_ref.shape
    heads = log_ref.shape[0]
    capacity = hot_ref.shape[1] // 2
    for part in chunks(features):
        picked = dot(named_ref[...], q_ref[:, part]).astype(BF)
        left_ref[0, :, part] = picked[:capacity]
        right_ref[0, :, part] = picked[capacity:]

    first = (lax.axis_index("seq") * rows).astype(jnp.int32)
    position = first + iota((rows, 1), 0)
    position_row = first + iota((1, rows), 1)
    segment = jnp.zeros((rows, 1), jnp.int32)
    segment_row = jnp.zeros((1, rows), jnp.int32)
    segment_first = jnp.int32(0)
    segment_last = jnp.int32(0)
    opens_first = jnp.int32(0)
    opens = jnp.int32(0)
    start = jnp.int32(0)
    for n in range(docs_ref.shape[0]):
        segment += (position >= start).astype(jnp.int32)
        segment_row += (position_row >= start).astype(jnp.int32)
        segment_first += (first >= start).astype(jnp.int32)
        segment_last += (first + rows - 1 >= start).astype(jnp.int32)
        opens_first += (first == start).astype(jnp.int32)
        opens += ((start >= first) & (start < first + rows)).astype(jnp.int32)
        start += docs_ref[n]
    below = iota((rows, rows), 0) >= iota((rows, rows), 1)
    scale = -0.5 * math.log2(features // heads)
    mask_ref[...] = jnp.where((segment == segment_row) & below, scale, MASKED)
    triangle = one_hot(below)
    logs = jnp.concatenate([log_ref[...], jnp.zeros((128 - heads, rows), F32)], axis=0).T
    high, middle, low = pieces(logs)
    running = (dot(triangle, high) + (dot(triangle, middle) + dot(triangle, low))) * LOG2E
    rows_ref[...] = running.T[:heads]
    final = running[rows - 1 : rows, :]
    keep_f = segment == segment_last
    keep_e = (segment == segment_first) & (opens_first == 0)
    leaving = jnp.where(keep_f, jnp.exp2(final - running), 0.0)
    entering = jnp.where(keep_e, jnp.exp2(running + scale), 0.0)
    through = jnp.where(opens == 0, jnp.exp2(final), 0.0)
    cols_ref[0], cols_ref[1], cols_ref[2] = leaving, entering, running
    lane = iota((rows, 128), 1)
    taken = along_rows(take_ref[...])
    for start_row in range(0, rows, 128):
        own_ref[:, start_row : start_row + 128] = one_hot(taken - capacity == lane + start_row)
    hot_ref[:, :capacity] = one_hot(taken == lane)
    hot_ref[:, capacity:] = one_hot(taken - (capacity + rows) == lane)
    leave_ref[...] = sum(dot_tn(hot_ref[...], piece) for piece in pieces(leaving))
    facts_ref[:heads] = leave_ref[capacity:, :].T[:heads]
    facts_ref[heads:] = along_rows(through, capacity)[:heads]
    for part in chunks(features):
        for source, target in ((k_ref, ko_ref), (v_ref, vo_ref), (q_ref, qo_ref)):
            target[:, part] = dot(own_ref[...], source[:, part]).astype(BF)
    for h, part in enumerate(head_slices(features, heads)):
        kf = (ko_ref[:, part].astype(F32) * cols_ref[0, :, h : h + 1]).astype(BF)
        state_ref[h] = dot_tn(kf, vo_ref[:, part])


def prep(docs, take, log_decay, named, q, k, v):
    rows, features = q.shape
    heads = log_decay.shape[0]
    width = features // heads
    capacity = named.shape[0] // 2
    slots, own_rows = sds((1, capacity, features)), sds((rows, features))
    return local(
        prep_kernel,
        "prep",
        30,
        [
            slots, slots, own_rows, own_rows, own_rows,
            sds((rows, 2 * capacity)),
            sds((rows, rows), F32),
            sds((3, rows, 128), F32),
            sds((heads, rows), F32),
            sds((2 * heads, capacity), F32),
            sds((heads, width, width), F32),
            sds((2 * capacity, 128), F32),
        ],
        (docs, take, log_decay, named, q, k, v),
        scalars=1,
        scratch=(pltpu.VMEM((rows, rows), BF),),
    )


def state_kernel(left_ref, right_ref, leave_ref, own_ref, message_ref):
    heads, width = own_ref.shape[:2]
    for h, part in enumerate(head_slices(heads * width, heads)):
        k = jnp.concatenate([left_ref[0, :, part], right_ref[0, :, part]], axis=0)
        v = jnp.concatenate([left_ref[1, :, part], right_ref[1, :, part]], axis=0)
        kf = (k.astype(F32) * leave_ref[:, h : h + 1]).astype(BF)
        message_ref[h] = (own_ref[h] + dot_tn(kf, v)).astype(BF)


def assemble(hot_ref, left_ref, right_ref, index, own_rows, target):
    for part in chunks(target.shape[1]):
        extra = jnp.concatenate([left_ref[index, :, part], right_ref[index, :, part]], axis=0)
        target[:, part] = own_rows[:, part] + dot(hot_ref[...], extra).astype(BF)


def assemble_kernel(hot_ref, left_ref, right_ref, ko_ref, vo_ref, _, _before, _after, k_ref, v_ref):
    assemble(hot_ref, left_ref, right_ref, 0, ko_ref, k_ref)
    assemble(hot_ref, left_ref, right_ref, 1, vo_ref, v_ref)


def decay(mask_ref, cols_ref, rows_ref, h, top, half, reach):
    column = cols_ref[2, top : top + half, h : h + 1]
    row = rows_ref[h : h + 1, :reach]
    return jnp.exp2((column - row) + mask_ref[top : top + half, :reach])


def inside_kernel(hot_ref, left_ref, right_ref, qo_ref, k_ref, v_ref, mask_ref, cols_ref, rows_ref, q_ref, qe_ref, weight_ref, p_ref, o_ref):
    rows, features = k_ref.shape
    assemble(hot_ref, left_ref, right_ref, 0, qo_ref, q_ref)
    heads, half = p_ref.shape[0], rows // 2
    for h, part in enumerate(head_slices(features, heads)):
        for i in range(2):
            top, reach = i * half, (i + 1) * half
            here = slice(top, top + half)
            scores = dot_nt(q_ref[here, part], k_ref[:reach, part])
            weight = decay(mask_ref, cols_ref, rows_ref, h, top, half, reach)
            weight_ref[h, here, :reach] = weight
            p = (scores * weight).astype(BF)
            p_ref[h, here, :reach] = p
            o_ref[here, part] = dot(p, v_ref[:reach, part])
        qe = (q_ref[:, part].astype(F32) * cols_ref[1, :, h : h + 1]).astype(BF)
        qe_ref[h] = qe.T


def shards_before(direction):
    index = lax.axis_index("seq")
    return index if direction > 0 else lax.axis_size("seq") - 1 - index


def decayed(facts_ref, h, state):
    heads, width = facts_ref.shape[0] // 2, state.shape[1]
    return facts_ref[heads + h : heads + h + 1, :width] * state


def carried_sum(before, facts_ref, near_ref, far_ref, h):
    near = near_ref[h].astype(F32)
    far = decayed(facts_ref, h, far_ref[h].astype(F32))
    near = jnp.where(before >= 1, near, 0.0)
    return near + jnp.where(before >= 2, far, 0.0)


def joined(before, facts_ref, near_ref, far_ref, h):
    return carried_sum(before, facts_ref, near_ref, far_ref, h).astype(BF)


def output_kernel(scale_ref, o_ref, q_ref, facts_ref, near_ref, far_ref, cols_ref, ct_ref, u_ref, h_ref, sums_ref):
    rows, features = q_ref.shape
    heads, width = h_ref.shape[:2]
    before = shards_before(1)
    squares = jnp.zeros((rows, width), F32)
    cross = jnp.zeros((rows, width), F32)
    for h, part in enumerate(head_slices(features, heads)):
        carried_in = joined(before, facts_ref, near_ref, far_ref, h)
        h_ref[h] = carried_in
        outer = dot(q_ref[:, part], carried_in) * cols_ref[1, :, h : h + 1]
        u = (o_ref[:, part] + outer) * scale_ref[h]
        u_ref[:, part] = u
        squares += u * u
        cross += ct_ref[:, part].astype(F32) * u
    sums_ref[0:1, :] = jnp.sum(squares.T, axis=0, keepdims=True)
    sums_ref[1:2, :] = jnp.sum(cross.T, axis=0, keepdims=True)


def norm_kernel(total, scale_ref, u_ref, ct_ref, qe_ref, *refs):
    *sums, g_ref, message_ref, inverse_ref = refs
    features = u_ref.shape[1]
    heads, width = qe_ref.shape[:2]
    summed = sums[0][...]
    for more in sums[1:]:
        summed += more[...]
    inverse = lax.rsqrt(along_rows(summed[0:1, :], width) / total + EPSILON)
    mean = inverse * inverse * inverse * (along_rows(summed[1:2, :], width) / total)
    inverse_ref[...] = inverse
    for h, part in enumerate(head_slices(features, heads)):
        g = (inverse * ct_ref[:, part].astype(F32) - u_ref[:, part] * mean) * scale_ref[h]
        g = g.astype(BF)
        g_ref[:, part] = g
        message_ref[h] = dot(qe_ref[h], g).astype(BF)


def normed_kernel(u_ref, inverse_ref, _, normed_ref):
    rows, features = u_ref.shape
    width = inverse_ref.shape[1]
    for part in head_slices(features, features // width):
        normed_ref[:, part] = (u_ref[:, part] * inverse_ref[...]).astype(BF)


def send_back(hot, source, left_ref, right_ref, index):
    capacity = left_ref.shape[1]
    for part in chunks(source.shape[1]):
        back = dot(hot, source[:, part]).astype(BF)
        left_ref[index, :, part] = back[:capacity]
        right_ref[index, :, part] = back[capacity:]


def slots_hot(take_ref, capacity):
    rows = take_ref.shape[1]
    taken = jnp.broadcast_to(take_ref[...], (capacity, rows))
    slot = iota((capacity, rows), 0)
    return jnp.concatenate(
        [one_hot(taken == slot), one_hot(taken - (capacity + rows) == slot)], axis=0
    )


def grad_q_kernel(take_ref, g_ref, k_ref, v_ref, h_ref, weight_ref, cols_ref, dq_ref, z_ref, left_ref, right_ref):
    rows, features = k_ref.shape
    heads, half = h_ref.shape[0], rows // 2
    for h, part in enumerate(head_slices(features, heads)):
        for i in range(2):
            top, reach = i * half, (i + 1) * half
            here = slice(top, top + half)
            g = g_ref[here, part]
            z = (dot_nt(g, v_ref[:reach, part]) * weight_ref[h, here, :reach]).astype(BF)
            z_ref[h, here, :reach] = z
            outer = dot_nt(g, h_ref[h]) * cols_ref[1, here, h : h + 1]
            dq_ref[here, part] = (dot(z, k_ref[:reach, part]) + outer).astype(BF)
    send_back(slots_hot(take_ref, left_ref.shape[1]), dq_ref, left_ref, right_ref, 0)


def inner_kernel(z_ref, p_ref, q_ref, g_ref, dk_ref, dv_ref):
    rows, features = q_ref.shape
    heads, half = z_ref.shape[0], rows // 2
    for h, part in enumerate(head_slices(features, heads)):
        for square, source, target in ((z_ref, q_ref, dk_ref), (p_ref, g_ref, dv_ref)):
            for j in range(2):
                here = slice(j * half, (j + 1) * half)
                target[here, part] = dot_tn(square[h, j * half :, here], source[j * half :, part])


def right_kernel(take_ref, dk_ref, dv_ref, _, right_ref):
    capacity, features = right_ref.shape[1:]
    hot = slots_hot(take_ref, capacity)[capacity:]
    for index, source in enumerate((dk_ref, dv_ref)):
        for part in chunks(features):
            right_ref[index, :, part] = dot(hot, source[:, part].astype(BF)).astype(BF)


def grad_kv_kernel(take_ref, far_ref, near_ref, facts_ref, k_ref, v_ref, cols_ref, dki_ref, dvi_ref, dk_ref, dv_ref, left_ref):
    rows, features = k_ref.shape
    heads = near_ref.shape[0]
    before = shards_before(-1)
    for h, part in enumerate(head_slices(features, heads)):
        state_grad = joined(before, facts_ref, near_ref, far_ref, h)
        leaving = cols_ref[0, :, h : h + 1]
        dk_ref[:, part] = (dki_ref[:, part] + leaving * dot_nt(v_ref[:, part], state_grad)).astype(BF)
        dv_ref[:, part] = (dvi_ref[:, part] + leaving * dot(k_ref[:, part], state_grad)).astype(BF)
    hot = slots_hot(take_ref, left_ref.shape[1])[: left_ref.shape[1]]
    for index, source in enumerate((dk_ref, dv_ref)):
        for part in chunks(features):
            left_ref[index, :, part] = dot(hot, source[:, part]).astype(BF)


def lend_kernel(facts_ref, after_ref, near_ref, far_ref, message_ref, lent_ref, rows_ref, _, dk_ref, dv_ref):
    features = dk_ref.shape[1]
    heads, width = message_ref.shape[:2]
    before = shards_before(-1)
    for h, part in enumerate(head_slices(features, heads)):
        after = carried_sum(before, after_ref, near_ref, far_ref, h)
        state_grad = (message_ref[h].astype(F32) + decayed(facts_ref, h, after)).astype(BF)
        leaving = along_rows(lent_ref[h : h + 1, :], width)
        dk_ref[:, part] = leaving * dot_nt(rows_ref[1, :, part], state_grad)
        dv_ref[:, part] = leaving * dot(rows_ref[0, :, part], state_grad)


def own_kernel(capacity, count, take_ref, *refs):
    rows = refs[0].shape[0]
    taken = jnp.broadcast_to(take_ref[...], (rows, rows))
    hot = one_hot(taken - capacity == iota((rows, rows), 0))
    for source, target in zip(refs[:count], refs[-count:]):
        for part in chunks(source.shape[1]):
            target[:, part] = dot(hot, source[:, part]).astype(BF)


def finish_kernel(count, lending, send_ref, left_ref, right_ref, *refs):
    lent, refs = refs[:lending], refs[lending:]
    rows = refs[0].shape[0]
    capacity = send_ref.shape[1]
    line = iota((rows, capacity), 0)
    hot = jnp.concatenate(
        [
            one_hot(jnp.broadcast_to(send_ref[side : side + 1, :], (rows, capacity)) == line)
            for side in range(2)
        ],
        axis=1,
    )
    for index, (source, target) in enumerate(zip(refs[:count], refs[count : 2 * count])):
        for part in chunks(source.shape[1]):
            left = left_ref[index, :, part]
            if lending:
                left = (left.astype(F32) + lent[index][:, part]).astype(BF)
            back = jnp.concatenate([left, right_ref[index, :, part]], axis=0)
            target[:, part] = source[:, part] + dot(hot, back).astype(BF)
    for order in refs[2 * count :]:
        order[...] = jnp.zeros_like(order)


def shifted(array, by):
    peers = lax.axis_size("seq")
    return lax.ppermute(array, "seq", [(i, (i + by) % peers) for i in range(peers)])


def shifted_open(array, by):
    peers = lax.axis_size("seq")
    return lax.ppermute(array, "seq", [(i, i + by) for i in range(peers) if 0 <= i + by < peers])


def add_kernel(a_ref, b_ref, sum_ref):
    sum_ref[...] = a_ref[...] + b_ref[...]


def over_heads(sums):
    peers = lax.axis_size("head")
    distance = 1
    pair = (sums,)
    while distance < peers:
        if len(pair) == 2:
            pair = local(add_kernel, "add", 1, [sds(sums.shape, F32)], pair)
        pairs = [(i, i ^ distance) for i in range(peers)]
        pair = (pair[0], lax.ppermute(pair[0], "head", pairs))
        distance *= 2
    return pair


def carried(message, facts, direction):
    peers = lax.axis_size("seq")
    reach = peers // 4
    if reach <= 2:
        return shifted(message, direction), shifted(message, 2 * direction)
    own_state = message.astype(F32)
    through = facts[message.shape[0] :, :1, None]

    def relay(_, state_here):
        return shifted_open((through * state_here + own_state).astype(BF), direction).astype(F32)

    incoming = lax.fori_loop(0, reach, relay, jnp.zeros_like(own_state)).astype(BF)
    return incoming, jnp.zeros_like(message)


def on_device(
    queries, key_vectors, value_vectors, log_decay, head_scale,
    send_rows, take_rows, doc_lengths, cotangent,
):
    rows, features = queries.shape
    heads = head_scale.shape[0]
    width = features // heads
    capacity = send_rows.shape[2]
    send = send_rows.reshape(2, capacity)
    take = take_rows.reshape(1, rows)
    total = features * lax.axis_size("head")
    full, full32 = sds((rows, features)), sds((rows, features), F32)
    squares = sds((heads, rows, rows))
    message_shape = sds((heads, width, width))
    one_side, two_sides = sds((1, capacity, features)), sds((2, capacity, features))

    kv_left, kv_right, named = pick(send, key_vectors, value_vectors)
    kv_before, kv_after = shifted(kv_right, 1), shifted(kv_left, -1)
    (
        q_left, q_right, q_own, k_own, v_own, hot, mask, cols, turned, facts, state_own, leave
    ) = prep(doc_lengths, take, log_decay.T, named, queries, key_vectors, value_vectors)
    q_before, q_after = shifted(q_right, 1), shifted(q_left, -1)
    (message,) = local(
        state_kernel, "state", 30, [message_shape], (kv_before, kv_after, leave, state_own)
    )
    near, far = carried(message, facts, 1)
    facts_before, facts_after = shifted(facts, 1), shifted(facts, -1)
    k, v = local(
        assemble_kernel,
        "assemble",
        5,
        [full, full],
        (hot, kv_before, kv_after, k_own, v_own, message, facts_before, facts_after),
    )
    q, qe, weight, probs, o_inside = local(
        inside_kernel,
        "inside",
        30,
        [full, sds((heads, width, rows)), sds((heads, rows, rows), F32), squares, full32],
        (hot, q_before, q_after, q_own, k, v, mask, cols, turned),
    )
    u, state_low, sums = local(
        output_kernel,
        "output",
        3,
        [full32, sds((heads, width, width)), sds((2, rows), F32)],
        (head_scale, o_inside, q, facts_before, near, far, cols, cotangent),
        scalars=1,
    )
    sums = over_heads(sums)
    g, grad_message, inverse = local(
        functools.partial(norm_kernel, total),
        "norm",
        4,
        [full, message_shape, sds((rows, width), F32)],
        (head_scale, u, cotangent, qe, *sums),
        scalars=1,
    )
    grad_near, grad_far = carried(grad_message, facts, -1)
    dq, z, dq_left, dq_right = local(
        grad_q_kernel,
        "grad_q",
        30,
        [full, squares, one_side, one_side],
        (take, g, k, v, state_low, weight, cols),
    )
    dq_before, dq_after = shifted(dq_right, 1), shifted(dq_left, -1)
    dk_inner, dv_inner = local(inner_kernel, "inner", 5, [full32, full32], (z, probs, q, g))
    (dkv_right,) = local(
        right_kernel, "right", 30, [two_sides], (take, dk_inner, dv_inner, grad_near)
    )
    dkv_before = shifted(dkv_right, 1)
    dk, dv, dkv_left = local(
        grad_kv_kernel,
        "grad_kv",
        3,
        [full, full, two_sides],
        (take, grad_far, grad_near, facts_after, k, v, cols, dk_inner, dv_inner),
    )
    dkv_after = shifted(dkv_left, -1)
    lent_rows = sds((capacity, features), F32)
    dk_lent, dv_lent = local(
        lend_kernel,
        "lend",
        2,
        [lent_rows, lent_rows],
        (facts, facts_after, grad_near, grad_far, grad_message, facts_before, kv_left, dk),
    )
    (normed,) = local(normed_kernel, "normed", 2, [full], (u, inverse, dk))
    (dq_own,) = local(
        functools.partial(own_kernel, capacity, 1), "own_q", 2, [full], (take, dq, dk)
    )
    grad_queries, order = local(
        functools.partial(finish_kernel, 1, 0),
        "finish_q",
        2,
        [full, sds((16, 128))],
        (send, dq_before, dq_after, dq_own),
    )
    dk_own, dv_own = local(
        functools.partial(own_kernel, capacity, 2), "own_kv", 2, [full, full],
        (take, dk, dv, order),
    )
    grad_keys, grad_values = local(
        functools.partial(finish_kernel, 2, 2),
        "finish_kv",
        2,
        [full, full],
        (send, dkv_before, dkv_after, dk_lent, dv_lent, dk_own, dv_own),
    )
    return normed, grad_queries, grad_keys, grad_values


def solution(mesh):
    both = P("seq", "head")
    in_specs = (both, both, both, both, P("head"), P("seq", None, None), P("seq"), P(), both)
    return jax.shard_map(
        on_device, mesh=mesh, in_specs=in_specs, out_specs=(both,) * 4, check_vma=False
    )
```

```python
import functools
import math

import jax
import jax.numpy as jnp
from jax import lax
from jax.experimental import pallas as pl
from jax.experimental.pallas import tpu as pltpu
from jax.sharding import PartitionSpec as P

EPSILON = 1e-05
LOG2E = math.log2(math.e)
MASKED = -1e30
MIB = 1024 * 1024
BF = jnp.bfloat16
F32 = jnp.float32
NT = (((1,), (1,)), ((), ()))
TN = (((0,), (0,)), ((), ()))
CHUNK = 256


def dot(a, b):
    return jnp.dot(a, b, preferred_element_type=F32)


def dot_nt(a, b):
    return lax.dot_general(a, b, NT, preferred_element_type=F32)


def dot_tn(a, b):
    return lax.dot_general(a, b, TN, preferred_element_type=F32)


def along_rows(row, lanes=128):
    return jnp.broadcast_to(row, (lanes, row.shape[1])).T


def iota(shape, dim):
    return lax.broadcasted_iota(jnp.int32, shape, dim)


def one_hot(hit):
    return jnp.where(hit, 1.0, 0.0).astype(BF)


def pieces(x):
    high = x.astype(BF)
    rest = x - high.astype(F32)
    middle = rest.astype(BF)
    return high, middle, (rest - middle.astype(F32)).astype(BF)


def chunks(features):
    return [slice(start, start + CHUNK) for start in range(0, features, CHUNK)]


def head_slices(features, heads):
    width = features // heads
    return [slice(h * width, (h + 1) * width) for h in range(heads)]


def local(kernel, name, us, out_shape, operands, scalars=0, scratch=(), spaces=None):
    vmem = pl.BlockSpec(memory_space=pltpu.VMEM)
    smem = pl.BlockSpec(memory_space=pltpu.SMEM)
    specs = [smem] * scalars + [vmem] * (len(operands) - scalars)
    if spaces is not None:
        specs = [pl.BlockSpec(memory_space=space) for space in spaces]
    return pl.pallas_call(
        kernel,
        in_specs=specs,
        out_specs=[vmem] * len(out_shape),
        out_shape=out_shape,
        scratch_shapes=list(scratch),
        compiler_params=pltpu.CompilerParams(vmem_limit_bytes=16 * MIB),
        cost_estimate=pl.CostEstimate(
            flops=int(us * 1.1e9), bytes_accessed=1_000_000, transcendentals=0
        ),
        name=name,
    )(*operands)


def sds(shape, dtype=BF):
    return jax.ShapeDtypeStruct(shape, dtype)


def is_odd():
    return lax.rem(lax.axis_index("seq"), 2) == 1


def pick_kernel(send_hbm, k_hbm, v_hbm, pair_ref, other_ref, hot_ref, send_ref, k_ref, v_ref, sem):
    rows, features = k_ref.shape
    capacity = send_ref.shape[1]
    named_copy = pltpu.make_async_copy(send_hbm, send_ref, sem.at[0])
    named_copy.start()
    copies = []
    for source, target in ((k_hbm, k_ref), (v_hbm, v_ref)):
        for start in range(0, rows, 128):
            part = slice(start, start + 128)
            copy = pltpu.make_async_copy(source.at[part], target.at[part], sem.at[1 + len(copies)])
            copy.start()
            copies.append(copy)
    named_copy.wait()
    lane = iota((capacity, 128), 1)
    for side in range(2):
        slots = jnp.where(is_odd(), send_ref[side : side + 1, :], send_ref[1 - side : 2 - side, :])
        named = along_rows(slots)
        for start in range(0, rows, 128):
            hot_ref[side * capacity : (side + 1) * capacity, start : start + 128] = one_hot(
                named == lane + start
            )
    for index, target in enumerate((k_ref, v_ref)):
        for copy in copies[index * len(copies) // 2 : (index + 1) * len(copies) // 2]:
            copy.wait()
        for part in chunks(features):
            picked = dot(hot_ref[...], target[:, part]).astype(BF)
            pair_ref[index, :, part] = picked[:capacity]
            other_ref[index, :, part] = picked[capacity:]


def pick(send, k, v):
    rows, features = k.shape
    capacity = send.shape[1]
    slots = sds((2, capacity, features))
    return local(
        pick_kernel,
        "pick",
        2,
        [slots, slots, sds((2 * capacity, rows))],
        [pltpu.with_memory_space_constraint(x, pltpu.HBM) for x in (send, k, v)],
        scratch=(
            pltpu.VMEM((2, capacity), jnp.int32),
            pltpu.VMEM((rows, features), BF),
            pltpu.VMEM((rows, features), BF),
            pltpu.SemaphoreType.DMA((1 + 2 * (rows // 128),)),
        ),
        spaces=(pl.ANY, pl.ANY, pl.ANY),
    )


def prep_kernel(
    docs_ref, take_ref, log_ref, named_ref, q_ref, k_ref, v_ref,
    left_ref, right_ref, qo_ref, ko_ref, vo_ref, hot_ref,
    mask_ref, cols_ref, rows_ref, facts_ref, state_ref, leave_ref, own_ref,
):
    rows, features = q_ref.shape
    heads = log_ref.shape[0]
    capacity = hot_ref.shape[1] // 2
    for part in chunks(features):
        picked = dot(named_ref[...], q_ref[:, part]).astype(BF)
        left_ref[0, :, part] = picked[:capacity]
        right_ref[0, :, part] = picked[capacity:]

    first = (lax.axis_index("seq") * rows).astype(jnp.int32)
    position = first + iota((rows, 1), 0)
    position_row = first + iota((1, rows), 1)
    segment = jnp.zeros((rows, 1), jnp.int32)
    segment_row = jnp.zeros((1, rows), jnp.int32)
    segment_first = jnp.int32(0)
    segment_last = jnp.int32(0)
    opens_first = jnp.int32(0)
    opens = jnp.int32(0)
    start = jnp.int32(0)
    for n in range(docs_ref.shape[0]):
        segment += (position >= start).astype(jnp.int32)
        segment_row += (position_row >= start).astype(jnp.int32)
        segment_first += (first >= start).astype(jnp.int32)
        segment_last += (first + rows - 1 >= start).astype(jnp.int32)
        opens_first += (first == start).astype(jnp.int32)
        opens += ((start >= first) & (start < first + rows)).astype(jnp.int32)
        start += docs_ref[n]
    below = iota((rows, rows), 0) >= iota((rows, rows), 1)
    scale = -0.5 * math.log2(features // heads)
    mask_ref[...] = jnp.where((segment == segment_row) & below, scale, MASKED)
    triangle = one_hot(below)
    logs = jnp.concatenate([log_ref[...], jnp.zeros((128 - heads, rows), F32)], axis=0).T
    high, middle, low = pieces(logs)
    running = (dot(triangle, high) + (dot(triangle, middle) + dot(triangle, low))) * LOG2E
    rows_ref[...] = running.T[:heads]
    final = running[rows - 1 : rows, :]
    keep_f = segment == segment_last
    keep_e = (segment == segment_first) & (opens_first == 0)
    leaving = jnp.where(keep_f, jnp.exp2(final - running), 0.0)
    entering = jnp.where(keep_e, jnp.exp2(running + scale), 0.0)
    through = jnp.where(opens == 0, jnp.exp2(final), 0.0)
    cols_ref[0], cols_ref[1], cols_ref[2] = leaving, entering, running
    lane = iota((rows, 128), 1)
    taken = along_rows(take_ref[...])
    for start_row in range(0, rows, 128):
        own_ref[:, start_row : start_row + 128] = one_hot(taken - capacity == lane + start_row)
    right = capacity + rows
    odd = is_odd()
    hot_ref[:, :capacity] = one_hot(taken - jnp.where(odd, 0, right) == lane)
    hot_ref[:, capacity:] = one_hot(taken - jnp.where(odd, right, 0) == lane)
    leave_ref[...] = sum(dot_tn(hot_ref[...], piece) for piece in pieces(leaving))
    facts_ref[:heads] = jnp.where(odd, leave_ref[capacity:, :], leave_ref[:capacity, :]).T[:heads]
    facts_ref[heads:] = along_rows(through, capacity)[:heads]
    for part in chunks(features):
        for source, target in ((k_ref, ko_ref), (v_ref, vo_ref), (q_ref, qo_ref)):
            target[:, part] = dot(own_ref[...], source[:, part]).astype(BF)
    for h, part in enumerate(head_slices(features, heads)):
        kf = (ko_ref[:, part].astype(F32) * cols_ref[0, :, h : h + 1]).astype(BF)
        state_ref[h] = dot_tn(kf, vo_ref[:, part])


def prep(docs, take, log_decay, named, q, k, v):
    rows, features = q.shape
    heads = log_decay.shape[0]
    width = features // heads
    capacity = named.shape[0] // 2
    slots, own_rows = sds((1, capacity, features)), sds((rows, features))
    return local(
        prep_kernel,
        "prep",
        30,
        [
            slots, slots, own_rows, own_rows, own_rows,
            sds((rows, 2 * capacity)),
            sds((rows, rows), F32),
            sds((3, rows, 128), F32),
            sds((heads, rows), F32),
            sds((2 * heads, capacity), F32),
            sds((heads, width, width), F32),
            sds((2 * capacity, 128), F32),
        ],
        (docs, take, log_decay, named, q, k, v),
        scalars=1,
        scratch=(pltpu.VMEM((rows, rows), BF),),
    )


def state_kernel(left_ref, right_ref, leave_ref, own_ref, message_ref):
    heads, width = own_ref.shape[:2]
    for h, part in enumerate(head_slices(heads * width, heads)):
        k = jnp.concatenate([left_ref[0, :, part], right_ref[0, :, part]], axis=0)
        v = jnp.concatenate([left_ref[1, :, part], right_ref[1, :, part]], axis=0)
        kf = (k.astype(F32) * leave_ref[:, h : h + 1]).astype(BF)
        message_ref[h] = (own_ref[h] + dot_tn(kf, v)).astype(BF)


def assemble(hot_ref, left_ref, right_ref, index, own_rows, target):
    for part in chunks(target.shape[1]):
        extra = jnp.concatenate([left_ref[index, :, part], right_ref[index, :, part]], axis=0)
        target[:, part] = own_rows[:, part] + dot(hot_ref[...], extra).astype(BF)


def assemble_kernel(hot_ref, left_ref, right_ref, ko_ref, vo_ref, _, _before, _after, k_ref, v_ref):
    assemble(hot_ref, left_ref, right_ref, 0, ko_ref, k_ref)
    assemble(hot_ref, left_ref, right_ref, 1, vo_ref, v_ref)


def decay(mask_ref, cols_ref, rows_ref, h, top, half, reach):
    column = cols_ref[2, top : top + half, h : h + 1]
    row = rows_ref[h : h + 1, :reach]
    return jnp.exp2((column - row) + mask_ref[top : top + half, :reach])


def inside_kernel(hot_ref, left_ref, right_ref, qo_ref, k_ref, v_ref, mask_ref, cols_ref, rows_ref, q_ref, qe_ref, weight_ref, p_ref, o_ref):
    rows, features = k_ref.shape
    assemble(hot_ref, left_ref, right_ref, 0, qo_ref, q_ref)
    heads, half = p_ref.shape[0], rows // 2
    for h, part in enumerate(head_slices(features, heads)):
        for i in range(2):
            top, reach = i * half, (i + 1) * half
            here = slice(top, top + half)
            scores = dot_nt(q_ref[here, part], k_ref[:reach, part])
            weight = decay(mask_ref, cols_ref, rows_ref, h, top, half, reach)
            weight_ref[h, here, :reach] = weight
            p = (scores * weight).astype(BF)
            p_ref[h, here, :reach] = p
            o_ref[here, part] = dot(p, v_ref[:reach, part])
        qe = (q_ref[:, part].astype(F32) * cols_ref[1, :, h : h + 1]).astype(BF)
        qe_ref[h] = qe.T


def shards_before(direction):
    index = lax.axis_index("seq")
    return index if direction > 0 else lax.axis_size("seq") - 1 - index


def decayed(facts_ref, h, state):
    heads, width = facts_ref.shape[0] // 2, state.shape[1]
    return facts_ref[heads + h : heads + h + 1, :width] * state


def carried_sum(before, facts_ref, near_ref, far_ref, h):
    near = near_ref[h].astype(F32)
    far = decayed(facts_ref, h, far_ref[h].astype(F32))
    near = jnp.where(before >= 1, near, 0.0)
    return near + jnp.where(before >= 2, far, 0.0)


def joined(before, facts_ref, near_ref, far_ref, h):
    return carried_sum(before, facts_ref, near_ref, far_ref, h).astype(BF)


def output_kernel(scale_ref, o_ref, q_ref, facts_ref, near_ref, far_ref, cols_ref, ct_ref, u_ref, h_ref, sums_ref):
    rows, features = q_ref.shape
    heads, width = h_ref.shape[:2]
    before = shards_before(1)
    squares = jnp.zeros((rows, width), F32)
    cross = jnp.zeros((rows, width), F32)
    for h, part in enumerate(head_slices(features, heads)):
        carried_in = joined(before, facts_ref, near_ref, far_ref, h)
        h_ref[h] = carried_in
        outer = dot(q_ref[:, part], carried_in) * cols_ref[1, :, h : h + 1]
        u = (o_ref[:, part] + outer) * scale_ref[h]
        u_ref[:, part] = u
        squares += u * u
        cross += ct_ref[:, part].astype(F32) * u
    sums_ref[0:1, :] = jnp.sum(squares.T, axis=0, keepdims=True)
    sums_ref[1:2, :] = jnp.sum(cross.T, axis=0, keepdims=True)


def norm_kernel(total, scale_ref, u_ref, ct_ref, qe_ref, *refs):
    *sums, g_ref, message_ref, inverse_ref = refs
    features = u_ref.shape[1]
    heads, width = qe_ref.shape[:2]
    summed = sums[0][...]
    for more in sums[1:]:
        summed += more[...]
    inverse = lax.rsqrt(along_rows(summed[0:1, :], width) / total + EPSILON)
    mean = inverse * inverse * inverse * (along_rows(summed[1:2, :], width) / total)
    inverse_ref[...] = inverse
    for h, part in enumerate(head_slices(features, heads)):
        g = (inverse * ct_ref[:, part].astype(F32) - u_ref[:, part] * mean) * scale_ref[h]
        g = g.astype(BF)
        g_ref[:, part] = g
        message_ref[h] = dot(qe_ref[h], g).astype(BF)


def normed_kernel(u_ref, inverse_ref, _, normed_ref):
    rows, features = u_ref.shape
    width = inverse_ref.shape[1]
    for part in head_slices(features, features // width):
        normed_ref[:, part] = (u_ref[:, part] * inverse_ref[...]).astype(BF)


def send_back(hot, source, left_ref, right_ref, index):
    capacity = left_ref.shape[1]
    for part in chunks(source.shape[1]):
        back = dot(hot, source[:, part]).astype(BF)
        left_ref[index, :, part] = back[:capacity]
        right_ref[index, :, part] = back[capacity:]


def slots_hot(take_ref, capacity):
    rows = take_ref.shape[1]
    taken = jnp.broadcast_to(take_ref[...], (capacity, rows))
    slot = iota((capacity, rows), 0)
    return jnp.concatenate(
        [one_hot(taken == slot), one_hot(taken - (capacity + rows) == slot)], axis=0
    )


def grad_q_kernel(take_ref, g_ref, k_ref, v_ref, h_ref, weight_ref, cols_ref, dq_ref, z_ref, left_ref, right_ref):
    rows, features = k_ref.shape
    heads, half = h_ref.shape[0], rows // 2
    for h, part in enumerate(head_slices(features, heads)):
        for i in range(2):
            top, reach = i * half, (i + 1) * half
            here = slice(top, top + half)
            g = g_ref[here, part]
            z = (dot_nt(g, v_ref[:reach, part]) * weight_ref[h, here, :reach]).astype(BF)
            z_ref[h, here, :reach] = z
            outer = dot_nt(g, h_ref[h]) * cols_ref[1, here, h : h + 1]
            dq_ref[here, part] = (dot(z, k_ref[:reach, part]) + outer).astype(BF)
    send_back(slots_hot(take_ref, left_ref.shape[1]), dq_ref, left_ref, right_ref, 0)


def inner_kernel(z_ref, p_ref, q_ref, g_ref, dk_ref, dv_ref):
    rows, features = q_ref.shape
    heads, half = z_ref.shape[0], rows // 2
    for h, part in enumerate(head_slices(features, heads)):
        for square, source, target in ((z_ref, q_ref, dk_ref), (p_ref, g_ref, dv_ref)):
            for j in range(2):
                here = slice(j * half, (j + 1) * half)
                target[here, part] = dot_tn(square[h, j * half :, here], source[j * half :, part])


def right_kernel(take_ref, dk_ref, dv_ref, _, right_ref):
    capacity, features = right_ref.shape[1:]
    hot = slots_hot(take_ref, capacity)[capacity:]
    for index, source in enumerate((dk_ref, dv_ref)):
        for part in chunks(features):
            right_ref[index, :, part] = dot(hot, source[:, part].astype(BF)).astype(BF)


def grad_kv_kernel(take_ref, far_ref, near_ref, facts_ref, k_ref, v_ref, cols_ref, dki_ref, dvi_ref, dk_ref, dv_ref, left_ref):
    rows, features = k_ref.shape
    heads = near_ref.shape[0]
    before = shards_before(-1)
    for h, part in enumerate(head_slices(features, heads)):
        state_grad = joined(before, facts_ref, near_ref, far_ref, h)
        leaving = cols_ref[0, :, h : h + 1]
        dk_ref[:, part] = (dki_ref[:, part] + leaving * dot_nt(v_ref[:, part], state_grad)).astype(BF)
        dv_ref[:, part] = (dvi_ref[:, part] + leaving * dot(k_ref[:, part], state_grad)).astype(BF)
    hot = slots_hot(take_ref, left_ref.shape[1])[: left_ref.shape[1]]
    for index, source in enumerate((dk_ref, dv_ref)):
        for part in chunks(features):
            left_ref[index, :, part] = dot(hot, source[:, part]).astype(BF)


def lend_kernel(facts_ref, after_ref, near_ref, far_ref, message_ref, lent_ref, pair_ref, other_ref, _, dk_ref, dv_ref):
    features = dk_ref.shape[1]
    heads, width = message_ref.shape[:2]
    before = shards_before(-1)
    for h, part in enumerate(head_slices(features, heads)):
        after = carried_sum(before, after_ref, near_ref, far_ref, h)
        state_grad = (message_ref[h].astype(F32) + decayed(facts_ref, h, after)).astype(BF)
        leaving = along_rows(lent_ref[h : h + 1, :], width)
        k, v = [
            jnp.where(is_odd(), pair_ref[index, :, part], other_ref[index, :, part])
            for index in range(2)
        ]
        dk_ref[:, part] = leaving * dot_nt(v, state_grad)
        dv_ref[:, part] = leaving * dot(k, state_grad)


def own_kernel(capacity, count, take_ref, *refs):
    rows = refs[0].shape[0]
    taken = jnp.broadcast_to(take_ref[...], (rows, rows))
    hot = one_hot(taken - capacity == iota((rows, rows), 0))
    for source, target in zip(refs[:count], refs[-count:]):
        for part in chunks(source.shape[1]):
            target[:, part] = dot(hot, source[:, part]).astype(BF)


def finish_kernel(count, lending, send_ref, right_ref, left_ref, *refs):
    lent, refs = refs[:lending], refs[lending:]
    rows = refs[0].shape[0]
    capacity = send_ref.shape[1]
    line = iota((rows, capacity), 0)
    hot = jnp.concatenate(
        [
            one_hot(jnp.broadcast_to(send_ref[side : side + 1, :], (rows, capacity)) == line)
            for side in range(2)
        ],
        axis=1,
    )
    for index, (source, target) in enumerate(zip(refs[:count], refs[count : 2 * count])):
        for part in chunks(source.shape[1]):
            left = left_ref[index, :, part]
            if lending:
                left = (left.astype(F32) + lent[index][:, part]).astype(BF)
            back = jnp.concatenate([left, right_ref[index, :, part]], axis=0)
            target[:, part] = source[:, part] + dot(hot, back).astype(BF)
    for order in refs[2 * count :]:
        order[...] = jnp.zeros_like(order)


def shifted(array, by):
    peers = lax.axis_size("seq")
    return lax.ppermute(array, "seq", [(i, (i + by) % peers) for i in range(peers)])


def swapped(array, first):
    peers = lax.axis_size("seq")
    partners = [(i - first ^ 1) + first for i in range(peers)]
    return lax.ppermute(
        array, "seq", [(i, j if 0 <= j < peers else i) for i, j in enumerate(partners)]
    )


def shifted_open(array, by):
    peers = lax.axis_size("seq")
    return lax.ppermute(array, "seq", [(i, i + by) for i in range(peers) if 0 <= i + by < peers])


def add_kernel(a_ref, b_ref, sum_ref):
    sum_ref[...] = a_ref[...] + b_ref[...]


def over_heads(sums):
    peers = lax.axis_size("head")
    distance = 1
    pair = (sums,)
    while distance < peers:
        if len(pair) == 2:
            pair = local(add_kernel, "add", 1, [sds(sums.shape, F32)], pair)
        pairs = [(i, i ^ distance) for i in range(peers)]
        pair = (pair[0], lax.ppermute(pair[0], "head", pairs))
        distance *= 2
    return pair


def carried(message, facts, direction):
    peers = lax.axis_size("seq")
    reach = peers // 4
    if reach <= 2:
        return shifted(message, direction), shifted(message, 2 * direction)
    own_state = message.astype(F32)
    through = facts[message.shape[0] :, :1, None]

    def relay(_, state_here):
        return shifted_open((through * state_here + own_state).astype(BF), direction).astype(F32)

    incoming = lax.fori_loop(0, reach, relay, jnp.zeros_like(own_state)).astype(BF)
    return incoming, jnp.zeros_like(message)


def on_device(
    queries, key_vectors, value_vectors, log_decay, head_scale,
    send_rows, take_rows, doc_lengths, cotangent,
):
    rows, features = queries.shape
    heads = head_scale.shape[0]
    width = features // heads
    capacity = send_rows.shape[2]
    send = send_rows.reshape(2, capacity)
    take = take_rows.reshape(1, rows)
    total = features * lax.axis_size("head")
    full, full32 = sds((rows, features)), sds((rows, features), F32)
    squares = sds((heads, rows, rows))
    message_shape = sds((heads, width, width))
    one_side, two_sides = sds((1, capacity, features)), sds((2, capacity, features))

    kv_pair, kv_other, named = pick(send, key_vectors, value_vectors)
    kv_first, kv_second = swapped(kv_pair, 0), swapped(kv_other, 1)
    (
        q_pair, q_other, q_own, k_own, v_own, hot, mask, cols, turned, facts, state_own, leave
    ) = prep(doc_lengths, take, log_decay.T, named, queries, key_vectors, value_vectors)
    q_first, q_second = swapped(q_pair, 0), swapped(q_other, 1)
    (message,) = local(
        state_kernel, "state", 30, [message_shape], (kv_first, kv_second, leave, state_own)
    )
    near, far = carried(message, facts, 1)
    facts_before, facts_after = shifted(facts, 1), shifted(facts, -1)
    k, v = local(
        assemble_kernel,
        "assemble",
        5,
        [full, full],
        (hot, kv_first, kv_second, k_own, v_own, message, facts_before, facts_after),
    )
    q, qe, weight, probs, o_inside = local(
        inside_kernel,
        "inside",
        30,
        [full, sds((heads, width, rows)), sds((heads, rows, rows), F32), squares, full32],
        (hot, q_first, q_second, q_own, k, v, mask, cols, turned),
    )
    u, state_low, sums = local(
        output_kernel,
        "output",
        3,
        [full32, sds((heads, width, width)), sds((2, rows), F32)],
        (head_scale, o_inside, q, facts_before, near, far, cols, cotangent),
        scalars=1,
    )
    peers = lax.axis_size("head")
    sums = [sums] + [
        lax.ppermute(sums, "head", [(i, i ^ by) for i in range(peers)]) for by in range(1, peers)
    ]
    g, grad_message, inverse = local(
        functools.partial(norm_kernel, total),
        "norm",
        4,
        [full, message_shape, sds((rows, width), F32)],
        (head_scale, u, cotangent, qe, *sums),
        scalars=1,
    )
    grad_near, grad_far = carried(grad_message, facts, -1)
    dq, z, dq_left, dq_right = local(
        grad_q_kernel,
        "grad_q",
        30,
        [full, squares, one_side, one_side],
        (take, g, k, v, state_low, weight, cols),
    )
    dq_before, dq_after = shifted(dq_right, 1), shifted(dq_left, -1)
    dk_inner, dv_inner = local(inner_kernel, "inner", 5, [full32, full32], (z, probs, q, g))
    (dkv_right,) = local(
        right_kernel, "right", 30, [two_sides], (take, dk_inner, dv_inner, grad_near)
    )
    dkv_before = shifted(dkv_right, 1)
    dk, dv, dkv_left = local(
        grad_kv_kernel,
        "grad_kv",
        3,
        [full, full, two_sides],
        (take, grad_far, grad_near, facts_after, k, v, cols, dk_inner, dv_inner),
    )
    dkv_after = shifted(dkv_left, -1)
    lent_rows = sds((capacity, features), F32)
    dk_lent, dv_lent = local(
        lend_kernel,
        "lend",
        2,
        [lent_rows, lent_rows],
        (facts, facts_after, grad_near, grad_far, grad_message, facts_before, kv_pair, kv_other, dk),
    )
    (normed,) = local(normed_kernel, "normed", 2, [full], (u, inverse, dk))
    (dq_own,) = local(
        functools.partial(own_kernel, capacity, 1), "own_q", 2, [full], (take, dq, dk)
    )
    grad_queries, order = local(
        functools.partial(finish_kernel, 1, 0),
        "finish_q",
        2,
        [full, sds((16, 128))],
        (send, dq_after, dq_before, dq_own),
    )
    dk_own, dv_own = local(
        functools.partial(own_kernel, capacity, 2), "own_kv", 2, [full, full],
        (take, dk, dv, order),
    )
    grad_keys, grad_values = local(
        functools.partial(finish_kernel, 2, 2),
        "finish_kv",
        2,
        [full, full],
        (send, dkv_after, dkv_before, dk_lent, dv_lent, dk_own, dv_own),
    )
    return normed, grad_queries, grad_keys, grad_values


def solution(mesh):
    both = P("seq", "head")
    in_specs = (both, both, both, both, P("head"), P("seq", None, None), P("seq"), P(), both)
    return jax.shard_map(
        on_device, mesh=mesh, in_specs=in_specs, out_specs=(both,) * 4, check_vma=False
    )
```

```python
import functools
import math

import jax
import jax.numpy as jnp
from jax import lax
from jax.experimental import pallas as pl
from jax.experimental.pallas import tpu as pltpu
from jax.sharding import PartitionSpec as P

EPSILON = 1e-05
LOG2E = math.log2(math.e)
MASKED = -1e30
MIB = 1024 * 1024
BF = jnp.bfloat16
F32 = jnp.float32
NT = (((1,), (1,)), ((), ()))
TN = (((0,), (0,)), ((), ()))
CHUNK = 256


def dot(a, b):
    return jnp.dot(a, b, preferred_element_type=F32)


def dot_nt(a, b):
    return lax.dot_general(a, b, NT, preferred_element_type=F32)


def dot_tn(a, b):
    return lax.dot_general(a, b, TN, preferred_element_type=F32)


def along_rows(row, lanes=128):
    return jnp.broadcast_to(row, (lanes, row.shape[1])).T


def iota(shape, dim):
    return lax.broadcasted_iota(jnp.int32, shape, dim)


def one_hot(hit):
    return jnp.where(hit, 1.0, 0.0).astype(BF)


def pieces(x):
    high = x.astype(BF)
    rest = x - high.astype(F32)
    middle = rest.astype(BF)
    return high, middle, (rest - middle.astype(F32)).astype(BF)


def chunks(features):
    return [slice(start, start + CHUNK) for start in range(0, features, CHUNK)]


def head_slices(features, heads):
    width = features // heads
    return [slice(h * width, (h + 1) * width) for h in range(heads)]


def local(kernel, name, us, out_shape, operands, scalars=0, scratch=(), spaces=None):
    vmem = pl.BlockSpec(memory_space=pltpu.VMEM)
    smem = pl.BlockSpec(memory_space=pltpu.SMEM)
    specs = [smem] * scalars + [vmem] * (len(operands) - scalars)
    if spaces is not None:
        specs = [pl.BlockSpec(memory_space=space) for space in spaces]
    return pl.pallas_call(
        kernel,
        in_specs=specs,
        out_specs=[vmem] * len(out_shape),
        out_shape=out_shape,
        scratch_shapes=list(scratch),
        compiler_params=pltpu.CompilerParams(vmem_limit_bytes=16 * MIB),
        cost_estimate=pl.CostEstimate(
            flops=int(us * 1.1e9), bytes_accessed=1_000_000, transcendentals=0
        ),
        name=name,
    )(*operands)


def sds(shape, dtype=BF):
    return jax.ShapeDtypeStruct(shape, dtype)


def is_odd():
    return lax.rem(lax.axis_index("seq"), 2) == 1


def pick_kernel(send_hbm, k_hbm, v_hbm, pair_ref, other_ref, hot_ref, send_ref, k_ref, v_ref, sem):
    rows, features = k_ref.shape
    capacity = send_ref.shape[1]
    named_copy = pltpu.make_async_copy(send_hbm, send_ref, sem.at[0])
    named_copy.start()
    copies = []
    for source, target in ((k_hbm, k_ref), (v_hbm, v_ref)):
        for start in range(0, rows, 128):
            part = slice(start, start + 128)
            copy = pltpu.make_async_copy(source.at[part], target.at[part], sem.at[1 + len(copies)])
            copy.start()
            copies.append(copy)
    named_copy.wait()
    lane = iota((capacity, 128), 1)
    for side in range(2):
        slots = jnp.where(is_odd(), send_ref[side : side + 1, :], send_ref[1 - side : 2 - side, :])
        named = along_rows(slots)
        for start in range(0, rows, 128):
            hot_ref[side * capacity : (side + 1) * capacity, start : start + 128] = one_hot(
                named == lane + start
            )
    for index, target in enumerate((k_ref, v_ref)):
        for copy in copies[index * len(copies) // 2 : (index + 1) * len(copies) // 2]:
            copy.wait()
        for part in chunks(features):
            picked = dot(hot_ref[...], target[:, part]).astype(BF)
            pair_ref[index, :, part] = picked[:capacity]
            other_ref[index, :, part] = picked[capacity:]


def pick(send, k, v):
    rows, features = k.shape
    capacity = send.shape[1]
    slots = sds((2, capacity, features))
    return local(
        pick_kernel,
        "pick",
        2,
        [slots, slots, sds((2 * capacity, rows))],
        [pltpu.with_memory_space_constraint(x, pltpu.HBM) for x in (send, k, v)],
        scratch=(
            pltpu.VMEM((2, capacity), jnp.int32),
            pltpu.VMEM((rows, features), BF),
            pltpu.VMEM((rows, features), BF),
            pltpu.SemaphoreType.DMA((1 + 2 * (rows // 128),)),
        ),
        spaces=(pl.ANY, pl.ANY, pl.ANY),
    )


def prep_kernel(
    docs_ref, take_ref, log_ref, named_ref, q_ref, k_ref, v_ref,
    left_ref, right_ref, qo_ref, ko_ref, vo_ref, hot_ref,
    mask_ref, cols_ref, rows_ref, facts_ref, state_ref, leave_ref, own_ref,
):
    rows, features = q_ref.shape
    heads = log_ref.shape[0]
    capacity = hot_ref.shape[1] // 2
    for part in chunks(features):
        picked = dot(named_ref[...], q_ref[:, part]).astype(BF)
        left_ref[0, :, part] = picked[:capacity]
        right_ref[0, :, part] = picked[capacity:]

    first = (lax.axis_index("seq") * rows).astype(jnp.int32)
    position = first + iota((rows, 1), 0)
    position_row = first + iota((1, rows), 1)
    segment = jnp.zeros((rows, 1), jnp.int32)
    segment_row = jnp.zeros((1, rows), jnp.int32)
    segment_first = jnp.int32(0)
    segment_last = jnp.int32(0)
    opens_first = jnp.int32(0)
    opens = jnp.int32(0)
    start = jnp.int32(0)
    for n in range(docs_ref.shape[0]):
        segment += (position >= start).astype(jnp.int32)
        segment_row += (position_row >= start).astype(jnp.int32)
        segment_first += (first >= start).astype(jnp.int32)
        segment_last += (first + rows - 1 >= start).astype(jnp.int32)
        opens_first += (first == start).astype(jnp.int32)
        opens += ((start >= first) & (start < first + rows)).astype(jnp.int32)
        start += docs_ref[n]
    below = iota((rows, rows), 0) >= iota((rows, rows), 1)
    scale = -0.5 * math.log2(features // heads)
    mask_ref[...] = jnp.where((segment == segment_row) & below, scale, MASKED)
    triangle = one_hot(below)
    logs = jnp.concatenate([log_ref[...], jnp.zeros((128 - heads, rows), F32)], axis=0).T
    high, middle, low = pieces(logs)
    running = (dot(triangle, high) + (dot(triangle, middle) + dot(triangle, low))) * LOG2E
    rows_ref[...] = running.T[:heads]
    final = running[rows - 1 : rows, :]
    keep_f = segment == segment_last
    keep_e = (segment == segment_first) & (opens_first == 0)
    leaving = jnp.where(keep_f, jnp.exp2(final - running), 0.0)
    entering = jnp.where(keep_e, jnp.exp2(running + scale), 0.0)
    through = jnp.where(opens == 0, jnp.exp2(final), 0.0)
    cols_ref[0], cols_ref[1], cols_ref[2] = leaving, entering, running
    lane = iota((rows, 128), 1)
    taken = along_rows(take_ref[...])
    for start_row in range(0, rows, 128):
        own_ref[:, start_row : start_row + 128] = one_hot(taken - capacity == lane + start_row)
    right = capacity + rows
    odd = is_odd()
    hot_ref[:, :capacity] = one_hot(taken - jnp.where(odd, 0, right) == lane)
    hot_ref[:, capacity:] = one_hot(taken - jnp.where(odd, right, 0) == lane)
    leave_ref[...] = sum(dot_tn(hot_ref[...], piece) for piece in pieces(leaving))
    facts_ref[:heads] = jnp.where(odd, leave_ref[capacity:, :], leave_ref[:capacity, :]).T[:heads]
    facts_ref[heads:] = along_rows(through, capacity)[:heads]
    for part in chunks(features):
        for source, target in ((k_ref, ko_ref), (v_ref, vo_ref), (q_ref, qo_ref)):
            target[:, part] = dot(own_ref[...], source[:, part]).astype(BF)
    for h, part in enumerate(head_slices(features, heads)):
        kf = (ko_ref[:, part].astype(F32) * cols_ref[0, :, h : h + 1]).astype(BF)
        state_ref[h] = dot_tn(kf, vo_ref[:, part])


def prep(docs, take, log_decay, named, q, k, v):
    rows, features = q.shape
    heads = log_decay.shape[0]
    width = features // heads
    capacity = named.shape[0] // 2
    slots, own_rows = sds((1, capacity, features)), sds((rows, features))
    return local(
        prep_kernel,
        "prep",
        30,
        [
            slots, slots, own_rows, own_rows, own_rows,
            sds((rows, 2 * capacity)),
            sds((rows, rows), F32),
            sds((3, rows, 128), F32),
            sds((heads, rows), F32),
            sds((2 * heads, capacity), F32),
            sds((heads, width, width), F32),
            sds((2 * capacity, 128), F32),
        ],
        (docs, take, log_decay, named, q, k, v),
        scalars=1,
        scratch=(pltpu.VMEM((rows, rows), BF),),
    )


def state_kernel(left_ref, right_ref, leave_ref, own_ref, message_ref):
    heads, width = own_ref.shape[:2]
    for h, part in enumerate(head_slices(heads * width, heads)):
        k = jnp.concatenate([left_ref[0, :, part], right_ref[0, :, part]], axis=0)
        v = jnp.concatenate([left_ref[1, :, part], right_ref[1, :, part]], axis=0)
        kf = (k.astype(F32) * leave_ref[:, h : h + 1]).astype(BF)
        message_ref[h] = (own_ref[h] + dot_tn(kf, v)).astype(BF)


def assemble(hot_ref, left_ref, right_ref, index, own_rows, target):
    for part in chunks(target.shape[1]):
        extra = jnp.concatenate([left_ref[index, :, part], right_ref[index, :, part]], axis=0)
        target[:, part] = own_rows[:, part] + dot(hot_ref[...], extra).astype(BF)


def assemble_kernel(hot_ref, left_ref, right_ref, ko_ref, vo_ref, _, _before, _after, k_ref, v_ref):
    assemble(hot_ref, left_ref, right_ref, 0, ko_ref, k_ref)
    assemble(hot_ref, left_ref, right_ref, 1, vo_ref, v_ref)


def decay(mask_ref, cols_ref, rows_ref, h, top, half, reach):
    column = cols_ref[2, top : top + half, h : h + 1]
    row = rows_ref[h : h + 1, :reach]
    return jnp.exp2((column - row) + mask_ref[top : top + half, :reach])


def inside_kernel(hot_ref, left_ref, right_ref, qo_ref, k_ref, v_ref, mask_ref, cols_ref, rows_ref, q_ref, qe_ref, weight_ref, p_ref, o_ref):
    rows, features = k_ref.shape
    assemble(hot_ref, left_ref, right_ref, 0, qo_ref, q_ref)
    heads, half = p_ref.shape[0], rows // 2
    for h, part in enumerate(head_slices(features, heads)):
        for i in range(2):
            top, reach = i * half, (i + 1) * half
            here = slice(top, top + half)
            scores = dot_nt(q_ref[here, part], k_ref[:reach, part])
            weight = decay(mask_ref, cols_ref, rows_ref, h, top, half, reach)
            weight_ref[h, here, :reach] = weight
            p = (scores * weight).astype(BF)
            p_ref[h, here, :reach] = p
            o_ref[here, part] = dot(p, v_ref[:reach, part])
        qe = (q_ref[:, part].astype(F32) * cols_ref[1, :, h : h + 1]).astype(BF)
        qe_ref[h] = qe.T


def shards_before(direction):
    index = lax.axis_index("seq")
    return index if direction > 0 else lax.axis_size("seq") - 1 - index


def decayed(facts_ref, h, state):
    heads, width = facts_ref.shape[0] // 2, state.shape[1]
    return facts_ref[heads + h : heads + h + 1, :width] * state


def carried_sum(before, facts_ref, near_ref, far_ref, h):
    near = near_ref[h].astype(F32)
    far = decayed(facts_ref, h, far_ref[h].astype(F32))
    near = jnp.where(before >= 1, near, 0.0)
    return near + jnp.where(before >= 2, far, 0.0)


def joined(before, facts_ref, near_ref, far_ref, h):
    return carried_sum(before, facts_ref, near_ref, far_ref, h).astype(BF)


def output_kernel(scale_ref, o_ref, q_ref, far_ref, near_ref, facts_ref, cols_ref, ct_ref, u_ref, h_ref, sums_ref):
    rows, features = q_ref.shape
    heads, width = h_ref.shape[:2]
    before = shards_before(1)
    squares = jnp.zeros((rows, width), F32)
    cross = jnp.zeros((rows, width), F32)
    for h, part in enumerate(head_slices(features, heads)):
        carried_in = joined(before, facts_ref, near_ref, far_ref, h)
        h_ref[h] = carried_in
        outer = dot(q_ref[:, part], carried_in) * cols_ref[1, :, h : h + 1]
        u = (o_ref[:, part] + outer) * scale_ref[h]
        u_ref[:, part] = u
        squares += u * u
        cross += ct_ref[:, part].astype(F32) * u
    sums_ref[0:1, :] = jnp.sum(squares.T, axis=0, keepdims=True)
    sums_ref[1:2, :] = jnp.sum(cross.T, axis=0, keepdims=True)


def norm_kernel(total, scale_ref, u_ref, ct_ref, qe_ref, *refs):
    *sums, g_ref, message_ref, inverse_ref = refs
    features = u_ref.shape[1]
    heads, width = qe_ref.shape[:2]
    summed = sums[0][...]
    for more in sums[1:]:
        summed += more[...]
    inverse = lax.rsqrt(along_rows(summed[0:1, :], width) / total + EPSILON)
    mean = inverse * inverse * inverse * (along_rows(summed[1:2, :], width) / total)
    inverse_ref[...] = inverse
    for h, part in enumerate(head_slices(features, heads)):
        g = (inverse * ct_ref[:, part].astype(F32) - u_ref[:, part] * mean) * scale_ref[h]
        g = g.astype(BF)
        g_ref[:, part] = g
        message_ref[h] = dot(qe_ref[h], g).astype(BF)


def normed_kernel(u_ref, inverse_ref, _, normed_ref):
    rows, features = u_ref.shape
    width = inverse_ref.shape[1]
    for part in head_slices(features, features // width):
        normed_ref[:, part] = (u_ref[:, part] * inverse_ref[...]).astype(BF)


def send_back(hot, source, left_ref, right_ref, index):
    capacity = left_ref.shape[1]
    for part in chunks(source.shape[1]):
        back = dot(hot, source[:, part]).astype(BF)
        left_ref[index, :, part] = back[:capacity]
        right_ref[index, :, part] = back[capacity:]


def slots_hot(take_ref, capacity):
    rows = take_ref.shape[1]
    taken = jnp.broadcast_to(take_ref[...], (capacity, rows))
    slot = iota((capacity, rows), 0)
    return jnp.concatenate(
        [one_hot(taken == slot), one_hot(taken - (capacity + rows) == slot)], axis=0
    )


def grad_q_kernel(take_ref, g_ref, k_ref, v_ref, h_ref, weight_ref, cols_ref, dq_ref, z_ref, left_ref, right_ref):
    rows, features = k_ref.shape
    heads, half = h_ref.shape[0], rows // 2
    for h, part in enumerate(head_slices(features, heads)):
        for i in range(2):
            top, reach = i * half, (i + 1) * half
            here = slice(top, top + half)
            g = g_ref[here, part]
            z = (dot_nt(g, v_ref[:reach, part]) * weight_ref[h, here, :reach]).astype(BF)
            z_ref[h, here, :reach] = z
            outer = dot_nt(g, h_ref[h]) * cols_ref[1, here, h : h + 1]
            dq_ref[here, part] = (dot(z, k_ref[:reach, part]) + outer).astype(BF)
    send_back(slots_hot(take_ref, left_ref.shape[1]), dq_ref, left_ref, right_ref, 0)


def inner_kernel(z_ref, p_ref, q_ref, g_ref, dk_ref, dv_ref):
    rows, features = q_ref.shape
    heads, half = z_ref.shape[0], rows // 2
    for h, part in enumerate(head_slices(features, heads)):
        for square, source, target in ((z_ref, q_ref, dk_ref), (p_ref, g_ref, dv_ref)):
            for j in range(2):
                here = slice(j * half, (j + 1) * half)
                target[here, part] = dot_tn(square[h, j * half :, here], source[j * half :, part])


def right_kernel(take_ref, dk_ref, dv_ref, _, right_ref):
    capacity, features = right_ref.shape[1:]
    hot = slots_hot(take_ref, capacity)[capacity:]
    for index, source in enumerate((dk_ref, dv_ref)):
        for part in chunks(features):
            right_ref[index, :, part] = dot(hot, source[:, part].astype(BF)).astype(BF)


def grad_kv_kernel(take_ref, far_ref, near_ref, facts_ref, k_ref, v_ref, cols_ref, dki_ref, dvi_ref, dk_ref, dv_ref, left_ref):
    rows, features = k_ref.shape
    heads = near_ref.shape[0]
    before = shards_before(-1)
    for h, part in enumerate(head_slices(features, heads)):
        state_grad = joined(before, facts_ref, near_ref, far_ref, h)
        leaving = cols_ref[0, :, h : h + 1]
        dk_ref[:, part] = (dki_ref[:, part] + leaving * dot_nt(v_ref[:, part], state_grad)).astype(BF)
        dv_ref[:, part] = (dvi_ref[:, part] + leaving * dot(k_ref[:, part], state_grad)).astype(BF)
    hot = slots_hot(take_ref, left_ref.shape[1])[: left_ref.shape[1]]
    for index, source in enumerate((dk_ref, dv_ref)):
        for part in chunks(features):
            left_ref[index, :, part] = dot(hot, source[:, part]).astype(BF)


def lend_kernel(facts_ref, after_ref, near_ref, far_ref, message_ref, lent_ref, pair_ref, other_ref, _, dk_ref, dv_ref):
    features = dk_ref.shape[1]
    heads, width = message_ref.shape[:2]
    before = shards_before(-1)
    for h, part in enumerate(head_slices(features, heads)):
        after = carried_sum(before, after_ref, near_ref, far_ref, h)
        state_grad = (message_ref[h].astype(F32) + decayed(facts_ref, h, after)).astype(BF)
        leaving = along_rows(lent_ref[h : h + 1, :], width)
        k, v = [
            jnp.where(is_odd(), pair_ref[index, :, part], other_ref[index, :, part])
            for index in range(2)
        ]
        dk_ref[:, part] = leaving * dot_nt(v, state_grad)
        dv_ref[:, part] = leaving * dot(k, state_grad)


def own_kernel(capacity, count, take_ref, *refs):
    rows = refs[0].shape[0]
    taken = jnp.broadcast_to(take_ref[...], (rows, rows))
    hot = one_hot(taken - capacity == iota((rows, rows), 0))
    for source, target in zip(refs[:count], refs[-count:]):
        for part in chunks(source.shape[1]):
            target[:, part] = dot(hot, source[:, part]).astype(BF)


def finish_kernel(count, lending, send_ref, right_ref, left_ref, *refs):
    lent, refs = refs[:lending], refs[lending:]
    rows = refs[0].shape[0]
    capacity = send_ref.shape[1]
    line = iota((rows, capacity), 0)
    hot = jnp.concatenate(
        [
            one_hot(jnp.broadcast_to(send_ref[side : side + 1, :], (rows, capacity)) == line)
            for side in range(2)
        ],
        axis=1,
    )
    for index, (source, target) in enumerate(zip(refs[:count], refs[count : 2 * count])):
        for part in chunks(source.shape[1]):
            left = left_ref[index, :, part]
            if lending:
                left = (left.astype(F32) + lent[index][:, part]).astype(BF)
            back = jnp.concatenate([left, right_ref[index, :, part]], axis=0)
            target[:, part] = source[:, part] + dot(hot, back).astype(BF)
    for order in refs[2 * count :]:
        order[...] = jnp.zeros_like(order)


def shifted(array, by):
    peers = lax.axis_size("seq")
    return lax.ppermute(array, "seq", [(i, (i + by) % peers) for i in range(peers)])


def swapped(array, first):
    peers = lax.axis_size("seq")
    partners = [(i - first ^ 1) + first for i in range(peers)]
    return lax.ppermute(
        array, "seq", [(i, j if 0 <= j < peers else i) for i, j in enumerate(partners)]
    )


def shifted_open(array, by):
    peers = lax.axis_size("seq")
    return lax.ppermute(array, "seq", [(i, i + by) for i in range(peers) if 0 <= i + by < peers])


def add_kernel(a_ref, b_ref, sum_ref):
    sum_ref[...] = a_ref[...] + b_ref[...]


def over_heads(sums):
    peers = lax.axis_size("head")
    distance = 1
    pair = (sums,)
    while distance < peers:
        if len(pair) == 2:
            pair = local(add_kernel, "add", 1, [sds(sums.shape, F32)], pair)
        pairs = [(i, i ^ distance) for i in range(peers)]
        pair = (pair[0], lax.ppermute(pair[0], "head", pairs))
        distance *= 2
    return pair


def carried(message, facts, direction):
    peers = lax.axis_size("seq")
    reach = peers // 4
    if reach <= 2:
        return shifted(message, direction), shifted(message, 2 * direction)
    own_state = message.astype(F32)
    through = facts[message.shape[0] :, :1, None]

    def relay(_, state_here):
        return shifted_open((through * state_here + own_state).astype(BF), direction).astype(F32)

    incoming = lax.fori_loop(0, reach, relay, jnp.zeros_like(own_state)).astype(BF)
    return incoming, jnp.zeros_like(message)


def on_device(
    queries, key_vectors, value_vectors, log_decay, head_scale,
    send_rows, take_rows, doc_lengths, cotangent,
):
    rows, features = queries.shape
    heads = head_scale.shape[0]
    width = features // heads
    capacity = send_rows.shape[2]
    send = send_rows.reshape(2, capacity)
    take = take_rows.reshape(1, rows)
    total = features * lax.axis_size("head")
    full, full32 = sds((rows, features)), sds((rows, features), F32)
    squares = sds((heads, rows, rows))
    message_shape = sds((heads, width, width))
    one_side, two_sides = sds((1, capacity, features)), sds((2, capacity, features))

    kv_pair, kv_other, named = pick(send, key_vectors, value_vectors)
    kv_first, kv_second = swapped(kv_pair, 0), swapped(kv_other, 1)
    (
        q_pair, q_other, q_own, k_own, v_own, hot, mask, cols, turned, facts, state_own, leave
    ) = prep(doc_lengths, take, log_decay.T, named, queries, key_vectors, value_vectors)
    q_first, q_second = swapped(q_pair, 0), swapped(q_other, 1)
    (message,) = local(
        state_kernel, "state", 30, [message_shape], (kv_first, kv_second, leave, state_own)
    )
    near, far = carried(message, facts, 1)
    facts_before, facts_after = shifted(facts, 1), shifted(facts, -1)
    k, v = local(
        assemble_kernel,
        "assemble",
        5,
        [full, full],
        (hot, kv_first, kv_second, k_own, v_own, message, facts_before, facts_after),
    )
    q, qe, weight, probs, o_inside = local(
        inside_kernel,
        "inside",
        30,
        [full, sds((heads, width, rows)), sds((heads, rows, rows), F32), squares, full32],
        (hot, q_first, q_second, q_own, k, v, mask, cols, turned),
    )
    u, state_low, sums = local(
        output_kernel,
        "output",
        3,
        [full32, sds((heads, width, width)), sds((2, rows), F32)],
        (head_scale, o_inside, q, far, near, facts_before, cols, cotangent),
        scalars=1,
    )
    peers = lax.axis_size("head")
    sums = [sums] + [
        lax.ppermute(sums, "head", [(i, i ^ by) for i in range(peers)]) for by in range(1, peers)
    ]
    g, grad_message, inverse = local(
        functools.partial(norm_kernel, total),
        "norm",
        4,
        [full, message_shape, sds((rows, width), F32)],
        (head_scale, u, cotangent, qe, *sums),
        scalars=1,
    )
    grad_near, grad_far = carried(grad_message, facts, -1)
    dq, z, dq_left, dq_right = local(
        grad_q_kernel,
        "grad_q",
        30,
        [full, squares, one_side, one_side],
        (take, g, k, v, state_low, weight, cols),
    )
    dq_before, dq_after = shifted(dq_right, 1), shifted(dq_left, -1)
    dk_inner, dv_inner = local(inner_kernel, "inner", 5, [full32, full32], (z, probs, q, g))
    (dkv_right,) = local(
        right_kernel, "right", 30, [two_sides], (take, dk_inner, dv_inner, grad_near)
    )
    dkv_before = shifted(dkv_right, 1)
    dk, dv, dkv_left = local(
        grad_kv_kernel,
        "grad_kv",
        3,
        [full, full, two_sides],
        (take, grad_far, grad_near, facts_after, k, v, cols, dk_inner, dv_inner),
    )
    dkv_after = shifted(dkv_left, -1)
    lent_rows = sds((capacity, features), F32)
    dk_lent, dv_lent = local(
        lend_kernel,
        "lend",
        2,
        [lent_rows, lent_rows],
        (facts, facts_after, grad_near, grad_far, grad_message, facts_before, kv_pair, kv_other, dk),
    )
    (normed,) = local(normed_kernel, "normed", 2, [full], (u, inverse, dk))
    (dq_own,) = local(
        functools.partial(own_kernel, capacity, 1), "own_q", 2, [full], (take, dq, dk)
    )
    grad_queries, order = local(
        functools.partial(finish_kernel, 1, 0),
        "finish_q",
        2,
        [full, sds((16, 128))],
        (send, dq_after, dq_before, dq_own),
    )
    dk_own, dv_own = local(
        functools.partial(own_kernel, capacity, 2), "own_kv", 2, [full, full],
        (take, dk, dv, order),
    )
    grad_keys, grad_values = local(
        functools.partial(finish_kernel, 2, 2),
        "finish_kv",
        2,
        [full, full],
        (send, dkv_after, dkv_before, dk_lent, dv_lent, dk_own, dv_own),
    )
    return normed, grad_queries, grad_keys, grad_values


def solution(mesh):
    both = P("seq", "head")
    in_specs = (both, both, both, both, P("head"), P("seq", None, None), P("seq"), P(), both)
    return jax.shard_map(
        on_device, mesh=mesh, in_specs=in_specs, out_specs=(both,) * 4, check_vma=False
    )
```
